512 devices in a mesh: elem: 64 (over y, z), mode: 8 (over x, core).
Axes of the slice: x: 4, y: 4, z: 16, core: 2. Of those that a mesh axis runs over, the one named last changes fastest.
Arguments:
- velocity: float32 [3, 512, 41472], P(None, 'mode', 'elem'), may hold values from -0.375 to 0.375
- metric: float32 [4, 41472], P(None, 'elem'), may hold values from -4 to 4
- mass: float32 [41472], P('elem'), may hold values from 0.1 to 1
- local_ids: int32 [41472], P('elem'), may hold values from 0 to 584, as said below
- edge_ids: int32 [64, 2, 65], P('elem'), may hold values from 0 to 584, as said below
Outputs:
- velocity_new: float32 [3, 512, 41472], P(None, 'mode', 'elem')
- pressure: float32 [512, 41472], P('mode', 'elem')
The draws below stay inside these ranges and needn't reach their ends.
Inputs may be any that keep to these rules, and one draw needn't show every extreme that they name: `local_ids`: on each device every number of 0 to 584 is used; copies of one node on a device carry one number. Quads share nodes only with quads of their own device and, through the nodes of edge_ids, with the devices just before and after it around the cycle of elem indices. edge_ids[e, 0] and edge_ids[e, 1] each list 65 distinct local numbers of device e, disjoint from each other: the nodes shared with device e - 1 and with device e + 1 (around the cycle). edge_ids[e, 1, k] and edge_ids[e + 1, 0, k] name the same node.
All inputs are finite; a program needn't handle non-finite values.
Results may differ from the reference program's by a relative error of at most 0.0001.
Values sent between devices are 32-bit elements; how exact they have to be, the bound alone decides.
No kernel may reach another device: no remote copies, remote signals or barrier semaphores. Data moves between devices by JAX's collectives and lax.ppermute only.
A program may use at most 64 MiB of HBM per device.

```python
import math
import jax
import jax.numpy as jnp
import numpy as np
from jax import lax

SIDE = 9
QUAD_NODES = 81
PLANES = 512
RADIAL = 8
COLS = 1
ITERS = 2
NODES = 41472
LOCAL_NODES = 585
N_ELEM = 64


def mesh_tables(key):
    radial_grid_lines = (SIDE - 1) * RADIAL + 1
    count_of_nodes = ((SIDE - 1) * COLS + 1) * radial_grid_lines
    random_key_list = jax.random.split(key, N_ELEM)

    def relabel_single_node(random_key_handle):
        middle = jax.random.permutation(random_key_handle, count_of_nodes - 2).astype(jnp.int32) + 1
        return jnp.concatenate([jnp.zeros((1,), jnp.int32), middle, jnp.full((1,), count_of_nodes - 1, jnp.int32)])

    def order_one(random_key_handle):
        return jax.random.permutation(jax.random.fold_in(random_key_handle, 7), RADIAL * COLS)
    relabel_nodes = jax.vmap(relabel_single_node)(random_key_list).astype(jnp.int32)
    quad_order = jax.vmap(order_one)(random_key_list).astype(jnp.int32)
    radial_pos = quad_order // COLS
    around_pos = quad_order % COLS
    side_pos = jnp.arange(SIDE, dtype=jnp.int32)
    natural_ordering = ((SIDE - 1) * around_pos[:, :, None, None] + side_pos[None, None, :, None]) * radial_grid_lines
    natural_ordering = natural_ordering + (SIDE - 1) * radial_pos[:, :, None, None] + side_pos[None, None, None, :]
    natural_ordering = natural_ordering.reshape(N_ELEM, -1)
    local_node_labels = jnp.take_along_axis(relabel_nodes, natural_ordering, axis=1)
    element_edges = jnp.stack([relabel_nodes[:, :radial_grid_lines], relabel_nodes[:, count_of_nodes - radial_grid_lines:]], axis=1)
    return (local_node_labels.reshape(-1).astype(jnp.int32), element_edges.astype(jnp.int32))


def draw_local_ids(key, part):
    return mesh_tables(key)[0]


def draw_edge_ids(key, part):
    return mesh_tables(key)[1]


def block_levels(key, dims, shards, low, high):
    loudness = 1.0
    for axis_at, shards_of in shards:
        steps = jax.random.uniform(jax.random.fold_in(jax.random.fold_in(key, 6), axis_at), (shards_of,), jnp.float32, low / len(shards), high / len(shards))
        loudness = loudness * jnp.repeat(jnp.exp(steps), dims[axis_at] // shards_of).reshape((-1,) + (1,) * (len(dims) - 1 - axis_at))
    return loudness


def noise(own_key, dims, width, limit, shards=(), held_as=jnp.bfloat16):
    result = width * jax.random.normal(own_key, dims, jnp.float32)
    if shards:
        result = result * block_levels(own_key, dims, shards, -0.22, 0.18)
    return jnp.clip(result, -limit, limit).astype(held_as)


def setup_inputs(seed: int = 0) -> dict:
    splits = jax.random.split(jax.random.key(seed), 6)
    velocity = noise(splits[0], (3, PLANES, NODES), ((2.0 / PLANES) ** 0.5), 0.375, ((1, 8), (2, 64)), jnp.float32)
    metric = noise(splits[1], (4, NODES), 1.0, 4.0, ((1, 64),), jnp.float32)
    mass = jnp.clip(jnp.exp(math.log(1.0) - 2.3025851 * jax.random.uniform(splits[2], (NODES,), jnp.float32) ** block_levels(splits[2], (NODES,), ((0, 64),), -0.2, 0.2)), 0.1, 1.0)
    local_ids = draw_local_ids(jax.random.fold_in(splits[5], 71), 0)
    edge_ids = draw_edge_ids(jax.random.fold_in(splits[5], 71), 0)
    return dict(velocity=velocity, metric=metric, mass=mass, local_ids=local_ids, edge_ids=edge_ids)


penalty = 1.0
time_step = 0.01

def legendre_pair(points, degree):
    previous = points * 0.0 + 1.0
    current = points.copy()
    for order in range(2, degree + 1):
        following = ((2.0 * order - 1.0) * points * current - (order - 1.0) * previous) / order
        previous = current
        current = following
    return (previous, current)

def derivative_table():
    degree = SIDE - 1
    points = np.cos(math.pi * np.arange(degree + 1) / degree)
    for sweep in range(100):
        lower, upper = legendre_pair(points, degree)
        points = points - (points * upper - lower) / ((degree + 1.0) * upper)
    points = points[::-1].copy()
    values = legendre_pair(points, degree)[1]
    identity = np.eye(SIDE)
    differ = points[:, None] - points[None, :] + identity
    matrix = np.where(identity > 0.5, 0.0, values[:, None] / (values[None, :] * differ))
    matrix[0, 0] = -degree * (degree + 1) / 4.0
    matrix[degree, degree] = degree * (degree + 1) / 4.0
    along_r = np.kron(matrix, identity)
    along_s = np.kron(identity, matrix)
    return np.concatenate([along_r.T, along_s.T], axis=1).astype(np.float32)

def fourier_tables(planes):
    positions = jnp.arange(planes, dtype=jnp.int32)
    mode_number = positions // 2
    frequency = jnp.where(positions == 1, planes // 2, mode_number)
    phase_int = positions[:, None] * frequency[None, :] % planes
    angles = 2.0 * math.pi / planes * phase_int.astype(jnp.float32)
    cosine = jnp.cos(angles)
    sines = jnp.sin(angles)
    cos_like = (positions % 2 == 0) | (positions == 1)
    synthesis = jnp.where(cos_like[None, :], cosine, sines)
    wavenumber = 8.0 / planes * mode_number.astype(jnp.float32)
    slope_table = jnp.where(cos_like[None, :], -wavenumber[None, :] * sines, wavenumber[None, :] * cosine)
    weight = jnp.where(positions < 2, 1.0, 2.0) / planes
    retained = (mode_number <= planes // 3) & (positions != 1)
    forward = jnp.transpose(synthesis * jnp.where(retained, weight, 0.0)[None, :])
    return (synthesis, slope_table, forward, wavenumber)

def along_z(spectral, wavenumber):
    dims_shape = spectral.shape
    paired = spectral.reshape(dims_shape[:-2] + (dims_shape[-2] // 2, 2, dims_shape[-1]))
    rate_col = wavenumber[0::2][:, None]
    turned = jnp.stack([rate_col * paired[..., 1, :], -rate_col * paired[..., 0, :]], axis=-2)
    return turned.reshape(dims_shape)

def element_grad(field, metric, diff_table):
    derived = jnp.dot(field.reshape(-1, QUAD_NODES), diff_table, precision=lax.Precision.HIGHEST, preferred_element_type=jnp.float32)
    grad_r = derived[:, :QUAD_NODES].reshape(field.shape)
    grad_s = derived[:, QUAD_NODES:].reshape(field.shape)
    return (metric[0] * grad_r + metric[2] * grad_s, metric[1] * grad_r + metric[3] * grad_s)

def element_div(flux_x, flux_y, metric, diff_table):
    part_r = metric[0] * flux_x + metric[1] * flux_y
    part_s = metric[2] * flux_x + metric[3] * flux_y
    joined = jnp.concatenate([part_r.reshape(-1, QUAD_NODES), part_s.reshape(-1, QUAD_NODES)], axis=1)
    return jnp.dot(joined, diff_table.T, precision=lax.Precision.HIGHEST, preferred_element_type=jnp.float32).reshape(flux_x.shape)

def assemble(values, local_ids, edge_ids):
    row_count = values.shape[0]
    nodes_dev = values.shape[1] // N_ELEM
    blocks = jnp.transpose(values.reshape(row_count, N_ELEM, nodes_dev), (1, 0, 2))
    numbers = local_ids.reshape(N_ELEM, nodes_dev)

    def gather_copies(block, number):
        return jnp.zeros((row_count, LOCAL_NODES), values.dtype).at[:, number].add(block)
    summed = jax.vmap(gather_copies)(blocks, numbers)

    def take_rim(total, element_edges):
        return (total[:, element_edges[0]], total[:, element_edges[1]])
    to_prev, to_next = jax.vmap(take_rim)(summed, edge_ids)
    from_prev = jnp.roll(to_next, 1, axis=0)
    from_next = jnp.roll(to_prev, -1, axis=0)

    def add_rim(total, element_edges, lower, upper):
        return total.at[:, element_edges[0]].add(lower).at[:, element_edges[1]].add(upper)
    summed = jax.vmap(add_rim)(summed, edge_ids, from_prev, from_next)

    def spread(total, number):
        return total[:, number]
    copies = jax.vmap(spread)(summed, numbers)
    return jnp.transpose(copies, (1, 0, 2)).reshape(row_count, N_ELEM * nodes_dev)

def reference(velocity, metric, mass, local_ids, edge_ids):
    diff_table = jnp.asarray(derivative_table()).astype(jnp.float32)
    synthesis, slope_table, forward, wavenumber = fourier_tables(PLANES)
    node_total = velocity.shape[2]
    nodes_dev = node_total // N_ELEM
    vel_blocks = jnp.transpose(velocity.reshape(3, PLANES, N_ELEM, nodes_dev), (2, 0, 1, 3))
    met_blocks = jnp.transpose(metric.reshape(4, N_ELEM, nodes_dev), (1, 0, 2))

    def convective(pair):
        velocity_block, metric_block = pair
        grad_x, grad_y = element_grad(velocity_block, metric_block, diff_table)
        fields = jnp.concatenate([velocity_block, grad_x, grad_y, along_z(velocity_block, wavenumber)], axis=0)
        physical = jnp.einsum('nj,fjm->fnm', synthesis, fields, precision=lax.Precision.HIGHEST)
        nonlinear = -(physical[0] * physical[3:6] + physical[1] * physical[6:9] + physical[2] * physical[9:12])
        return jnp.einsum('jn,cnm->cjm', forward, nonlinear, precision=lax.Precision.HIGHEST)
    convect = lax.map(convective, (vel_blocks, met_blocks))
    convect = jnp.transpose(convect, (1, 2, 0, 3)).reshape(3, PLANES, node_total)
    weighted = (mass * convect).reshape(3 * PLANES, node_total)
    stacked = jnp.concatenate([weighted, mass[None, :], jnp.ones_like(mass)[None, :]], axis=0)
    assembled = assemble(stacked, local_ids, edge_ids)
    projected = assembled[:3 * PLANES].reshape(3, PLANES, node_total) / assembled[3 * PLANES]
    inverse = 1.0 / assembled[3 * PLANES + 1]
    velocity_star = velocity + time_step * projected
    star_x, star_y = element_grad(velocity_star[:2], metric, diff_table)
    divergence = star_x[0] + star_y[1] + along_z(velocity_star[2], wavenumber)
    right_side = -assemble(mass * divergence, local_ids, edge_ids) / time_step
    helmholtz_shift = (wavenumber * wavenumber + penalty)[:, None]

    def operate(field):
        grad_x, grad_y = element_grad(field, metric, diff_table)
        element_part = element_div(mass * grad_x, mass * grad_y, metric, diff_table) + helmholtz_shift * mass * field
        return assemble(element_part, local_ids, edge_ids)

    def inner_product(left, right):
        return lax.optimization_barrier(jnp.sum(inverse * left * right, axis=1))
    pressure = jnp.zeros_like(right_side)
    residual = right_side
    direction = right_side
    norm_now = inner_product(residual, residual)
    for iteration in range(ITERS):
        applied = operate(direction)
        step_size = norm_now / inner_product(direction, applied)
        pressure = pressure + step_size[:, None] * direction
        residual = residual - step_size[:, None] * applied
        norm_next = inner_product(residual, residual)
        direction = residual + (norm_next / norm_now)[:, None] * direction
        norm_now = norm_next
    press_x, press_y = element_grad(pressure, metric, diff_table)
    press_z = along_z(pressure, wavenumber)
    velocity_new = velocity_star - time_step * jnp.stack([press_x, press_y, press_z], axis=0)
    return (velocity_new, pressure)
```

```python
import functools
import math

import jax
import jax.numpy as jnp
import numpy as np
from jax import lax
from jax.experimental import pallas as pl
from jax.experimental.pallas import tpu as pltpu
from jax.sharding import PartitionSpec as P

SIDE = 9
QUAD_NODES = 81
PLANES = 512
QUADS = 8
EDGE = 65
LANES = 128
WIDE = QUADS * LANES
PACK = 256
ROWS = 64
KEPT = 384
STACK = 200

PENALTY = 1.0
TIME_STEP = 0.01

f32 = jnp.float32
bf16 = jnp.bfloat16


def legendre_pair(points, degree):
    previous = points * 0.0 + 1.0
    current = points.copy()
    for order in range(2, degree + 1):
        following = ((2.0 * order - 1.0) * points * current - (order - 1.0) * previous) / order
        previous = current
        current = following
    return (previous, current)


def derivative_matrix():
    degree = SIDE - 1
    points = np.cos(math.pi * np.arange(degree + 1) / degree)
    for sweep in range(100):
        lower, upper = legendre_pair(points, degree)
        points = points - (points * upper - lower) / ((degree + 1.0) * upper)
    points = points[::-1].copy()
    values = legendre_pair(points, degree)[1]
    identity = np.eye(SIDE)
    differ = points[:, None] - points[None, :] + identity
    matrix = np.where(identity > 0.5, 0.0, values[:, None] / (values[None, :] * differ))
    matrix[0, 0] = -degree * (degree + 1) / 4.0
    matrix[degree, degree] = degree * (degree + 1) / 4.0
    return matrix


def halves(table):
    high = table.astype(np.float32).astype(jnp.bfloat16)
    low = (table - high.astype(np.float64)).astype(np.float32).astype(jnp.bfloat16)
    return np.stack([high, low])


def derivative_tables():
    matrix = derivative_matrix()
    table = np.zeros((LANES, 2 * LANES))
    table[:QUAD_NODES, :QUAD_NODES] = np.kron(matrix, np.eye(SIDE)).T
    table[:QUAD_NODES, LANES : LANES + QUAD_NODES] = np.kron(np.eye(SIDE), matrix).T
    table = table.astype(np.float32).astype(np.float64)
    return halves(table), halves(table.T.copy())


def fourier_tables():
    positions = np.arange(PLANES)
    mode_number = positions // 2
    frequency = np.where(positions == 1, PLANES // 2, mode_number)
    angles = 2.0 * math.pi / PLANES * (positions[:, None] * frequency[None, :] % PLANES)
    cosine = np.cos(angles)
    sines = np.sin(angles)
    cos_like = (positions % 2 == 0) | (positions == 1)
    synthesis = np.where(cos_like[None, :], cosine, sines)
    wavenumber = 8.0 / PLANES * mode_number
    slope = np.where(cos_like[None, :], -wavenumber[None, :] * sines, wavenumber[None, :] * cosine)
    weight = np.where(positions < 2, 1.0, 2.0) / PLANES
    retained = (mode_number <= PLANES // 3) & (positions != 1)
    forward = (synthesis * np.where(retained, weight, 0.0)[None, :]).T
    return halves(np.concatenate([synthesis, slope])), halves(forward[:KEPT])


def split2(x):
    high = x.astype(bf16)
    return high, (x - high.astype(f32)).astype(bf16)


def split3(x):
    high = x.astype(bf16)
    rest = x - high.astype(f32)
    middle = rest.astype(bf16)
    return high, middle, (rest - middle.astype(f32)).astype(bf16)


def mm(a, b):
    return jnp.dot(a, b, preferred_element_type=f32)


def times_table(x, table):
    rows = x.shape[0]
    high, low = split2(x)
    both = mm(jnp.concatenate([high, low], axis=0), table[0])
    return both[:rows] + both[rows:] + mm(high, table[1])


def table_times(table, x):
    high, low = split2(x)
    cols = x.shape[1]
    both = mm(table[0], jnp.concatenate([high, low], axis=1))
    return both[:, :cols] + both[:, cols:] + mm(table[1], high)


def times_incidence(x, incidence):
    rows = x.shape[0]
    out = mm(jnp.concatenate(split3(x), axis=0), incidence)
    return out[:rows] + (out[rows : 2 * rows] + out[2 * rows :])


def stacked(x):
    return jnp.concatenate([x[:, LANES * q : LANES * (q + 1)] for q in range(QUADS)], axis=0)


def unstacked(x):
    rows = x.shape[0] // QUADS
    return jnp.concatenate([x[rows * q : rows * (q + 1)] for q in range(QUADS)], axis=1)


def gradient(x, metric, table):
    derived = times_table(stacked(x), table)
    along_r = unstacked(derived[:, :LANES])
    along_s = unstacked(derived[:, LANES:])
    return (
        metric[0:1] * along_r + metric[2:3] * along_s,
        metric[1:2] * along_r + metric[3:4] * along_s,
    )


def rates(mode):
    row = lax.broadcasted_iota(jnp.int32, (ROWS, 1), 0)
    return (8.0 / PLANES) * ((mode * ROWS + row) // 2).astype(f32), row % 2 == 0


def along_z(x, mode):
    rate, even = rates(mode)
    return rate * jnp.where(even, pltpu.roll(x, ROWS - 1, 0), -pltpu.roll(x, 1, 0))


def unpacked(x, field):
    if field:
        x = pltpu.roll(x, PACK - QUAD_NODES * field, 1)
    return x[:, :LANES]


def pack_kernel(velocity, packed):
    for q in range(QUADS):
        for c in range(3):
            packed[q, :, QUAD_NODES * c : QUAD_NODES * (c + 1)] = velocity[
                c, :, QUAD_NODES * q : QUAD_NODES * (q + 1)
            ]
        packed[q, :, 3 * QUAD_NODES :] = jnp.zeros((ROWS, PACK - 3 * QUAD_NODES), f32)


def prepare_kernel(mode, velocity, nodal, ids, edges, field, nodal_wide, own_metric, joins, rims):
    lane = lax.broadcasted_iota(jnp.int32, (1, LANES), 1)
    field[...] = jnp.zeros_like(field)
    nodal_wide[...] = jnp.zeros_like(nodal_wide)
    for q in range(QUADS):
        here = slice(LANES * q, LANES * q + QUAD_NODES)
        there = slice(QUAD_NODES * q, QUAD_NODES * (q + 1))
        for c in range(3):
            field[ROWS * c : ROWS * (c + 1), here] = velocity[c, :, there]
        nodal_wide[0:5, here] = nodal[0:5, there]
        nodal_wide[5:6, here] = jnp.ones((1, QUAD_NODES), f32)
    own = jnp.zeros((8, LANES), f32)
    for q in range(QUADS):
        own = own + jnp.where(mode[0] == q, nodal_wide[:, LANES * q : LANES * (q + 1)], 0.0)
    own_metric[...] = own
    ids_row = [
        jnp.concatenate(
            [
                ids[:, QUAD_NODES * q : QUAD_NODES * (q + 1)],
                jnp.full((1, LANES - QUAD_NODES), -1, jnp.int32),
            ],
            axis=1,
        ).astype(f32)
        for q in range(QUADS)
    ]
    ids_wide = jnp.concatenate(ids_row, axis=1)
    edge_row = [
        jnp.concatenate(
            [edges[s : s + 1, :], jnp.full((1, LANES - EDGE), -2, jnp.int32)], axis=1
        ).astype(f32)
        for s in range(2)
    ]
    edge_wide = jnp.concatenate(edge_row, axis=1)
    columns = jnp.transpose(jnp.concatenate(ids_row, axis=0))
    edge_columns = jnp.transpose(jnp.concatenate(edge_row + [edge_row[0]] * 6, axis=0))
    for q in range(QUADS):
        column = columns[:, q : q + 1]
        joins[LANES * q : LANES * (q + 1), :] = jnp.where(column == ids_wide, 1.0, 0.0).astype(bf16)
        rims[LANES * q : LANES * (q + 1), :] = jnp.where(column == edge_wide, 1.0, 0.0).astype(bf16)
    for s in range(2):
        column = edge_columns[:, s : s + 1]
        joins[WIDE + LANES * s : WIDE + LANES * (s + 1), :] = jnp.where(
            column == ids_wide, 1.0, 0.0
        ).astype(bf16)


def convect_kernel(packed, own_metric, synthesis, forward, derive, out, products):
    coefficients = packed[...].reshape(PLANES, PACK)
    high, low = split2(coefficients)
    both = jnp.concatenate([high, low], axis=1)
    metric = own_metric[...]
    lane = lax.broadcasted_iota(jnp.int32, (1, LANES), 1)
    inside = lane < QUAD_NODES
    table = (derive[0], derive[1])
    chunk = 128

    def planes(first):
        rows = pl.ds(first, chunk)
        wide = mm(synthesis[0, rows, :], both)
        return wide[:, :PACK] + wide[:, PACK:] + mm(synthesis[1, rows, :], high)

    for first in range(0, PLANES, chunk):
        value = planes(first)
        slope = planes(PLANES + first)
        speed = [unpacked(value, c) for c in range(3)]
        derived = times_table(jnp.concatenate(speed, axis=0), table)
        weight_r = speed[0] * metric[0:1] + speed[1] * metric[1:2]
        weight_s = speed[0] * metric[2:3] + speed[1] * metric[3:4]
        total = None
        for c in range(3):
            part = derived[chunk * c : chunk * (c + 1)]
            term = (
                weight_r * part[:, :LANES]
                + weight_s * part[:, LANES:]
                + speed[2] * unpacked(slope, c)
            )
            term = jnp.where(inside, -term, 0.0)
            term = jnp.concatenate([term, jnp.zeros((chunk, PACK - LANES), f32)], axis=1)
            if c:
                term = pltpu.roll(term, QUAD_NODES * c, 1)
            total = term if total is None else total + term
        products[first : first + chunk, :] = total
    spectral = table_times((forward[0], forward[1]), products[...])
    out[0 : KEPT // ROWS] = spectral.reshape(KEPT // ROWS, ROWS, PACK)
    out[KEPT // ROWS :] = jnp.zeros((QUADS - KEPT // ROWS, ROWS, PACK), f32)


def weigh_kernel(spectral, nodal, rims, share, to_prev, to_next):
    for q in range(QUADS):
        here = slice(LANES * q, LANES * (q + 1))
        mass = nodal[4:5, here]
        block = spectral[q]
        for c in range(3):
            share[ROWS * c : ROWS * (c + 1), here] = mass * jnp.where(
                mass > 0.0, unpacked(block, c), 0.0
            )
    share[3 * ROWS : 3 * ROWS + 1, :] = nodal[4:5, :]
    share[3 * ROWS + 1 : 3 * ROWS + 2, :] = nodal[5:6, :]
    share[3 * ROWS + 2 :, :] = jnp.zeros((STACK - 3 * ROWS - 2, WIDE), f32)
    rim = times_incidence(share[...], rims[...])
    to_prev[...] = rim[:, :LANES]
    to_next[...] = rim[:, LANES:]


def joined(share, from_prev, from_next, joins):
    return times_incidence(
        jnp.concatenate([share[...], from_prev[...], from_next[...]], axis=1), joins[...]
    )


def star_kernel(
    mode, share, from_prev, from_next, joins, rims, field, nodal, derive,
    star, inverse, share_out, to_prev, to_next,
):
    total = joined(share, from_prev, from_next, joins)
    metric = nodal[...]
    inside = metric[5:6] > 0.0
    scale = TIME_STEP / jnp.where(inside, total[3 * ROWS : 3 * ROWS + 1], 1.0)
    inverse[...] = jnp.where(
        inside, 1.0 / jnp.where(inside, total[3 * ROWS + 1 : 3 * ROWS + 2], 1.0), 0.0
    )
    star[...] = field[...] + scale * total[: 3 * ROWS]
    table = (derive[0], derive[1])
    star_x = gradient(star[0:ROWS], metric, table)[0]
    star_y = gradient(star[ROWS : 2 * ROWS], metric, table)[1]
    divergence = star_x + star_y + along_z(star[2 * ROWS :], mode[0])
    result = (-1.0 / TIME_STEP) * (metric[4:5] * divergence)
    share_out[...] = result
    rim = times_incidence(result, rims[...])
    to_prev[...] = rim[:, :LANES]
    to_next[...] = rim[:, LANES:]


def lane_sum(x):
    total = x[:, :LANES]
    for q in range(1, QUADS):
        total = total + x[:, LANES * q : LANES * (q + 1)]
    return jnp.sum(total, axis=1, keepdims=True)


def helmholtz_kernel(
    mode, share, from_prev, from_next, joins, rims, nodal, inverse, derive, derive_back,
    right, right_x, right_y, share_out, to_prev, to_next, sums,
):
    total = joined(share, from_prev, from_next, joins)
    metric = nodal[...]
    mass = metric[4:5]
    rate, even = rates(mode[0])
    shift = rate * rate + PENALTY
    grad_x, grad_y = gradient(total, metric, (derive[0], derive[1]))
    right[...] = total
    right_x[...] = grad_x
    right_y[...] = grad_y
    flux_x = mass * grad_x
    flux_y = mass * grad_y
    weighted = shift * (mass * total)
    part_r = metric[0:1] * flux_x + metric[1:2] * flux_y
    part_s = metric[2:3] * flux_x + metric[3:4] * flux_y
    both = jnp.concatenate([stacked(part_r), stacked(part_s)], axis=1)
    result = unstacked(times_table(both, (derive_back[0], derive_back[1]))) + weighted
    share_out[...] = result
    rim = times_incidence(result, rims[...])
    to_prev[...] = rim[:, :LANES]
    to_next[...] = rim[:, LANES:]
    square = lane_sum(total * total * inverse[...])
    energy = lane_sum(flux_x * grad_x + flux_y * grad_y + weighted * total)
    column = lax.broadcasted_iota(jnp.int32, (ROWS, LANES), 1)
    sums[...] = jnp.where(column == 0, square, jnp.where(column == 1, energy, 0.0))


def image_kernel(
    mode, share, from_prev, from_next, joins, nodal, inverse, derive, sums,
    image, image_x, image_y, spread,
):
    total = joined(share, from_prev, from_next, joins)
    metric = nodal[...]
    mass = metric[4:5]
    rate, even = rates(mode[0])
    shift = rate * rate + PENALTY
    grad_x, grad_y = gradient(total, metric, (derive[0], derive[1]))
    image[...] = total
    image_x[...] = grad_x
    image_y[...] = grad_y
    square = lane_sum(total * total * inverse[...])
    energy = lane_sum(mass * (grad_x * grad_x + grad_y * grad_y + shift * (total * total)))
    column = lax.broadcasted_iota(jnp.int32, (ROWS, LANES), 1)
    table = jnp.where(column == 2, square, jnp.where(column == 3, energy, sums[...]))
    table = jnp.concatenate([table, jnp.zeros((LANES - ROWS, LANES), f32)], axis=0)
    turned = jnp.transpose(table)
    short = jnp.concatenate(
        [
            turned[0:1] + pltpu.roll(turned[1:2], ROWS, 1),
            turned[2:3] + pltpu.roll(turned[3:4], ROWS, 1),
        ],
        axis=1,
    )
    spread[...] = jnp.broadcast_to(short, spread.shape)


def finish_kernel(
    mode, gathered, star, right, right_x, right_y, image, image_x, image_y,
    velocity_out, pressure_out,
):
    sums = jnp.sum(gathered[...], axis=0, keepdims=True)
    first = sums[:, :LANES]
    second = sums[:, LANES:]
    g0 = first
    g1 = pltpu.roll(first, ROWS, 1)
    g2 = second
    g3 = pltpu.roll(second, ROWS, 1)
    step0 = g0 / g1
    new = step0 * step0 * g2 - g0
    ratio = new / g0
    curve = (1.0 + ratio) * ((1.0 + ratio) * g1 - 2.0 * step0 * g2) + step0 * step0 * g3
    step1 = new / curve
    by_right = step0 + step1 * (1.0 + ratio)
    by_image = -step1 * step0
    pair = jnp.concatenate([by_right, by_image, jnp.zeros((6, LANES), f32)], axis=0)
    turned = jnp.transpose(pair)
    by_right = turned[:ROWS, 0:1]
    by_image = turned[:ROWS, 1:2]
    pressure = by_right * right[...] + by_image * image[...]
    outs = [
        star[0:ROWS] - TIME_STEP * (by_right * right_x[...] + by_image * image_x[...]),
        star[ROWS : 2 * ROWS] - TIME_STEP * (by_right * right_y[...] + by_image * image_y[...]),
        star[2 * ROWS :] - TIME_STEP * along_z(pressure, mode[0]),
    ]
    for q in range(QUADS):
        here = slice(QUAD_NODES * q, QUAD_NODES * (q + 1))
        there = slice(LANES * q, LANES * q + QUAD_NODES)
        for c in range(3):
            velocity_out[c, :, here] = outs[c][:, there]
        pressure_out[:, here] = pressure[:, there]


VMEM = pl.BlockSpec(memory_space=pltpu.VMEM)
SMEM = pl.BlockSpec(memory_space=pltpu.SMEM)


def call(kernel, ins, outs, scratch=(), flops=0, name=None):
    specs = [SMEM if a.dtype == jnp.int32 and a.shape == (1,) else VMEM for a in ins]
    shapes = [jax.ShapeDtypeStruct(s, d) for s, d in outs]
    size = sum(math.prod(a.shape) * a.dtype.itemsize for a in list(ins) + shapes)
    return pl.pallas_call(
        kernel,
        in_specs=specs,
        out_specs=[VMEM] * len(shapes),
        out_shape=shapes,
        scratch_shapes=list(scratch),
        name=name,
        cost_estimate=pl.CostEstimate(flops=flops, bytes_accessed=size, transcendentals=0),
        compiler_params=pltpu.CompilerParams(vmem_limit_bytes=40 * 1024 * 1024),
    )(*ins)


def on_device(velocity, metric, mass, local_ids, edge_ids):
    derive, derive_back = (jnp.asarray(t) for t in derivative_tables())
    synthesis, forward = (jnp.asarray(t) for t in fourier_tables())
    mode = lax.axis_index("mode").astype(jnp.int32).reshape(1)
    count = lax.axis_size("elem")
    onward = [(i, (i + 1) % count) for i in range(count)]
    backward = [(target, source) for source, target in onward]

    def swap(to_prev, to_next):
        return lax.ppermute(to_next, "elem", onward), lax.ppermute(to_prev, "elem", backward)

    (packed,) = call(pack_kernel, [velocity], [((QUADS, ROWS, PACK), f32)], name="pack")
    nodal = jnp.concatenate([metric, mass[None]], axis=0)
    field, nodal, own_metric, joins, rims = call(
        prepare_kernel,
        [mode, velocity, nodal, local_ids[None], edge_ids[0]],
        [
            ((3 * ROWS, WIDE), f32),
            ((8, WIDE), f32),
            ((8, LANES), f32),
            ((WIDE + 2 * LANES, WIDE), bf16),
            ((WIDE, 2 * LANES), bf16),
        ],
        flops=1 << 24,
        name="prepare",
    )
    arrived = lax.all_to_all(packed, "mode", 0, 0)
    (spectral,) = call(
        convect_kernel,
        [arrived, own_metric, synthesis, forward, derive],
        [((QUADS, ROWS, PACK), f32)],
        scratch=[pltpu.VMEM((PLANES, PACK), f32)],
        flops=1 << 30,
        name="convect",
    )
    returned = lax.all_to_all(spectral, "mode", 0, 0)
    rim_out = [((STACK, LANES), f32)] * 2
    share, to_prev, to_next = call(
        weigh_kernel, [returned, nodal, rims], [((STACK, WIDE), f32)] + rim_out,
        flops=1 << 28, name="weigh",
    )
    from_prev, from_next = swap(to_prev, to_next)
    one = ((ROWS, WIDE), f32)
    rim_out = [((ROWS, LANES), f32)] * 2
    star, inverse, share, to_prev, to_next = call(
        star_kernel,
        [mode, share, from_prev, from_next, joins, rims, field, nodal, derive],
        [((3 * ROWS, WIDE), f32), ((1, WIDE), f32), one] + rim_out,
        flops=1 << 29, name="star",
    )
    from_prev, from_next = swap(to_prev, to_next)
    right, right_x, right_y, share, to_prev, to_next, sums = call(
        helmholtz_kernel,
        [mode, share, from_prev, from_next, joins, rims, nodal, inverse, derive, derive_back],
        [one, one, one, one] + rim_out + [((ROWS, LANES), f32)],
        flops=1 << 29, name="helmholtz",
    )
    from_prev, from_next = swap(to_prev, to_next)
    image, image_x, image_y, spread = call(
        image_kernel,
        [mode, share, from_prev, from_next, joins, nodal, inverse, derive, sums],
        [one, one, one, ((count, 1, 2 * LANES), f32)],
        flops=1 << 29, name="image",
    )
    gathered = lax.all_to_all(spread, "elem", 0, 0)
    gathered = gathered.reshape(count, 2 * LANES)
    velocity_new, pressure = call(
        finish_kernel,
        [mode, gathered, star, right, right_x, right_y, image, image_x, image_y],
        [((3, ROWS, QUADS * QUAD_NODES), f32), ((ROWS, QUADS * QUAD_NODES), f32)],
        name="finish",
    )
    return velocity_new, pressure


def solution(mesh):
    in_specs = (
        P(None, "mode", "elem"),
        P(None, "elem"),
        P("elem"),
        P("elem"),
        P("elem", None, None),
    )
    out_specs = (P(None, "mode", "elem"), P("mode", "elem"))
    return jax.shard_map(
        on_device, mesh=mesh, in_specs=in_specs, out_specs=out_specs, check_vma=False
    )
```

```python
import functools
import math

import jax
import jax.numpy as jnp
import numpy as np
from jax import lax
from jax.experimental import pallas as pl
from jax.experimental.pallas import tpu as pltpu
from jax.sharding import PartitionSpec as P

SIDE = 9
QUAD_NODES = 81
PLANES = 512
QUADS = 8
EDGE = 65
LANES = 128
WIDE = QUADS * LANES
PACK = 256
ROWS = 64
KEPT = 192
STACK = 200
CHUNK = 64
HALF = 256

PENALTY = 1.0
TIME_STEP = 0.01

f32 = jnp.float32
bf16 = jnp.bfloat16


def legendre_pair(points, degree):
    previous = points * 0.0 + 1.0
    current = points.copy()
    for order in range(2, degree + 1):
        following = ((2.0 * order - 1.0) * points * current - (order - 1.0) * previous) / order
        previous = current
        current = following
    return (previous, current)


def derivative_matrix():
    degree = SIDE - 1
    points = np.cos(math.pi * np.arange(degree + 1) / degree)
    for sweep in range(100):
        lower, upper = legendre_pair(points, degree)
        points = points - (points * upper - lower) / ((degree + 1.0) * upper)
    points = points[::-1].copy()
    values = legendre_pair(points, degree)[1]
    identity = np.eye(SIDE)
    differ = points[:, None] - points[None, :] + identity
    matrix = np.where(identity > 0.5, 0.0, values[:, None] / (values[None, :] * differ))
    matrix[0, 0] = -degree * (degree + 1) / 4.0
    matrix[degree, degree] = degree * (degree + 1) / 4.0
    return matrix


def halves(table):
    high = table.astype(np.float32).astype(jnp.bfloat16)
    low = (table - high.astype(np.float64)).astype(np.float32).astype(jnp.bfloat16)
    return np.stack([high, low])


def derivative_tables():
    matrix = derivative_matrix()
    table = np.zeros((LANES, 2 * LANES))
    table[:QUAD_NODES, :QUAD_NODES] = np.kron(matrix, np.eye(SIDE)).T
    table[:QUAD_NODES, LANES : LANES + QUAD_NODES] = np.kron(np.eye(SIDE), matrix).T
    table = table.astype(np.float32).astype(np.float64)
    return halves(table), halves(table.T.copy())


def fourier_tables():
    index = np.arange(HALF)
    angles = 2.0 * math.pi / PLANES * (index[:, None] * index[None, :] % PLANES)
    return np.stack([halves(np.cos(angles)), halves(np.sin(angles))])


def split2(x):
    high = x.astype(bf16)
    return high, (x - high.astype(f32)).astype(bf16)


def split3(x):
    high = x.astype(bf16)
    rest = x - high.astype(f32)
    middle = rest.astype(bf16)
    return high, middle, (rest - middle.astype(f32)).astype(bf16)


def mm(a, b):
    return jnp.dot(a, b, preferred_element_type=f32)


def times_table(x, table):
    rows = x.shape[0]
    high, low = split2(x)
    both = mm(jnp.concatenate([high, low], axis=0), table[0])
    return both[:rows] + both[rows:] + mm(high, table[1])


def table_times(table, x):
    high, low = split2(x)
    cols = x.shape[1]
    both = mm(table[0], jnp.concatenate([high, low], axis=1))
    return both[:, :cols] + both[:, cols:] + mm(table[1], high)


def times_incidence(x, incidence):
    rows = x.shape[0]
    out = mm(jnp.concatenate(split3(x), axis=0), incidence)
    return out[:rows] + (out[rows : 2 * rows] + out[2 * rows :])


def stacked(x):
    return jnp.concatenate([x[:, LANES * q : LANES * (q + 1)] for q in range(QUADS)], axis=0)


def unstacked(x):
    rows = x.shape[0] // QUADS
    return jnp.concatenate([x[rows * q : rows * (q + 1)] for q in range(QUADS)], axis=1)


def gradient(x, metric, table):
    derived = times_table(stacked(x), table)
    along_r = unstacked(derived[:, :LANES])
    along_s = unstacked(derived[:, LANES:])
    return (
        metric[0:1] * along_r + metric[2:3] * along_s,
        metric[1:2] * along_r + metric[3:4] * along_s,
    )


def rates(mode):
    row = lax.broadcasted_iota(jnp.int32, (ROWS, 1), 0)
    return (8.0 / PLANES) * ((mode * ROWS + row) // 2).astype(f32), row % 2 == 0


def along_z(x, mode):
    rate, even = rates(mode)
    return rate * jnp.where(even, pltpu.roll(x, ROWS - 1, 0), -pltpu.roll(x, 1, 0))


def unpacked(x, field):
    if field:
        x = pltpu.roll(x, PACK - QUAD_NODES * field, 1)
    return x[:, :LANES]


def pack_kernel(velocity, packed):
    for q in range(QUADS):
        for c in range(3):
            start, stop = QUAD_NODES * c, QUAD_NODES * (c + 1)
            for tile in range(start // LANES, (stop - 1) // LANES + 1):
                low, high = max(start, LANES * tile), min(stop, LANES * (tile + 1))
                node = QUAD_NODES * q - start
                packed[q, tile, :, low - LANES * tile : high - LANES * tile] = velocity[
                    c, :, node + low : node + high
                ]
        packed[q, 1, :, 3 * QUAD_NODES - LANES :] = jnp.zeros((ROWS, PACK - 3 * QUAD_NODES), f32)


def matches(column, row):
    return jnp.where(column == row, 1.0, 0.0)


def prepare_kernel(
    mode, velocity, nodal, ids, edges, fourier, derive,
    field, nodal_wide, own_metric, joins, rims, fourier_on, derive_on,
):
    lane = lax.broadcasted_iota(jnp.int32, (1, LANES), 1)
    inside = lane < QUAD_NODES
    field[...] = jnp.zeros_like(field)
    nodal_wide[...] = jnp.zeros_like(nodal_wide)
    for q in range(QUADS):
        here = slice(LANES * q, LANES * q + QUAD_NODES)
        there = slice(QUAD_NODES * q, QUAD_NODES * (q + 1))
        for c in range(3):
            field[ROWS * c : ROWS * (c + 1), here] = velocity[c, :, there]
        nodal_wide[0:5, here] = nodal[0:5, there]
        nodal_wide[5:6, here] = jnp.ones((1, QUAD_NODES), f32)
    own = jnp.zeros((8, LANES), f32)
    for q in range(QUADS):
        own = own + jnp.where(mode[0] == q, nodal_wide[:, LANES * q : LANES * (q + 1)], 0.0)
    own_metric[...] = own
    ids_row = [
        jnp.concatenate(
            [
                ids[:, QUAD_NODES * q : QUAD_NODES * (q + 1)],
                jnp.full((1, LANES - QUAD_NODES), -1, jnp.int32),
            ],
            axis=1,
        ).astype(f32)
        for q in range(QUADS)
    ]
    ids_wide = jnp.concatenate(ids_row, axis=1)
    edge_row = [
        jnp.concatenate(
            [edges[s : s + 1, :], jnp.full((1, LANES - EDGE), -2, jnp.int32)], axis=1
        ).astype(f32)
        for s in range(2)
    ]
    columns = jnp.transpose(jnp.concatenate(ids_row, axis=0))
    column = [columns[:, q : q + 1] for q in range(QUADS)]
    row_at = lax.broadcasted_iota(jnp.int32, (LANES, LANES), 0)
    lane_at = lax.broadcasted_iota(jnp.int32, (LANES, LANES), 1)
    opens = []
    for q in range(QUADS):
        total = jnp.zeros((LANES, LANES), f32)
        before = jnp.zeros((LANES, LANES), f32)
        for p in range(QUADS):
            same = matches(column[p], ids_row[q])
            total = total + same
            if p < q:
                before = before + same
            if p == q:
                before = before + jnp.where(row_at < lane_at, same, 0.0)
        copies = jnp.sum(total, axis=0, keepdims=True)
        earlier = jnp.sum(before, axis=0, keepdims=True)
        shared = jnp.where(inside & (copies > 1.5), 1.0, 0.0)
        opens.append(jnp.where(earlier < 0.5, shared, 0.0))
        nodal_wide[6:7, LANES * q : LANES * (q + 1)] = jnp.where(inside, 1.0 - shared, 0.0)
    opens = jnp.concatenate(opens, axis=0)
    triangle = jnp.where(row_at < lane_at, 1.0, 0.0).astype(bf16)
    rank = mm(opens.astype(bf16), triangle)
    counts = jnp.sum(opens, axis=1, keepdims=True)
    offset = jnp.zeros((1, 1), f32)
    offsets = []
    for q in range(QUADS):
        offsets.append(offset)
        offset = offset + counts[q : q + 1]
    slot = jnp.where(opens > 0.5, rank + jnp.concatenate(offsets, axis=0) + float(EDGE), -1.0)
    slots = jnp.transpose(slot)
    lanes = lane.astype(f32)
    hits = jnp.zeros((LANES, LANES), f32)
    named = jnp.zeros((LANES, LANES), f32)
    for q in range(QUADS):
        hit = matches(slots[:, q : q + 1], lanes)
        hits = hits + hit
        named = named + hit * column[q]
    hits = jnp.sum(hits, axis=0, keepdims=True)
    named = jnp.sum(named, axis=0, keepdims=True)
    first = jnp.where(lane < EDGE, edge_row[0], jnp.where(hits > 0.5, named, -3.0))
    keys = [first, edge_row[1]]
    key_columns = jnp.transpose(jnp.concatenate(keys + [first] * 6, axis=0))
    for q in range(QUADS):
        for s in range(2):
            rims[LANES * q : LANES * (q + 1), LANES * s : LANES * (s + 1)] = matches(
                column[q], keys[s]
            ).astype(bf16)
    for s in range(2):
        joins[LANES * s : LANES * (s + 1), :] = matches(
            key_columns[:, s : s + 1], ids_wide
        ).astype(bf16)


def convect_kernel(packed, own_metric, fourier, derive, out, even, odd, sums, differences):
    cosine = (fourier[0, 0], fourier[0, 1])
    sine = (fourier[1, 0], fourier[1, 1])
    metric = own_metric[...]
    lane = lax.broadcasted_iota(jnp.int32, (1, LANES), 1)
    inside = lane < QUAD_NODES
    table = (derive[0], derive[1])
    index = lax.broadcasted_iota(jnp.int32, (HALF, 1), 0)
    rate = (8.0 / PLANES) * index.astype(f32)
    sign = jnp.where(index % 2 == 0, 1.0, -1.0)
    cosines, sines = (
        jnp.concatenate(
            [
                jnp.concatenate(
                    [packed[m, tile, pl.ds(parity, ROWS // 2, stride=2), :] for tile in range(2)],
                    axis=1,
                )
                for m in range(QUADS)
            ],
            axis=0,
        )
        for parity in range(2)
    )
    highest = sines[0:1]
    to_even = jnp.concatenate([cosines, rate * sines], axis=1)
    to_odd = jnp.concatenate([sines, -rate * cosines], axis=1)
    even[...] = table_times(cosine, to_even)
    even[:, :PACK] = even[:, :PACK] + sign * highest
    middle = jnp.sum(sign * to_even, axis=0, keepdims=True)
    middle = middle + jnp.concatenate([highest, jnp.zeros_like(highest)], axis=1)
    odd[...] = table_times(sine, to_odd)
    opening = lax.broadcasted_iota(jnp.int32, (CHUNK, 1), 0) == 0
    product_middle = None
    for i in range(HALF // CHUNK):
        rows = slice(CHUNK * i, CHUNK * (i + 1))
        part_even = even[rows]
        part_odd = odd[rows]
        ahead = part_even + part_odd
        if i == 0:
            part_even = jnp.where(opening, middle, part_even)
        wide = jnp.concatenate([ahead, part_even - part_odd], axis=0)
        value = wide[:, :PACK]
        slope = wide[:, PACK:]
        speed = [unpacked(value, c) for c in range(3)]
        derived = times_table(jnp.concatenate(speed, axis=0), table)
        weight_r = speed[0] * metric[0:1] + speed[1] * metric[1:2]
        weight_s = speed[0] * metric[2:3] + speed[1] * metric[3:4]
        total = None
        for c in range(3):
            part = derived[2 * CHUNK * c : 2 * CHUNK * (c + 1)]
            term = (
                weight_r * part[:, :LANES]
                + weight_s * part[:, LANES:]
                + speed[2] * unpacked(slope, c)
            )
            term = jnp.where(inside, -term, 0.0)
            term = jnp.concatenate([term, jnp.zeros((2 * CHUNK, PACK - LANES), f32)], axis=1)
            if c:
                term = pltpu.roll(term, QUAD_NODES * c, 1)
            total = term if total is None else total + term
        ahead = total[:CHUNK]
        mirror = total[CHUNK:]
        differences[rows, :] = ahead - mirror
        if i == 0:
            product_middle = mirror[0:1]
            mirror = jnp.where(opening, 0.0, mirror)
        sums[rows, :] = ahead + mirror
    index = index[:KEPT]
    weight = jnp.where(index <= PLANES // 3, 2.0 / PLANES, 0.0)
    kept = [(fourier[t, 0, :KEPT], fourier[t, 1, :KEPT]) for t in range(2)]
    result = table_times(kept[0], sums[...]) + sign[:KEPT] * product_middle
    results = [jnp.where(index == 0, 0.5 * weight, weight) * result]
    result = table_times(kept[1], differences[...])
    results.append(jnp.where(index == 0, 0.0, weight) * result)
    half = ROWS // 2
    for m in range(KEPT // half):
        for tile in range(2):
            for parity in range(2):
                out[m, tile, pl.ds(parity, half, stride=2), :] = results[parity][
                    half * m : half * (m + 1), LANES * tile : LANES * (tile + 1)
                ]
    out[KEPT // half :] = jnp.zeros((QUADS - KEPT // half, 2, ROWS, LANES), f32)


def weigh_kernel(spectral, nodal, rims, share, to_prev, to_next):
    for q in range(QUADS):
        here = slice(LANES * q, LANES * (q + 1))
        mass = nodal[4:5, here]
        block = jnp.concatenate([spectral[q, 0], spectral[q, 1]], axis=1)
        for c in range(3):
            share[ROWS * c : ROWS * (c + 1), here] = mass * jnp.where(
                mass > 0.0, unpacked(block, c), 0.0
            )
    share[3 * ROWS : 3 * ROWS + 1, :] = nodal[4:5, :]
    share[3 * ROWS + 1 : 3 * ROWS + 2, :] = nodal[5:6, :]
    share[3 * ROWS + 2 :, :] = jnp.zeros((STACK - 3 * ROWS - 2, WIDE), f32)
    rim = times_incidence(share[...], rims[...])
    to_prev[...] = rim[:, :LANES]
    to_next[...] = rim[:, LANES:]


def joined(share, own, from_prev, from_next, joins, single):
    lane = lax.broadcasted_iota(jnp.int32, (1, LANES), 1)
    near = jnp.where(lane < EDGE, from_prev[...], own[...])
    sums = jnp.concatenate([near, from_next[...]], axis=1)
    return share[...] * single + times_incidence(sums, joins[...])


def star_kernel(
    mode, share, own, from_prev, from_next, joins, rims, field, nodal, derive,
    star, inverse, share_out, to_prev, to_next,
):
    metric = nodal[...]
    total = joined(share, own, from_prev, from_next, joins, metric[6:7])
    inside = metric[5:6] > 0.0
    scale = TIME_STEP / jnp.where(inside, total[3 * ROWS : 3 * ROWS + 1], 1.0)
    inverse[...] = jnp.where(
        inside, 1.0 / jnp.where(inside, total[3 * ROWS + 1 : 3 * ROWS + 2], 1.0), 0.0
    )
    star[...] = field[...] + scale * total[: 3 * ROWS]
    table = (derive[0], derive[1])
    star_x = gradient(star[0:ROWS], metric, table)[0]
    star_y = gradient(star[ROWS : 2 * ROWS], metric, table)[1]
    divergence = star_x + star_y + along_z(star[2 * ROWS :], mode[0])
    result = (-1.0 / TIME_STEP) * (metric[4:5] * divergence)
    share_out[...] = result
    rim = times_incidence(result, rims[...])
    to_prev[...] = rim[:, :LANES]
    to_next[...] = rim[:, LANES:]


def lane_sum(x):
    total = x[:, :LANES]
    for q in range(1, QUADS):
        total = total + x[:, LANES * q : LANES * (q + 1)]
    return jnp.sum(total, axis=1, keepdims=True)


def helmholtz_kernel(
    mode, share, own, from_prev, from_next, joins, rims, nodal, inverse, derive, derive_back,
    right, right_x, right_y, share_out, to_prev, to_next, sums,
):
    metric = nodal[...]
    total = joined(share, own, from_prev, from_next, joins, metric[6:7])
    mass = metric[4:5]
    rate, even = rates(mode[0])
    shift = rate * rate + PENALTY
    grad_x, grad_y = gradient(total, metric, (derive[0], derive[1]))
    right[...] = total
    right_x[...] = grad_x
    right_y[...] = grad_y
    flux_x = mass * grad_x
    flux_y = mass * grad_y
    weighted = shift * (mass * total)
    part_r = metric[0:1] * flux_x + metric[1:2] * flux_y
    part_s = metric[2:3] * flux_x + metric[3:4] * flux_y
    both = jnp.concatenate([stacked(part_r), stacked(part_s)], axis=1)
    result = unstacked(times_table(both, (derive_back[0], derive_back[1]))) + weighted
    share_out[...] = result
    rim = times_incidence(result, rims[...])
    to_prev[...] = rim[:, :LANES]
    to_next[...] = rim[:, LANES:]
    square = lane_sum(total * total * inverse[...])
    energy = lane_sum(flux_x * grad_x + flux_y * grad_y + weighted * total)
    column = lax.broadcasted_iota(jnp.int32, (ROWS, LANES), 1)
    sums[...] = jnp.where(column == 0, square, jnp.where(column == 1, energy, 0.0))


def image_kernel(
    mode, share, own, from_prev, from_next, joins, nodal, inverse, derive, sums,
    image, image_x, image_y, spread,
):
    metric = nodal[...]
    total = joined(share, own, from_prev, from_next, joins, metric[6:7])
    mass = metric[4:5]
    rate, even = rates(mode[0])
    shift = rate * rate + PENALTY
    grad_x, grad_y = gradient(total, metric, (derive[0], derive[1]))
    image[...] = total
    image_x[...] = grad_x
    image_y[...] = grad_y
    square = lane_sum(total * total * inverse[...])
    energy = lane_sum(mass * (grad_x * grad_x + grad_y * grad_y + shift * (total * total)))
    column = lax.broadcasted_iota(jnp.int32, (ROWS, LANES), 1)
    table = jnp.where(column == 2, square, jnp.where(column == 3, energy, sums[...]))
    table = jnp.concatenate([table, jnp.zeros((LANES - ROWS, LANES), f32)], axis=0)
    turned = jnp.transpose(table)
    short = jnp.concatenate(
        [
            turned[0:1] + pltpu.roll(turned[1:2], ROWS, 1),
            turned[2:3] + pltpu.roll(turned[3:4], ROWS, 1),
        ],
        axis=1,
    )
    spread[...] = jnp.broadcast_to(short, spread.shape)


def finish_kernel(
    mode, gathered, star, right, right_x, right_y, image, image_x, image_y,
    velocity_out, pressure_out,
):
    sums = jnp.sum(gathered[...], axis=0, keepdims=True)
    first = sums[:, :LANES]
    second = sums[:, LANES:]
    g0 = first
    g1 = pltpu.roll(first, ROWS, 1)
    g2 = second
    g3 = pltpu.roll(second, ROWS, 1)
    step0 = g0 / g1
    new = step0 * step0 * g2 - g0
    ratio = new / g0
    curve = (1.0 + ratio) * ((1.0 + ratio) * g1 - 2.0 * step0 * g2) + step0 * step0 * g3
    step1 = new / curve
    by_right = step0 + step1 * (1.0 + ratio)
    by_image = -step1 * step0
    pair = jnp.concatenate([by_right, by_image, jnp.zeros((6, LANES), f32)], axis=0)
    turned = jnp.transpose(pair)
    by_right = turned[:ROWS, 0:1]
    by_image = turned[:ROWS, 1:2]
    pressure = by_right * right[...] + by_image * image[...]
    slopes = [
        by_right * right_x[...] + by_image * image_x[...],
        by_right * right_y[...] + by_image * image_y[...],
        along_z(pressure, mode[0]),
    ]
    outs = [star[ROWS * c : ROWS * (c + 1)] - TIME_STEP * slopes[c] for c in range(3)]
    for q in range(QUADS):
        here = slice(QUAD_NODES * q, QUAD_NODES * (q + 1))
        there = slice(LANES * q, LANES * q + QUAD_NODES)
        for c in range(3):
            velocity_out[c, :, here] = outs[c][:, there]
        pressure_out[:, here] = pressure[:, there]


VMEM = pl.BlockSpec(memory_space=pltpu.VMEM)
SMEM = pl.BlockSpec(memory_space=pltpu.SMEM)
ANY = pl.BlockSpec(memory_space=pl.ANY)


def call(kernel, ins, outs, scratch=(), flops=0, name=None, aliases={}):
    specs = [SMEM if a.dtype == jnp.int32 and a.shape == (1,) else VMEM for a in ins]
    specs = [ANY if i in aliases else spec for i, spec in enumerate(specs)]
    shapes = [jax.ShapeDtypeStruct(s, d) for s, d in outs]
    size = sum(math.prod(a.shape) * a.dtype.itemsize for a in list(ins) + shapes)
    return pl.pallas_call(
        kernel,
        in_specs=specs,
        out_specs=[ANY if i in aliases.values() else VMEM for i in range(len(shapes))],
        out_shape=shapes,
        scratch_shapes=list(scratch),
        input_output_aliases=aliases,
        name=name,
        cost_estimate=pl.CostEstimate(flops=flops, bytes_accessed=size, transcendentals=0),
        compiler_params=pltpu.CompilerParams(vmem_limit_bytes=40 * 1024 * 1024),
    )(*ins)


def on_device(velocity, metric, mass, local_ids, edge_ids):
    derive, derive_back = (jnp.asarray(t) for t in derivative_tables())
    fourier = jnp.asarray(fourier_tables())
    mode = lax.axis_index("mode").astype(jnp.int32).reshape(1)
    count = lax.axis_size("elem")
    onward = [(i, (i + 1) % count) for i in range(count)]
    backward = [(target, source) for source, target in onward]

    def swap(to_prev, to_next):
        return lax.ppermute(to_next, "elem", onward), lax.ppermute(to_prev, "elem", backward)

    block = (QUADS, 2, ROWS, LANES)
    (packed,) = call(
        pack_kernel, [velocity], [(block, f32)],
        name="pack",
    )
    nodal = jnp.concatenate([metric, mass[None]], axis=0)
    tables = [fourier, derive]
    field, nodal, own_metric, joins, rims, fourier, derive = call(
        prepare_kernel,
        [mode, velocity, nodal, local_ids[None], edge_ids[0]] + tables,
        [
            ((3 * ROWS, WIDE), f32),
            ((8, WIDE), f32),
            ((8, LANES), f32),
            ((2 * LANES, WIDE), bf16),
            ((WIDE, 2 * LANES), bf16),
        ]
        + [(t.shape, bf16) for t in tables],
        flops=1 << 24,
        name="prepare",
        aliases={5: 5, 6: 6},
    )
    arrived = lax.all_to_all(packed, "mode", 0, 0)
    (spectral,) = call(
        convect_kernel,
        [arrived, own_metric, fourier, derive],
        [(block, f32)],
        scratch=[pltpu.VMEM((HALF, 2 * PACK), f32)] * 2 + [pltpu.VMEM((HALF, PACK), f32)] * 2,
        flops=1 << 30,
        name="convect",
    )
    returned = lax.all_to_all(spectral, "mode", 0, 0)
    rim_out = [((STACK, LANES), f32)] * 2
    share, to_prev, to_next = call(
        weigh_kernel, [returned, nodal, rims], [((STACK, WIDE), f32)] + rim_out,
        flops=1 << 28, name="weigh",
    )
    from_prev, from_next = swap(to_prev, to_next)
    one = ((ROWS, WIDE), f32)
    rim_out = [((ROWS, LANES), f32)] * 2
    star, inverse, share, to_prev, to_next = call(
        star_kernel,
        [mode, share, to_prev, from_prev, from_next, joins, rims, field, nodal, derive],
        [((3 * ROWS, WIDE), f32), ((1, WIDE), f32), one] + rim_out,
        flops=1 << 29, name="star",
    )
    from_prev, from_next = swap(to_prev, to_next)
    right, right_x, right_y, share, to_prev, to_next, sums = call(
        helmholtz_kernel,
        [mode, share, to_prev, from_prev, from_next, joins, rims, nodal, inverse, derive, derive_back],
        [one, one, one, one] + rim_out + [((ROWS, LANES), f32)],
        flops=1 << 29, name="helmholtz",
    )
    from_prev, from_next = swap(to_prev, to_next)
    image, image_x, image_y, spread = call(
        image_kernel,
        [mode, share, to_prev, from_prev, from_next, joins, nodal, inverse, derive, sums],
        [one, one, one, ((count, 1, 2 * LANES), f32)],
        flops=1 << 29, name="image",
    )
    gathered = lax.all_to_all(spread, "elem", 0, 0)
    gathered = gathered.reshape(count, 2 * LANES)
    velocity_new, pressure = call(
        finish_kernel,
        [mode, gathered, star, right, right_x, right_y, image, image_x, image_y],
        [((3, ROWS, QUADS * QUAD_NODES), f32), ((ROWS, QUADS * QUAD_NODES), f32)],
        name="finish",
    )
    return velocity_new, pressure


def solution(mesh):
    in_specs = (
        P(None, "mode", "elem"),
        P(None, "elem"),
        P("elem"),
        P("elem"),
        P("elem", None, None),
    )
    out_specs = (P(None, "mode", "elem"), P("mode", "elem"))
    return jax.shard_map(
        on_device, mesh=mesh, in_specs=in_specs, out_specs=out_specs, check_vma=False
    )
```

```python
import functools
import math

import jax
import jax.numpy as jnp
import numpy as np
from jax import lax
from jax.experimental import pallas as pl
from jax.experimental.pallas import tpu as pltpu
from jax.sharding import PartitionSpec as P

SIDE = 9
QUAD_NODES = 81
PLANES = 512
QUADS = 8
EDGE = 65
LANES = 128
WIDE = QUADS * LANES
PACK = 256
ROWS = 64
KEPT = 192
STACK = 200
CHUNK = 64
HALF = 256

PENALTY = 1.0
TIME_STEP = 0.01

f32 = jnp.float32
bf16 = jnp.bfloat16


def legendre_pair(points, degree):
    previous = points * 0.0 + 1.0
    current = points.copy()
    for order in range(2, degree + 1):
        following = ((2.0 * order - 1.0) * points * current - (order - 1.0) * previous) / order
        previous = current
        current = following
    return (previous, current)


def derivative_matrix():
    degree = SIDE - 1
    points = np.cos(math.pi * np.arange(degree + 1) / degree)
    for sweep in range(100):
        lower, upper = legendre_pair(points, degree)
        points = points - (points * upper - lower) / ((degree + 1.0) * upper)
    points = points[::-1].copy()
    values = legendre_pair(points, degree)[1]
    identity = np.eye(SIDE)
    differ = points[:, None] - points[None, :] + identity
    matrix = np.where(identity > 0.5, 0.0, values[:, None] / (values[None, :] * differ))
    matrix[0, 0] = -degree * (degree + 1) / 4.0
    matrix[degree, degree] = degree * (degree + 1) / 4.0
    return matrix


def halves(table):
    high = table.astype(np.float32).astype(jnp.bfloat16)
    low = (table - high.astype(np.float64)).astype(np.float32).astype(jnp.bfloat16)
    return high, low


def as_right(table):
    high, low = halves(table)
    return np.concatenate([high, high, low], axis=0)


def as_left(table):
    high, low = halves(table)
    return np.concatenate([high, high, low], axis=1)


def derivative_tables():
    matrix = derivative_matrix()
    table = np.zeros((LANES, 2 * LANES))
    table[:QUAD_NODES, :QUAD_NODES] = np.kron(matrix, np.eye(SIDE)).T
    table[:QUAD_NODES, LANES : LANES + QUAD_NODES] = np.kron(np.eye(SIDE), matrix).T
    table = table.astype(np.float32).astype(np.float64)
    return as_right(table), as_right(table.T.copy())


def fourier_tables():
    index = np.arange(HALF)
    angles = 2.0 * math.pi / PLANES * (index[:, None] * index[None, :] % PLANES)
    return np.stack([as_left(np.cos(angles)), as_left(np.sin(angles))])


def split2(x):
    high = x.astype(bf16)
    return high, (x - high.astype(f32)).astype(bf16)


def split3(x):
    high = x.astype(bf16)
    rest = x - high.astype(f32)
    middle = rest.astype(bf16)
    return high, middle, (rest - middle.astype(f32)).astype(bf16)


def mm(a, b):
    return jnp.dot(a, b, preferred_element_type=f32)


def times_table(x, table):
    high, low = split2(x)
    return mm(jnp.concatenate([high, low, high], axis=1), table)


def table_times(table, x):
    high, low = split2(x)
    return mm(table, jnp.concatenate([high, low, high], axis=0))


def times_incidence(x, incidence):
    rows = x.shape[0]
    out = mm(jnp.concatenate(split3(x), axis=0), incidence)
    return out[:rows] + (out[rows : 2 * rows] + out[2 * rows :])


def stacked(x):
    return jnp.concatenate([x[:, LANES * q : LANES * (q + 1)] for q in range(QUADS)], axis=0)


def unstacked(x):
    rows = x.shape[0] // QUADS
    return jnp.concatenate([x[rows * q : rows * (q + 1)] for q in range(QUADS)], axis=1)


def gradient(x, metric, table):
    derived = times_table(stacked(x), table)
    along_r = unstacked(derived[:, :LANES])
    along_s = unstacked(derived[:, LANES:])
    return (
        metric[0:1] * along_r + metric[2:3] * along_s,
        metric[1:2] * along_r + metric[3:4] * along_s,
    )


def rates(mode):
    row = lax.broadcasted_iota(jnp.int32, (ROWS, 1), 0)
    return (8.0 / PLANES) * ((mode * ROWS + row) // 2).astype(f32), row % 2 == 0


def along_z(x, mode):
    rate, even = rates(mode)
    return rate * jnp.where(even, pltpu.roll(x, ROWS - 1, 0), -pltpu.roll(x, 1, 0))


def unpacked(x, field):
    if field:
        x = pltpu.roll(x, PACK - QUAD_NODES * field, 1)
    return x[:, :LANES]


def pack_kernel(velocity, packed):
    for q in range(QUADS):
        for c in range(3):
            start, stop = QUAD_NODES * c, QUAD_NODES * (c + 1)
            for tile in range(start // LANES, (stop - 1) // LANES + 1):
                low, high = max(start, LANES * tile), min(stop, LANES * (tile + 1))
                node = QUAD_NODES * q - start
                packed[q, tile, :, low - LANES * tile : high - LANES * tile] = velocity[
                    c, :, node + low : node + high
                ]
        packed[q, 1, :, 3 * QUAD_NODES - LANES :] = jnp.zeros((ROWS, PACK - 3 * QUAD_NODES), f32)


def matches(column, row):
    return jnp.where(column == row, 1.0, 0.0)


def prepare_kernel(
    mode, parity, velocity, nodal, ids, edges, fourier, derive,
    field, nodal_wide, own_metric, joins, rims, fourier_on, derive_on,
):
    lane = lax.broadcasted_iota(jnp.int32, (1, LANES), 1)
    inside = lane < QUAD_NODES
    field[...] = jnp.zeros_like(field)
    nodal_wide[...] = jnp.zeros_like(nodal_wide)
    for q in range(QUADS):
        here = slice(LANES * q, LANES * q + QUAD_NODES)
        there = slice(QUAD_NODES * q, QUAD_NODES * (q + 1))
        for c in range(3):
            field[ROWS * c : ROWS * (c + 1), here] = velocity[c, :, there]
        nodal_wide[0:5, here] = nodal[0:5, there]
        nodal_wide[5:6, here] = jnp.ones((1, QUAD_NODES), f32)
    own = jnp.zeros((8, LANES), f32)
    for q in range(QUADS):
        own = own + jnp.where(mode[0] == q, nodal_wide[:, LANES * q : LANES * (q + 1)], 0.0)
    own_metric[...] = own
    ids_row = [
        jnp.concatenate(
            [
                ids[:, QUAD_NODES * q : QUAD_NODES * (q + 1)],
                jnp.full((1, LANES - QUAD_NODES), -1, jnp.int32),
            ],
            axis=1,
        ).astype(f32)
        for q in range(QUADS)
    ]
    ids_wide = jnp.concatenate(ids_row, axis=1)
    odd = parity[0] > 0
    edge_row = [
        jnp.concatenate(
            [
                jnp.where(odd, edges[1 - s : 2 - s, :], edges[s : s + 1, :]),
                jnp.full((1, LANES - EDGE), -2, jnp.int32),
            ],
            axis=1,
        ).astype(f32)
        for s in range(2)
    ]
    columns = jnp.transpose(jnp.concatenate(ids_row, axis=0))
    column = [columns[:, q : q + 1] for q in range(QUADS)]
    row_at = lax.broadcasted_iota(jnp.int32, (LANES, LANES), 0)
    lane_at = lax.broadcasted_iota(jnp.int32, (LANES, LANES), 1)
    opens = []
    for q in range(QUADS):
        total = jnp.zeros((LANES, LANES), f32)
        before = jnp.zeros((LANES, LANES), f32)
        for p in range(QUADS):
            same = matches(column[p], ids_row[q])
            total = total + same
            if p < q:
                before = before + same
            if p == q:
                before = before + jnp.where(row_at < lane_at, same, 0.0)
        copies = jnp.sum(total, axis=0, keepdims=True)
        earlier = jnp.sum(before, axis=0, keepdims=True)
        shared = jnp.where(inside & (copies > 1.5), 1.0, 0.0)
        opens.append(jnp.where(earlier < 0.5, shared, 0.0))
        nodal_wide[6:7, LANES * q : LANES * (q + 1)] = jnp.where(inside, 1.0 - shared, 0.0)
    opens = jnp.concatenate(opens, axis=0)
    triangle = jnp.where(row_at < lane_at, 1.0, 0.0).astype(bf16)
    rank = mm(opens.astype(bf16), triangle)
    counts = jnp.sum(opens, axis=1, keepdims=True)
    offset = jnp.zeros((1, 1), f32)
    offsets = []
    for q in range(QUADS):
        offsets.append(offset)
        offset = offset + counts[q : q + 1]
    slot = jnp.where(opens > 0.5, rank + jnp.concatenate(offsets, axis=0) + float(EDGE), -1.0)
    slots = jnp.transpose(slot)
    lanes = lane.astype(f32)
    hits = jnp.zeros((LANES, LANES), f32)
    named = jnp.zeros((LANES, LANES), f32)
    for q in range(QUADS):
        hit = matches(slots[:, q : q + 1], lanes)
        hits = hits + hit
        named = named + hit * column[q]
    hits = jnp.sum(hits, axis=0, keepdims=True)
    named = jnp.sum(named, axis=0, keepdims=True)
    first = jnp.where(lane < EDGE, edge_row[0], jnp.where(hits > 0.5, named, -3.0))
    keys = [first, edge_row[1]]
    key_columns = jnp.transpose(jnp.concatenate(keys + [first] * 6, axis=0))
    for q in range(QUADS):
        for s in range(2):
            rims[LANES * q : LANES * (q + 1), LANES * s : LANES * (s + 1)] = matches(
                column[q], keys[s]
            ).astype(bf16)
    for s in range(2):
        joins[LANES * s : LANES * (s + 1), :] = matches(
            key_columns[:, s : s + 1], ids_wide
        ).astype(bf16)


def convect_kernel(packed, own_metric, fourier, derive, out, even, odd, sums, differences):
    metric = own_metric[...]
    lane = lax.broadcasted_iota(jnp.int32, (1, LANES), 1)
    inside = lane < QUAD_NODES
    table = derive[...]
    index = lax.broadcasted_iota(jnp.int32, (HALF, 1), 0)
    rate = (8.0 / PLANES) * index.astype(f32)
    sign = jnp.where(index % 2 == 0, 1.0, -1.0)
    cosines, sines = (
        jnp.concatenate(
            [
                jnp.concatenate(
                    [packed[m, tile, pl.ds(parity, ROWS // 2, stride=2), :] for tile in range(2)],
                    axis=1,
                )
                for m in range(QUADS)
            ],
            axis=0,
        )
        for parity in range(2)
    )
    highest = sines[0:1]
    to_even = jnp.concatenate([cosines, rate * sines], axis=1)
    to_odd = jnp.concatenate([sines, -rate * cosines], axis=1)
    even[...] = table_times(fourier[0], to_even)
    even[:, :PACK] = even[:, :PACK] + sign * highest
    middle = jnp.sum(sign * to_even, axis=0, keepdims=True)
    middle = middle + jnp.concatenate([highest, jnp.zeros_like(highest)], axis=1)
    odd[...] = table_times(fourier[1], to_odd)
    opening = lax.broadcasted_iota(jnp.int32, (CHUNK, 1), 0) == 0
    product_middle = None
    for i in range(HALF // CHUNK):
        rows = slice(CHUNK * i, CHUNK * (i + 1))
        part_even = even[rows]
        part_odd = odd[rows]
        ahead = part_even + part_odd
        if i == 0:
            part_even = jnp.where(opening, middle, part_even)
        wide = jnp.concatenate([ahead, part_even - part_odd], axis=0)
        value = wide[:, :PACK]
        slope = wide[:, PACK:]
        speed = [unpacked(value, c) for c in range(3)]
        derived = times_table(jnp.concatenate(speed, axis=0), table)
        weight_r = speed[0] * metric[0:1] + speed[1] * metric[1:2]
        weight_s = speed[0] * metric[2:3] + speed[1] * metric[3:4]
        total = None
        for c in range(3):
            part = derived[2 * CHUNK * c : 2 * CHUNK * (c + 1)]
            term = (
                weight_r * part[:, :LANES]
                + weight_s * part[:, LANES:]
                + speed[2] * unpacked(slope, c)
            )
            term = jnp.where(inside, -term, 0.0)
            term = jnp.concatenate([term, jnp.zeros((2 * CHUNK, PACK - LANES), f32)], axis=1)
            if c:
                term = pltpu.roll(term, QUAD_NODES * c, 1)
            total = term if total is None else total + term
        ahead = total[:CHUNK]
        mirror = total[CHUNK:]
        differences[rows, :] = ahead - mirror
        if i == 0:
            product_middle = mirror[0:1]
            mirror = jnp.where(opening, 0.0, mirror)
        sums[rows, :] = ahead + mirror
    index = index[:KEPT]
    weight = jnp.where(index <= PLANES // 3, 2.0 / PLANES, 0.0)
    result = table_times(fourier[0, :KEPT], sums[...]) + sign[:KEPT] * product_middle
    results = [jnp.where(index == 0, 0.5 * weight, weight) * result]
    result = table_times(fourier[1, :KEPT], differences[...])
    results.append(jnp.where(index == 0, 0.0, weight) * result)
    half = ROWS // 2
    for m in range(KEPT // half):
        for tile in range(2):
            for parity in range(2):
                out[m, tile, pl.ds(parity, half, stride=2), :] = results[parity][
                    half * m : half * (m + 1), LANES * tile : LANES * (tile + 1)
                ]
    out[KEPT // half :] = jnp.zeros((QUADS - KEPT // half, 2, ROWS, LANES), f32)


def weigh_kernel(spectral, nodal, rims, share, first_out, second_out):
    for q in range(QUADS):
        here = slice(LANES * q, LANES * (q + 1))
        mass = nodal[4:5, here]
        block = jnp.concatenate([spectral[q, 0], spectral[q, 1]], axis=1)
        for c in range(3):
            share[ROWS * c : ROWS * (c + 1), here] = mass * jnp.where(
                mass > 0.0, unpacked(block, c), 0.0
            )
    share[3 * ROWS : 3 * ROWS + 1, :] = nodal[4:5, :]
    share[3 * ROWS + 1 : 3 * ROWS + 2, :] = nodal[5:6, :]
    share[3 * ROWS + 2 :, :] = jnp.zeros((STACK - 3 * ROWS - 2, WIDE), f32)
    rim = times_incidence(share[...], rims[...])
    first_out[...] = rim[:, :LANES]
    second_out[...] = rim[:, LANES:]


def joined(share, own, first_in, second_in, joins, single):
    lane = lax.broadcasted_iota(jnp.int32, (1, LANES), 1)
    near = jnp.where(lane < EDGE, first_in[...], own[...])
    sums = jnp.concatenate([near, second_in[...]], axis=1)
    return share[...] * single + times_incidence(sums, joins[...])


def star_kernel(
    mode, share, own, first_in, second_in, joins, rims, field, nodal, derive,
    star, inverse, share_out, first_out, second_out,
):
    metric = nodal[...]
    total = joined(share, own, first_in, second_in, joins, metric[6:7])
    inside = metric[5:6] > 0.0
    scale = TIME_STEP / jnp.where(inside, total[3 * ROWS : 3 * ROWS + 1], 1.0)
    inverse[...] = jnp.where(
        inside, 1.0 / jnp.where(inside, total[3 * ROWS + 1 : 3 * ROWS + 2], 1.0), 0.0
    )
    star[...] = field[...] + scale * total[: 3 * ROWS]
    table = derive[...]
    star_x = gradient(star[0:ROWS], metric, table)[0]
    star_y = gradient(star[ROWS : 2 * ROWS], metric, table)[1]
    divergence = star_x + star_y + along_z(star[2 * ROWS :], mode[0])
    result = (-1.0 / TIME_STEP) * (metric[4:5] * divergence)
    share_out[...] = result
    rim = times_incidence(result, rims[...])
    first_out[...] = rim[:, :LANES]
    second_out[...] = rim[:, LANES:]


def lane_sum(x):
    total = x[:, :LANES]
    for q in range(1, QUADS):
        total = total + x[:, LANES * q : LANES * (q + 1)]
    return jnp.sum(total, axis=1, keepdims=True)


def helmholtz_kernel(
    mode, share, own, first_in, second_in, joins, rims, nodal, inverse, derive, derive_back,
    right, right_x, right_y, share_out, first_out, second_out, sums,
):
    metric = nodal[...]
    total = joined(share, own, first_in, second_in, joins, metric[6:7])
    mass = metric[4:5]
    rate, even = rates(mode[0])
    shift = rate * rate + PENALTY
    grad_x, grad_y = gradient(total, metric, derive[...])
    right[...] = total
    right_x[...] = grad_x
    right_y[...] = grad_y
    flux_x = mass * grad_x
    flux_y = mass * grad_y
    weighted = shift * (mass * total)
    part_r = metric[0:1] * flux_x + metric[1:2] * flux_y
    part_s = metric[2:3] * flux_x + metric[3:4] * flux_y
    both = jnp.concatenate([stacked(part_r), stacked(part_s)], axis=1)
    result = unstacked(times_table(both, derive_back[...])) + weighted
    share_out[...] = result
    rim = times_incidence(result, rims[...])
    first_out[...] = rim[:, :LANES]
    second_out[...] = rim[:, LANES:]
    square = lane_sum(total * total * inverse[...])
    energy = lane_sum(flux_x * grad_x + flux_y * grad_y + weighted * total)
    column = lax.broadcasted_iota(jnp.int32, (ROWS, LANES), 1)
    sums[...] = jnp.where(column == 0, square, jnp.where(column == 1, energy, 0.0))


def image_kernel(
    mode, share, own, first_in, second_in, joins, nodal, inverse, derive, sums,
    image, image_x, image_y, spread,
):
    metric = nodal[...]
    total = joined(share, own, first_in, second_in, joins, metric[6:7])
    mass = metric[4:5]
    rate, even = rates(mode[0])
    shift = rate * rate + PENALTY
    grad_x, grad_y = gradient(total, metric, derive[...])
    image[...] = total
    image_x[...] = grad_x
    image_y[...] = grad_y
    square = lane_sum(total * total * inverse[...])
    energy = lane_sum(mass * (grad_x * grad_x + grad_y * grad_y + shift * (total * total)))
    column = lax.broadcasted_iota(jnp.int32, (ROWS, LANES), 1)
    table = jnp.where(column == 2, square, jnp.where(column == 3, energy, sums[...]))
    table = jnp.concatenate([table, jnp.zeros((LANES - ROWS, LANES), f32)], axis=0)
    turned = jnp.transpose(table)
    short = jnp.concatenate(
        [
            turned[0:1] + pltpu.roll(turned[1:2], ROWS, 1),
            turned[2:3] + pltpu.roll(turned[3:4], ROWS, 1),
        ],
        axis=1,
    )
    spread[...] = jnp.broadcast_to(short, spread.shape)


def finish_kernel(
    mode, gathered, star, right, right_x, right_y, image, image_x, image_y,
    velocity_out, pressure_out,
):
    sums = jnp.sum(gathered[...], axis=0, keepdims=True)
    first = sums[:, :LANES]
    second = sums[:, LANES:]
    g0 = first
    g1 = pltpu.roll(first, ROWS, 1)
    g2 = second
    g3 = pltpu.roll(second, ROWS, 1)
    step0 = g0 / g1
    new = step0 * step0 * g2 - g0
    ratio = new / g0
    curve = (1.0 + ratio) * ((1.0 + ratio) * g1 - 2.0 * step0 * g2) + step0 * step0 * g3
    step1 = new / curve
    by_right = step0 + step1 * (1.0 + ratio)
    by_image = -step1 * step0
    pair = jnp.concatenate([by_right, by_image, jnp.zeros((6, LANES), f32)], axis=0)
    turned = jnp.transpose(pair)
    by_right = turned[:ROWS, 0:1]
    by_image = turned[:ROWS, 1:2]
    pressure = by_right * right[...] + by_image * image[...]
    slopes = [
        by_right * right_x[...] + by_image * image_x[...],
        by_right * right_y[...] + by_image * image_y[...],
        along_z(pressure, mode[0]),
    ]
    outs = [star[ROWS * c : ROWS * (c + 1)] - TIME_STEP * slopes[c] for c in range(3)]
    for q in range(QUADS):
        here = slice(QUAD_NODES * q, QUAD_NODES * (q + 1))
        there = slice(LANES * q, LANES * q + QUAD_NODES)
        for c in range(3):
            velocity_out[c, :, here] = outs[c][:, there]
        pressure_out[:, here] = pressure[:, there]


VMEM = pl.BlockSpec(memory_space=pltpu.VMEM)
SMEM = pl.BlockSpec(memory_space=pltpu.SMEM)
ANY = pl.BlockSpec(memory_space=pl.ANY)


def call(kernel, ins, outs, scratch=(), flops=0, name=None, aliases={}):
    specs = [SMEM if a.dtype == jnp.int32 and a.shape == (1,) else VMEM for a in ins]
    specs = [ANY if i in aliases else spec for i, spec in enumerate(specs)]
    shapes = [jax.ShapeDtypeStruct(s, d) for s, d in outs]
    size = sum(math.prod(a.shape) * a.dtype.itemsize for a in list(ins) + shapes)
    return pl.pallas_call(
        kernel,
        in_specs=specs,
        out_specs=[ANY if i in aliases.values() else VMEM for i in range(len(shapes))],
        out_shape=shapes,
        scratch_shapes=list(scratch),
        input_output_aliases=aliases,
        name=name,
        cost_estimate=pl.CostEstimate(flops=flops, bytes_accessed=size, transcendentals=0),
        compiler_params=pltpu.CompilerParams(vmem_limit_bytes=40 * 1024 * 1024),
    )(*ins)


def on_device(velocity, metric, mass, local_ids, edge_ids):
    derive, derive_back = (jnp.asarray(t) for t in derivative_tables())
    fourier = jnp.asarray(fourier_tables())
    mode = lax.axis_index("mode").astype(jnp.int32).reshape(1)
    parity = (lax.axis_index("elem") % 2).astype(jnp.int32).reshape(1)
    count = lax.axis_size("elem")
    pairs = [[(i, (i + 1) % count) for i in range(start, count, 2)] for start in (1, 0)]
    pairs = [some + [(target, source) for source, target in some] for some in pairs]

    def swap(first, second):
        return lax.ppermute(first, "elem", pairs[0]), lax.ppermute(second, "elem", pairs[1])

    block = (QUADS, 2, ROWS, LANES)
    (packed,) = call(
        pack_kernel, [velocity], [(block, f32)],
        name="pack",
    )
    nodal = jnp.concatenate([metric, mass[None]], axis=0)
    tables = [fourier, derive]
    field, nodal, own_metric, joins, rims, fourier, derive = call(
        prepare_kernel,
        [mode, parity, velocity, nodal, local_ids[None], edge_ids[0]] + tables,
        [
            ((3 * ROWS, WIDE), f32),
            ((8, WIDE), f32),
            ((8, LANES), f32),
            ((2 * LANES, WIDE), bf16),
            ((WIDE, 2 * LANES), bf16),
        ]
        + [(t.shape, bf16) for t in tables],
        flops=1 << 24,
        name="prepare",
        aliases={6: 5, 7: 6},
    )
    arrived = lax.all_to_all(packed, "mode", 0, 0)
    (spectral,) = call(
        convect_kernel,
        [arrived, own_metric, fourier, derive],
        [(block, f32)],
        scratch=[pltpu.VMEM((HALF, 2 * PACK), f32)] * 2 + [pltpu.VMEM((HALF, PACK), f32)] * 2,
        flops=1 << 30,
        name="convect",
    )
    returned = lax.all_to_all(spectral, "mode", 0, 0)
    rim_out = [((STACK, LANES), f32)] * 2
    share, first_out, second_out = call(
        weigh_kernel, [returned, nodal, rims], [((STACK, WIDE), f32)] + rim_out,
        flops=1 << 28, name="weigh",
    )
    first_in, second_in = swap(first_out, second_out)
    one = ((ROWS, WIDE), f32)
    rim_out = [((ROWS, LANES), f32)] * 2
    star, inverse, share, first_out, second_out = call(
        star_kernel,
        [mode, share, first_out, first_in, second_in, joins, rims, field, nodal, derive],
        [((3 * ROWS, WIDE), f32), ((1, WIDE), f32), one] + rim_out,
        flops=1 << 29, name="star",
    )
    first_in, second_in = swap(first_out, second_out)
    right, right_x, right_y, share, first_out, second_out, sums = call(
        helmholtz_kernel,
        [mode, share, first_out, first_in, second_in, joins, rims, nodal, inverse, derive, derive_back],
        [one, one, one, one] + rim_out + [((ROWS, LANES), f32)],
        flops=1 << 29, name="helmholtz",
    )
    first_in, second_in = swap(first_out, second_out)
    image, image_x, image_y, spread = call(
        image_kernel,
        [mode, share, first_out, first_in, second_in, joins, nodal, inverse, derive, sums],
        [one, one, one, ((count, 1, 2 * LANES), f32)],
        flops=1 << 29, name="image",
    )
    gathered = lax.all_to_all(spread, "elem", 0, 0)
    gathered = gathered.reshape(count, 2 * LANES)
    velocity_new, pressure = call(
        finish_kernel,
        [mode, gathered, star, right, right_x, right_y, image, image_x, image_y],
        [((3, ROWS, QUADS * QUAD_NODES), f32), ((ROWS, QUADS * QUAD_NODES), f32)],
        name="finish",
    )
    return velocity_new, pressure


def solution(mesh):
    in_specs = (
        P(None, "mode", "elem"),
        P(None, "elem"),
        P("elem"),
        P("elem"),
        P("elem", None, None),
    )
    out_specs = (P(None, "mode", "elem"), P("mode", "elem"))
    return jax.shard_map(
        on_device, mesh=mesh, in_specs=in_specs, out_specs=out_specs, check_vma=False
    )
```

```python
import functools
import math

import jax
import jax.numpy as jnp
import numpy as np
from jax import lax
from jax.experimental import pallas as pl
from jax.experimental.pallas import tpu as pltpu
from jax.sharding import PartitionSpec as P

SIDE = 9
QUAD_NODES = 81
PLANES = 512
QUADS = 8
EDGE = 65
LANES = 128
WIDE = QUADS * LANES
PACK = 256
ROWS = 64
KEPT = 192
STACK = 200
CHUNK = 64
HALF = 256

PENALTY = 1.0
TIME_STEP = 0.01

f32 = jnp.float32
bf16 = jnp.bfloat16


def legendre_pair(points, degree):
    previous = points * 0.0 + 1.0
    current = points.copy()
    for order in range(2, degree + 1):
        following = ((2.0 * order - 1.0) * points * current - (order - 1.0) * previous) / order
        previous = current
        current = following
    return (previous, current)


def derivative_matrix():
    degree = SIDE - 1
    points = np.cos(math.pi * np.arange(degree + 1) / degree)
    for sweep in range(100):
        lower, upper = legendre_pair(points, degree)
        points = points - (points * upper - lower) / ((degree + 1.0) * upper)
    points = points[::-1].copy()
    values = legendre_pair(points, degree)[1]
    identity = np.eye(SIDE)
    differ = points[:, None] - points[None, :] + identity
    matrix = np.where(identity > 0.5, 0.0, values[:, None] / (values[None, :] * differ))
    matrix[0, 0] = -degree * (degree + 1) / 4.0
    matrix[degree, degree] = degree * (degree + 1) / 4.0
    return matrix


def halves(table):
    high = table.astype(np.float32).astype(jnp.bfloat16)
    low = (table - high.astype(np.float64)).astype(np.float32).astype(jnp.bfloat16)
    return high, low


def as_right(table):
    high, low = halves(table)
    return np.concatenate([high, high, low], axis=0)


def as_left(table):
    high, low = halves(table)
    return np.concatenate([high, high, low], axis=1)


def derivative_tables():
    matrix = derivative_matrix()
    table = np.zeros((LANES, 2 * LANES))
    table[:QUAD_NODES, :QUAD_NODES] = np.kron(matrix, np.eye(SIDE)).T
    table[:QUAD_NODES, LANES : LANES + QUAD_NODES] = np.kron(np.eye(SIDE), matrix).T
    table = table.astype(np.float32).astype(np.float64)
    return as_right(table), as_right(table.T.copy())


def fourier_tables():
    index = np.arange(HALF)
    angles = 2.0 * math.pi / PLANES * (index[:, None] * index[None, :] % PLANES)
    return np.stack([as_left(np.cos(angles)), as_left(np.sin(angles))])


def split2(x):
    high = x.astype(bf16)
    return high, (x - high.astype(f32)).astype(bf16)


def split3(x):
    high = x.astype(bf16)
    rest = x - high.astype(f32)
    middle = rest.astype(bf16)
    return high, middle, (rest - middle.astype(f32)).astype(bf16)


def mm(a, b):
    return jnp.dot(a, b, preferred_element_type=f32)


def times_table(x, table):
    high, low = split2(x)
    return mm(jnp.concatenate([high, low, high], axis=1), table)


def table_times(table, x):
    high, low = split2(x)
    return mm(table, jnp.concatenate([high, low, high], axis=0))


def times_incidence(x, incidence):
    rows = x.shape[0]
    out = mm(jnp.concatenate(split3(x), axis=0), incidence)
    return out[:rows] + (out[rows : 2 * rows] + out[2 * rows :])


def stacked(x):
    return jnp.concatenate([x[:, LANES * q : LANES * (q + 1)] for q in range(QUADS)], axis=0)


def unstacked(x):
    rows = x.shape[0] // QUADS
    return jnp.concatenate([x[rows * q : rows * (q + 1)] for q in range(QUADS)], axis=1)


def gradient(x, metric, table):
    derived = times_table(stacked(x), table)
    along_r = unstacked(derived[:, :LANES])
    along_s = unstacked(derived[:, LANES:])
    return (
        metric[0:1] * along_r + metric[2:3] * along_s,
        metric[1:2] * along_r + metric[3:4] * along_s,
    )


def rates(mode):
    row = lax.broadcasted_iota(jnp.int32, (ROWS, 1), 0)
    return (8.0 / PLANES) * ((mode * ROWS + row) // 2).astype(f32), row % 2 == 0


def along_z(x, mode):
    rate, even = rates(mode)
    return rate * jnp.where(even, pltpu.roll(x, ROWS - 1, 0), -pltpu.roll(x, 1, 0))


def unpacked(x, field):
    if field:
        x = pltpu.roll(x, PACK - QUAD_NODES * field, 1)
    return x[:, :LANES]


def pack_kernel(velocity, packed):
    for q in range(QUADS):
        for c in range(3):
            start, stop = QUAD_NODES * c, QUAD_NODES * (c + 1)
            for tile in range(start // LANES, (stop - 1) // LANES + 1):
                low, high = max(start, LANES * tile), min(stop, LANES * (tile + 1))
                node = QUAD_NODES * q - start
                packed[q, tile, :, low - LANES * tile : high - LANES * tile] = velocity[
                    c, :, node + low : node + high
                ]
        packed[q, 1, :, 3 * QUAD_NODES - LANES :] = jnp.zeros((ROWS, PACK - 3 * QUAD_NODES), f32)


def matches(column, row):
    return jnp.where(column == row, 1.0, 0.0)


def prepare_kernel(
    mode, parity, velocity, nodal, ids, edges, fourier, derive,
    field, nodal_wide, own_metric, joins, rims, fourier_on, derive_on,
):
    lane = lax.broadcasted_iota(jnp.int32, (1, LANES), 1)
    inside = lane < QUAD_NODES
    field[...] = jnp.zeros_like(field)
    nodal_wide[...] = jnp.zeros_like(nodal_wide)
    for q in range(QUADS):
        here = slice(LANES * q, LANES * q + QUAD_NODES)
        there = slice(QUAD_NODES * q, QUAD_NODES * (q + 1))
        for c in range(3):
            field[ROWS * c : ROWS * (c + 1), here] = velocity[c, :, there]
        nodal_wide[0:5, here] = nodal[0:5, there]
        nodal_wide[5:6, here] = jnp.ones((1, QUAD_NODES), f32)
    own = jnp.zeros((8, LANES), f32)
    for q in range(QUADS):
        own = own + jnp.where(mode[0] == q, nodal_wide[:, LANES * q : LANES * (q + 1)], 0.0)
    own_metric[...] = own
    ids_row = [
        jnp.concatenate(
            [
                ids[:, QUAD_NODES * q : QUAD_NODES * (q + 1)],
                jnp.full((1, LANES - QUAD_NODES), -1, jnp.int32),
            ],
            axis=1,
        ).astype(f32)
        for q in range(QUADS)
    ]
    ids_wide = jnp.concatenate(ids_row, axis=1)
    odd = parity[0] > 0
    edge_row = [
        jnp.concatenate(
            [
                jnp.where(odd, edges[1 - s : 2 - s, :], edges[s : s + 1, :]),
                jnp.full((1, LANES - EDGE), -2, jnp.int32),
            ],
            axis=1,
        ).astype(f32)
        for s in range(2)
    ]
    columns = jnp.transpose(jnp.concatenate(ids_row, axis=0))
    column = [columns[:, q : q + 1] for q in range(QUADS)]
    row_at = lax.broadcasted_iota(jnp.int32, (LANES, LANES), 0)
    lane_at = lax.broadcasted_iota(jnp.int32, (LANES, LANES), 1)
    opens = []
    for q in range(QUADS):
        total = jnp.zeros((LANES, LANES), f32)
        before = jnp.zeros((LANES, LANES), f32)
        for p in range(QUADS):
            same = matches(column[p], ids_row[q])
            total = total + same
            if p < q:
                before = before + same
            if p == q:
                before = before + jnp.where(row_at < lane_at, same, 0.0)
        copies = jnp.sum(total, axis=0, keepdims=True)
        earlier = jnp.sum(before, axis=0, keepdims=True)
        shared = jnp.where(inside & (copies > 1.5), 1.0, 0.0)
        opens.append(jnp.where(earlier < 0.5, shared, 0.0))
        nodal_wide[6:7, LANES * q : LANES * (q + 1)] = jnp.where(inside, 1.0 - shared, 0.0)
    opens = jnp.concatenate(opens, axis=0)
    triangle = jnp.where(row_at < lane_at, 1.0, 0.0).astype(bf16)
    rank = mm(opens.astype(bf16), triangle)
    counts = jnp.sum(opens, axis=1, keepdims=True)
    offset = jnp.zeros((1, 1), f32)
    offsets = []
    for q in range(QUADS):
        offsets.append(offset)
        offset = offset + counts[q : q + 1]
    slot = jnp.where(opens > 0.5, rank + jnp.concatenate(offsets, axis=0) + float(EDGE), -1.0)
    slots = jnp.transpose(slot)
    lanes = lane.astype(f32)
    hits = jnp.zeros((LANES, LANES), f32)
    named = jnp.zeros((LANES, LANES), f32)
    for q in range(QUADS):
        hit = matches(slots[:, q : q + 1], lanes)
        hits = hits + hit
        named = named + hit * column[q]
    hits = jnp.sum(hits, axis=0, keepdims=True)
    named = jnp.sum(named, axis=0, keepdims=True)
    first = jnp.where(lane < EDGE, edge_row[0], jnp.where(hits > 0.5, named, -3.0))
    keys = [first, edge_row[1]]
    key_columns = jnp.transpose(jnp.concatenate(keys + [first] * 6, axis=0))
    for q in range(QUADS):
        for s in range(2):
            rims[LANES * q : LANES * (q + 1), LANES * s : LANES * (s + 1)] = matches(
                column[q], keys[s]
            ).astype(bf16)
    for s in range(2):
        joins[LANES * s : LANES * (s + 1), :] = matches(
            key_columns[:, s : s + 1], ids_wide
        ).astype(bf16)


def convect_kernel(packed, own_metric, fourier, derive, out, even, odd, sums, differences):
    metric = own_metric[...]
    lane = lax.broadcasted_iota(jnp.int32, (1, LANES), 1)
    inside = lane < QUAD_NODES
    table = derive[...]
    index = lax.broadcasted_iota(jnp.int32, (HALF, 1), 0)
    rate = (8.0 / PLANES) * index.astype(f32)
    sign = jnp.where(index % 2 == 0, 1.0, -1.0)
    cosines, sines = (
        jnp.concatenate(
            [
                jnp.concatenate(
                    [packed[m, tile, pl.ds(parity, ROWS // 2, stride=2), :] for tile in range(2)],
                    axis=1,
                )
                for m in range(QUADS)
            ],
            axis=0,
        )
        for parity in range(2)
    )
    highest = sines[0:1]
    to_even = jnp.concatenate([cosines, rate * sines], axis=1)
    to_odd = jnp.concatenate([sines, -rate * cosines], axis=1)
    even[...] = table_times(fourier[0], to_even)
    even[:, :PACK] = even[:, :PACK] + sign * highest
    middle = jnp.sum(sign * to_even, axis=0, keepdims=True)
    middle = middle + jnp.concatenate([highest, jnp.zeros_like(highest)], axis=1)
    odd[...] = table_times(fourier[1], to_odd)
    opening = lax.broadcasted_iota(jnp.int32, (CHUNK, 1), 0) == 0
    product_middle = None
    for i in range(HALF // CHUNK):
        rows = slice(CHUNK * i, CHUNK * (i + 1))
        part_even = even[rows]
        part_odd = odd[rows]
        ahead = part_even + part_odd
        if i == 0:
            part_even = jnp.where(opening, middle, part_even)
        wide = jnp.concatenate([ahead, part_even - part_odd], axis=0)
        value = wide[:, :PACK]
        slope = wide[:, PACK:]
        speed = [unpacked(value, c) for c in range(3)]
        derived = times_table(jnp.concatenate(speed, axis=0), table)
        weight_r = speed[0] * metric[0:1] + speed[1] * metric[1:2]
        weight_s = speed[0] * metric[2:3] + speed[1] * metric[3:4]
        total = None
        for c in range(3):
            part = derived[2 * CHUNK * c : 2 * CHUNK * (c + 1)]
            term = (
                weight_r * part[:, :LANES]
                + weight_s * part[:, LANES:]
                + speed[2] * unpacked(slope, c)
            )
            term = jnp.where(inside, -term, 0.0)
            term = jnp.concatenate([term, jnp.zeros((2 * CHUNK, PACK - LANES), f32)], axis=1)
            if c:
                term = pltpu.roll(term, QUAD_NODES * c, 1)
            total = term if total is None else total + term
        ahead = total[:CHUNK]
        mirror = total[CHUNK:]
        differences[rows, :] = ahead - mirror
        if i == 0:
            product_middle = mirror[0:1]
            mirror = jnp.where(opening, 0.0, mirror)
        sums[rows, :] = ahead + mirror
    index = index[:KEPT]
    weight = jnp.where(index <= PLANES // 3, 2.0 / PLANES, 0.0)
    result = table_times(fourier[0, :KEPT], sums[...]) + sign[:KEPT] * product_middle
    results = [jnp.where(index == 0, 0.5 * weight, weight) * result]
    result = table_times(fourier[1, :KEPT], differences[...])
    results.append(jnp.where(index == 0, 0.0, weight) * result)
    half = ROWS // 2
    for m in range(KEPT // half):
        for tile in range(2):
            for parity in range(2):
                out[m, tile, pl.ds(parity, half, stride=2), :] = results[parity][
                    half * m : half * (m + 1), LANES * tile : LANES * (tile + 1)
                ]
    out[KEPT // half :] = jnp.zeros((QUADS - KEPT // half, 2, ROWS, LANES), f32)


def weigh_kernel(spectral, nodal, rims, share, first_out, second_out):
    for q in range(QUADS):
        here = slice(LANES * q, LANES * (q + 1))
        mass = nodal[4:5, here]
        block = jnp.concatenate([spectral[q, 0], spectral[q, 1]], axis=1)
        for c in range(3):
            share[ROWS * c : ROWS * (c + 1), here] = mass * jnp.where(
                mass > 0.0, unpacked(block, c), 0.0
            )
    share[3 * ROWS : 3 * ROWS + 1, :] = nodal[4:5, :]
    share[3 * ROWS + 1 : 3 * ROWS + 2, :] = nodal[5:6, :]
    share[3 * ROWS + 2 :, :] = jnp.zeros((STACK - 3 * ROWS - 2, WIDE), f32)
    rim = times_incidence(share[...], rims[...])
    first_out[...] = rim[:, :LANES]
    second_out[...] = rim[:, LANES:]


def joined(parity, share, own, first_in, second_in, joins, single):
    lane = lax.broadcasted_iota(jnp.int32, (1, LANES), 1)
    near = jnp.where(lane < EDGE, first_in[...], own[...])
    other = jnp.where(parity[0] > 0, second_in[0], second_in[1])
    sums = jnp.concatenate([near, other], axis=1)
    return share[...] * single + times_incidence(sums, joins[...])


def star_kernel(
    mode, parity, share, own, first_in, second_in, joins, rims, field, nodal, derive,
    star, inverse, share_out, first_out, second_out,
):
    metric = nodal[...]
    total = joined(parity, share, own, first_in, second_in, joins, metric[6:7])
    inside = metric[5:6] > 0.0
    scale = TIME_STEP / jnp.where(inside, total[3 * ROWS : 3 * ROWS + 1], 1.0)
    inverse[...] = jnp.where(
        inside, 1.0 / jnp.where(inside, total[3 * ROWS + 1 : 3 * ROWS + 2], 1.0), 0.0
    )
    star[...] = field[...] + scale * total[: 3 * ROWS]
    table = derive[...]
    star_x = gradient(star[0:ROWS], metric, table)[0]
    star_y = gradient(star[ROWS : 2 * ROWS], metric, table)[1]
    divergence = star_x + star_y + along_z(star[2 * ROWS :], mode[0])
    result = (-1.0 / TIME_STEP) * (metric[4:5] * divergence)
    share_out[...] = result
    rim = times_incidence(result, rims[...])
    first_out[...] = rim[:, :LANES]
    second_out[...] = rim[:, LANES:]


def lane_sum(x):
    total = x[:, :LANES]
    for q in range(1, QUADS):
        total = total + x[:, LANES * q : LANES * (q + 1)]
    return jnp.sum(total, axis=1, keepdims=True)


def helmholtz_kernel(
    mode, parity, share, own, first_in, second_in, joins, rims, nodal, inverse, derive, derive_back,
    right, right_x, right_y, share_out, first_out, second_out, sums,
):
    metric = nodal[...]
    total = joined(parity, share, own, first_in, second_in, joins, metric[6:7])
    mass = metric[4:5]
    rate, even = rates(mode[0])
    shift = rate * rate + PENALTY
    grad_x, grad_y = gradient(total, metric, derive[...])
    right[...] = total
    right_x[...] = grad_x
    right_y[...] = grad_y
    flux_x = mass * grad_x
    flux_y = mass * grad_y
    weighted = shift * (mass * total)
    part_r = metric[0:1] * flux_x + metric[1:2] * flux_y
    part_s = metric[2:3] * flux_x + metric[3:4] * flux_y
    both = jnp.concatenate([stacked(part_r), stacked(part_s)], axis=1)
    result = unstacked(times_table(both, derive_back[...])) + weighted
    share_out[...] = result
    rim = times_incidence(result, rims[...])
    first_out[...] = rim[:, :LANES]
    second_out[...] = rim[:, LANES:]
    square = lane_sum(total * total * inverse[...])
    energy = lane_sum(flux_x * grad_x + flux_y * grad_y + weighted * total)
    column = lax.broadcasted_iota(jnp.int32, (ROWS, LANES), 1)
    sums[...] = jnp.where(column == 0, square, jnp.where(column == 1, energy, 0.0))


def image_kernel(
    mode, parity, share, own, first_in, second_in, joins, nodal, inverse, derive, sums,
    image, image_x, image_y, spread,
):
    metric = nodal[...]
    total = joined(parity, share, own, first_in, second_in, joins, metric[6:7])
    mass = metric[4:5]
    rate, even = rates(mode[0])
    shift = rate * rate + PENALTY
    grad_x, grad_y = gradient(total, metric, derive[...])
    image[...] = total
    image_x[...] = grad_x
    image_y[...] = grad_y
    square = lane_sum(total * total * inverse[...])
    energy = lane_sum(mass * (grad_x * grad_x + grad_y * grad_y + shift * (total * total)))
    column = lax.broadcasted_iota(jnp.int32, (ROWS, LANES), 1)
    table = jnp.where(column == 2, square, jnp.where(column == 3, energy, sums[...]))
    table = jnp.concatenate([table, jnp.zeros((LANES - ROWS, LANES), f32)], axis=0)
    turned = jnp.transpose(table)
    short = jnp.concatenate(
        [
            turned[0:1] + pltpu.roll(turned[1:2], ROWS, 1),
            turned[2:3] + pltpu.roll(turned[3:4], ROWS, 1),
        ],
        axis=1,
    )
    spread[...] = jnp.broadcast_to(short, spread.shape)


def finish_kernel(
    mode, gathered, star, right, right_x, right_y, image, image_x, image_y,
    velocity_out, pressure_out,
):
    sums = jnp.sum(gathered[...], axis=0, keepdims=True)
    first = sums[:, :LANES]
    second = sums[:, LANES:]
    g0 = first
    g1 = pltpu.roll(first, ROWS, 1)
    g2 = second
    g3 = pltpu.roll(second, ROWS, 1)
    step0 = g0 / g1
    new = step0 * step0 * g2 - g0
    ratio = new / g0
    curve = (1.0 + ratio) * ((1.0 + ratio) * g1 - 2.0 * step0 * g2) + step0 * step0 * g3
    step1 = new / curve
    by_right = step0 + step1 * (1.0 + ratio)
    by_image = -step1 * step0
    pair = jnp.concatenate([by_right, by_image, jnp.zeros((6, LANES), f32)], axis=0)
    turned = jnp.transpose(pair)
    by_right = turned[:ROWS, 0:1]
    by_image = turned[:ROWS, 1:2]
    pressure = by_right * right[...] + by_image * image[...]
    slopes = [
        by_right * right_x[...] + by_image * image_x[...],
        by_right * right_y[...] + by_image * image_y[...],
        along_z(pressure, mode[0]),
    ]
    outs = [star[ROWS * c : ROWS * (c + 1)] - TIME_STEP * slopes[c] for c in range(3)]
    for q in range(QUADS):
        here = slice(QUAD_NODES * q, QUAD_NODES * (q + 1))
        there = slice(LANES * q, LANES * q + QUAD_NODES)
        for c in range(3):
            velocity_out[c, :, here] = outs[c][:, there]
        pressure_out[:, here] = pressure[:, there]


VMEM = pl.BlockSpec(memory_space=pltpu.VMEM)
SMEM = pl.BlockSpec(memory_space=pltpu.SMEM)
ANY = pl.BlockSpec(memory_space=pl.ANY)


def call(kernel, ins, outs, scratch=(), flops=0, name=None, aliases={}):
    specs = [SMEM if a.dtype == jnp.int32 and a.shape == (1,) else VMEM for a in ins]
    specs = [ANY if i in aliases else spec for i, spec in enumerate(specs)]
    shapes = [jax.ShapeDtypeStruct(s, d) for s, d in outs]
    size = sum(math.prod(a.shape) * a.dtype.itemsize for a in list(ins) + shapes)
    return pl.pallas_call(
        kernel,
        in_specs=specs,
        out_specs=[ANY if i in aliases.values() else VMEM for i in range(len(shapes))],
        out_shape=shapes,
        scratch_shapes=list(scratch),
        input_output_aliases=aliases,
        name=name,
        cost_estimate=pl.CostEstimate(flops=flops, bytes_accessed=size, transcendentals=0),
        compiler_params=pltpu.CompilerParams(vmem_limit_bytes=40 * 1024 * 1024),
    )(*ins)


def on_device(velocity, metric, mass, local_ids, edge_ids):
    derive, derive_back = (jnp.asarray(t) for t in derivative_tables())
    fourier = jnp.asarray(fourier_tables())
    mode = lax.axis_index("mode").astype(jnp.int32).reshape(1)
    parity = (lax.axis_index("elem") % 2).astype(jnp.int32).reshape(1)
    count = lax.axis_size("elem")
    across = [(i, (i + 1) % count) for i in range(1, count, 2)]
    across = across + [(target, source) for source, target in across]
    beside = [[i, i + 1] for i in range(0, count, 2)]

    def swap(first, second):
        return (
            lax.ppermute(first, "elem", across),
            lax.all_gather(second, "elem", axis_index_groups=beside),
        )

    block = (QUADS, 2, ROWS, LANES)
    (packed,) = call(
        pack_kernel, [velocity], [(block, f32)],
        name="pack",
    )
    nodal = jnp.concatenate([metric, mass[None]], axis=0)
    tables = [fourier, derive]
    field, nodal, own_metric, joins, rims, fourier, derive = call(
        prepare_kernel,
        [mode, parity, velocity, nodal, local_ids[None], edge_ids[0]] + tables,
        [
            ((3 * ROWS, WIDE), f32),
            ((8, WIDE), f32),
            ((8, LANES), f32),
            ((2 * LANES, WIDE), bf16),
            ((WIDE, 2 * LANES), bf16),
        ]
        + [(t.shape, bf16) for t in tables],
        flops=1 << 24,
        name="prepare",
        aliases={6: 5, 7: 6},
    )
    arrived = lax.all_to_all(packed, "mode", 0, 0)
    (spectral,) = call(
        convect_kernel,
        [arrived, own_metric, fourier, derive],
        [(block, f32)],
        scratch=[pltpu.VMEM((HALF, 2 * PACK), f32)] * 2 + [pltpu.VMEM((HALF, PACK), f32)] * 2,
        flops=1 << 30,
        name="convect",
    )
    returned = lax.all_to_all(spectral, "mode", 0, 0)
    rim_out = [((STACK, LANES), f32)] * 2
    share, first_out, second_out = call(
        weigh_kernel, [returned, nodal, rims], [((STACK, WIDE), f32)] + rim_out,
        flops=1 << 28, name="weigh",
    )
    first_in, second_in = swap(first_out, second_out)
    one = ((ROWS, WIDE), f32)
    rim_out = [((ROWS, LANES), f32)] * 2
    star, inverse, share, first_out, second_out = call(
        star_kernel,
        [mode, parity, share, first_out, first_in, second_in, joins, rims, field, nodal, derive],
        [((3 * ROWS, WIDE), f32), ((1, WIDE), f32), one] + rim_out,
        flops=1 << 29, name="star",
    )
    first_in, second_in = swap(first_out, second_out)
    right, right_x, right_y, share, first_out, second_out, sums = call(
        helmholtz_kernel,
        [mode, parity, share, first_out, first_in, second_in, joins, rims, nodal, inverse, derive, derive_back],
        [one, one, one, one] + rim_out + [((ROWS, LANES), f32)],
        flops=1 << 29, name="helmholtz",
    )
    first_in, second_in = swap(first_out, second_out)
    image, image_x, image_y, spread = call(
        image_kernel,
        [mode, parity, share, first_out, first_in, second_in, joins, nodal, inverse, derive, sums],
        [one, one, one, ((count, 1, 2 * LANES), f32)],
        flops=1 << 29, name="image",
    )
    gathered = lax.all_to_all(spread, "elem", 0, 0)
    gathered = gathered.reshape(count, 2 * LANES)
    velocity_new, pressure = call(
        finish_kernel,
        [mode, gathered, star, right, right_x, right_y, image, image_x, image_y],
        [((3, ROWS, QUADS * QUAD_NODES), f32), ((ROWS, QUADS * QUAD_NODES), f32)],
        name="finish",
    )
    return velocity_new, pressure


def solution(mesh):
    in_specs = (
        P(None, "mode", "elem"),
        P(None, "elem"),
        P("elem"),
        P("elem"),
        P("elem", None, None),
    )
    out_specs = (P(None, "mode", "elem"), P("mode", "elem"))
    return jax.shard_map(
        on_device, mesh=mesh, in_specs=in_specs, out_specs=out_specs, check_vma=False
    )
```

```python
import functools
import math

import jax
import jax.numpy as jnp
import numpy as np
from jax import lax
from jax.experimental import pallas as pl
from jax.experimental.pallas import tpu as pltpu
from jax.sharding import PartitionSpec as P

SIDE = 9
QUAD_NODES = 81
PLANES = 512
QUADS = 8
EDGE = 65
LANES = 128
WIDE = QUADS * LANES
PACK = 256
ROWS = 64
KEPT = 192
STACK = 200
CHUNK = 64
HALF = 256

PENALTY = 1.0
TIME_STEP = 0.01

f32 = jnp.float32
bf16 = jnp.bfloat16


def legendre_pair(points, degree):
    previous = points * 0.0 + 1.0
    current = points.copy()
    for order in range(2, degree + 1):
        following = ((2.0 * order - 1.0) * points * current - (order - 1.0) * previous) / order
        previous = current
        current = following
    return (previous, current)


def derivative_matrix():
    degree = SIDE - 1
    points = np.cos(math.pi * np.arange(degree + 1) / degree)
    for sweep in range(100):
        lower, upper = legendre_pair(points, degree)
        points = points - (points * upper - lower) / ((degree + 1.0) * upper)
    points = points[::-1].copy()
    values = legendre_pair(points, degree)[1]
    identity = np.eye(SIDE)
    differ = points[:, None] - points[None, :] + identity
    matrix = np.where(identity > 0.5, 0.0, values[:, None] / (values[None, :] * differ))
    matrix[0, 0] = -degree * (degree + 1) / 4.0
    matrix[degree, degree] = degree * (degree + 1) / 4.0
    return matrix


def halves(table):
    high = table.astype(np.float32).astype(jnp.bfloat16)
    low = (table - high.astype(np.float64)).astype(np.float32).astype(jnp.bfloat16)
    return high, low


def as_right(table):
    high, low = halves(table)
    return np.concatenate([high, high, low], axis=0)


def as_left(table):
    high, low = halves(table)
    return np.concatenate([high, high, low], axis=1)


def derivative_tables():
    matrix = derivative_matrix()
    table = np.zeros((LANES, 2 * LANES))
    table[:QUAD_NODES, :QUAD_NODES] = np.kron(matrix, np.eye(SIDE)).T
    table[:QUAD_NODES, LANES : LANES + QUAD_NODES] = np.kron(np.eye(SIDE), matrix).T
    table = table.astype(np.float32).astype(np.float64)
    return as_right(table), as_right(table.T.copy())


def fourier_tables():
    index = np.arange(HALF)
    angles = 2.0 * math.pi / PLANES * (index[:, None] * index[None, :] % PLANES)
    return np.stack([as_left(np.cos(angles)), as_left(np.sin(angles))])


def split2(x):
    high = x.astype(bf16)
    return high, (x - high.astype(f32)).astype(bf16)


def mm(a, b):
    return jnp.dot(a, b, preferred_element_type=f32)


def times_table(x, table):
    high, low = split2(x)
    return mm(jnp.concatenate([high, low, high], axis=1), table)


def table_times(table, x):
    high, low = split2(x)
    return mm(table, jnp.concatenate([high, low, high], axis=0))


def times_incidence(x, incidence):
    rows = x.shape[0]
    out = mm(jnp.concatenate(split2(x), axis=0), incidence)
    return out[:rows] + out[rows:]


def stacked(x):
    return jnp.concatenate([x[:, LANES * q : LANES * (q + 1)] for q in range(QUADS)], axis=0)


def unstacked(x):
    rows = x.shape[0] // QUADS
    return jnp.concatenate([x[rows * q : rows * (q + 1)] for q in range(QUADS)], axis=1)


def gradient(x, metric, table):
    derived = times_table(stacked(x), table)
    along_r = unstacked(derived[:, :LANES])
    along_s = unstacked(derived[:, LANES:])
    return (
        metric[0:1] * along_r + metric[2:3] * along_s,
        metric[1:2] * along_r + metric[3:4] * along_s,
    )


def rates(mode):
    row = lax.broadcasted_iota(jnp.int32, (ROWS, 1), 0)
    return (8.0 / PLANES) * ((mode * ROWS + row) // 2).astype(f32), row % 2 == 0


def along_z(x, mode):
    rate, even = rates(mode)
    return rate * jnp.where(even, pltpu.roll(x, ROWS - 1, 0), -pltpu.roll(x, 1, 0))


def lanes_at():
    return lax.broadcasted_iota(jnp.int32, (1, LANES), 1)


def unpacked(x, field):
    first, second = x[:, :LANES], x[:, LANES:]
    if field == 0:
        return first
    if field == 1:
        both = jnp.where(lanes_at() < QUAD_NODES, second, first)
        return pltpu.roll(both, LANES - QUAD_NODES, 1)
    return pltpu.roll(second, 2 * (LANES - QUAD_NODES), 1)


def repacked(fields):
    lane = lanes_at()
    second_at = 2 * QUAD_NODES - LANES
    middle = pltpu.roll(fields[1], QUAD_NODES, 1)
    last = jnp.where(lane < second_at + QUAD_NODES, pltpu.roll(fields[2], second_at, 1), 0.0)
    return jnp.concatenate(
        [jnp.where(lane < QUAD_NODES, fields[0], middle), jnp.where(lane < second_at, middle, last)],
        axis=1,
    )


def pack_kernel(velocity, packed):
    for q in range(QUADS):
        for c in range(3):
            start, stop = QUAD_NODES * c, QUAD_NODES * (c + 1)
            for tile in range(start // LANES, (stop - 1) // LANES + 1):
                low, high = max(start, LANES * tile), min(stop, LANES * (tile + 1))
                node = QUAD_NODES * q - start
                packed[q, tile, :, low - LANES * tile : high - LANES * tile] = velocity[
                    c, :, node + low : node + high
                ]
        packed[q, 1, :, 3 * QUAD_NODES - LANES :] = jnp.zeros((ROWS, PACK - 3 * QUAD_NODES), f32)


def matches(column, row):
    return jnp.where(column == row, 1.0, 0.0)


def prepare_kernel(
    mode, parity, velocity, nodal, ids, edges, fourier, derive,
    field, nodal_wide, own_metric, joins, rims, fourier_on, derive_on,
):
    lane = lax.broadcasted_iota(jnp.int32, (1, LANES), 1)
    inside = lane < QUAD_NODES
    field[...] = jnp.zeros_like(field)
    nodal_wide[...] = jnp.zeros_like(nodal_wide)
    for q in range(QUADS):
        here = slice(LANES * q, LANES * q + QUAD_NODES)
        there = slice(QUAD_NODES * q, QUAD_NODES * (q + 1))
        for c in range(3):
            field[ROWS * c : ROWS * (c + 1), here] = velocity[c, :, there]
        nodal_wide[0:5, here] = nodal[0:5, there]
        nodal_wide[5:6, here] = jnp.ones((1, QUAD_NODES), f32)
    own = jnp.zeros((8, LANES), f32)
    for q in range(QUADS):
        own = own + jnp.where(mode[0] == q, nodal_wide[:, LANES * q : LANES * (q + 1)], 0.0)
    own_metric[...] = own
    ids_row = [
        jnp.concatenate(
            [
                ids[:, QUAD_NODES * q : QUAD_NODES * (q + 1)],
                jnp.full((1, LANES - QUAD_NODES), -1, jnp.int32),
            ],
            axis=1,
        ).astype(f32)
        for q in range(QUADS)
    ]
    ids_wide = jnp.concatenate(ids_row, axis=1)
    odd = parity[0] > 0
    edge_row = [
        jnp.concatenate(
            [
                jnp.where(odd, edges[1 - s : 2 - s, :], edges[s : s + 1, :]),
                jnp.full((1, LANES - EDGE), -2, jnp.int32),
            ],
            axis=1,
        ).astype(f32)
        for s in range(2)
    ]
    columns = jnp.transpose(jnp.concatenate(ids_row, axis=0))
    column = [columns[:, q : q + 1] for q in range(QUADS)]
    row_at = lax.broadcasted_iota(jnp.int32, (LANES, LANES), 0)
    lane_at = lax.broadcasted_iota(jnp.int32, (LANES, LANES), 1)
    opens = []
    for q in range(QUADS):
        total = jnp.zeros((LANES, LANES), f32)
        before = jnp.zeros((LANES, LANES), f32)
        for p in range(QUADS):
            same = matches(column[p], ids_row[q])
            total = total + same
            if p < q:
                before = before + same
            if p == q:
                before = before + jnp.where(row_at < lane_at, same, 0.0)
        copies = jnp.sum(total, axis=0, keepdims=True)
        earlier = jnp.sum(before, axis=0, keepdims=True)
        shared = jnp.where(inside & (copies > 1.5), 1.0, 0.0)
        opens.append(jnp.where(earlier < 0.5, shared, 0.0))
        nodal_wide[6:7, LANES * q : LANES * (q + 1)] = jnp.where(inside, 1.0 - shared, 0.0)
    opens = jnp.concatenate(opens, axis=0)
    triangle = jnp.where(row_at < lane_at, 1.0, 0.0).astype(bf16)
    rank = mm(opens.astype(bf16), triangle)
    counts = jnp.sum(opens, axis=1, keepdims=True)
    offset = jnp.zeros((1, 1), f32)
    offsets = []
    for q in range(QUADS):
        offsets.append(offset)
        offset = offset + counts[q : q + 1]
    slot = jnp.where(opens > 0.5, rank + jnp.concatenate(offsets, axis=0) + float(EDGE), -1.0)
    slots = jnp.transpose(slot)
    lanes = lane.astype(f32)
    hits = jnp.zeros((LANES, LANES), f32)
    named = jnp.zeros((LANES, LANES), f32)
    for q in range(QUADS):
        hit = matches(slots[:, q : q + 1], lanes)
        hits = hits + hit
        named = named + hit * column[q]
    hits = jnp.sum(hits, axis=0, keepdims=True)
    named = jnp.sum(named, axis=0, keepdims=True)
    first = jnp.where(lane < EDGE, edge_row[0], jnp.where(hits > 0.5, named, -3.0))
    keys = [first, edge_row[1]]
    key_columns = jnp.transpose(jnp.concatenate(keys + [first] * 6, axis=0))
    for q in range(QUADS):
        for s in range(2):
            rims[LANES * q : LANES * (q + 1), LANES * s : LANES * (s + 1)] = matches(
                column[q], keys[s]
            ).astype(bf16)
    for s in range(2):
        joins[LANES * s : LANES * (s + 1), :] = matches(
            key_columns[:, s : s + 1], ids_wide
        ).astype(bf16)


def convect_kernel(packed, own_metric, fourier, derive, out, even, odd, sums, differences):
    metric = own_metric[...]
    table = derive[...]
    index = lax.broadcasted_iota(jnp.int32, (HALF, 1), 0)
    rate = (8.0 / PLANES) * index.astype(f32)
    sign = jnp.where(index % 2 == 0, 1.0, -1.0)
    cosines, sines = (
        jnp.concatenate(
            [
                jnp.concatenate(
                    [packed[m, tile, pl.ds(parity, ROWS // 2, stride=2), :] for tile in range(2)],
                    axis=1,
                )
                for m in range(QUADS)
            ],
            axis=0,
        )
        for parity in range(2)
    )
    highest = sines[0:1]
    to_even = jnp.concatenate([cosines, rate * sines], axis=1)
    to_odd = jnp.concatenate([sines, -rate * cosines], axis=1)
    even[...] = table_times(fourier[0], to_even)
    even[:, :PACK] = even[:, :PACK] + sign * highest
    middle = jnp.sum(sign * to_even, axis=0, keepdims=True)
    middle = middle + jnp.concatenate([highest, jnp.zeros_like(highest)], axis=1)
    odd[...] = table_times(fourier[1], to_odd)
    opening = lax.broadcasted_iota(jnp.int32, (CHUNK, 1), 0) == 0
    product_middle = None
    for i in range(HALF // CHUNK):
        rows = slice(CHUNK * i, CHUNK * (i + 1))
        part_even = even[rows]
        part_odd = odd[rows]
        ahead = part_even + part_odd
        if i == 0:
            part_even = jnp.where(opening, middle, part_even)
        wide = jnp.concatenate([ahead, part_even - part_odd], axis=0)
        value = wide[:, :PACK]
        slope = wide[:, PACK:]
        speed = [unpacked(value, c) for c in range(3)]
        derived = times_table(jnp.concatenate(speed, axis=0), table)
        weight_r = speed[0] * metric[0:1] + speed[1] * metric[1:2]
        weight_s = speed[0] * metric[2:3] + speed[1] * metric[3:4]
        terms = []
        for c in range(3):
            part = derived[2 * CHUNK * c : 2 * CHUNK * (c + 1)]
            terms.append(
                weight_r * part[:, :LANES]
                + weight_s * part[:, LANES:]
                + speed[2] * unpacked(slope, c)
            )
        total = repacked(terms)
        ahead = total[:CHUNK]
        mirror = total[CHUNK:]
        differences[rows, :] = ahead - mirror
        if i == 0:
            product_middle = mirror[0:1]
            mirror = jnp.where(opening, 0.0, mirror)
        sums[rows, :] = ahead + mirror
    index = index[:KEPT]
    weight = jnp.where(index <= PLANES // 3, -2.0 / PLANES, 0.0)
    result = table_times(fourier[0, :KEPT], sums[...]) + sign[:KEPT] * product_middle
    results = [jnp.where(index == 0, 0.5 * weight, weight) * result]
    result = table_times(fourier[1, :KEPT], differences[...])
    results.append(jnp.where(index == 0, 0.0, weight) * result)
    half = ROWS // 2
    for m in range(KEPT // half):
        for tile in range(2):
            for parity in range(2):
                out[m, tile, pl.ds(parity, half, stride=2), :] = results[parity][
                    half * m : half * (m + 1), LANES * tile : LANES * (tile + 1)
                ]
    out[KEPT // half :] = jnp.zeros((QUADS - KEPT // half, 2, ROWS, LANES), f32)


def weigh_kernel(spectral, nodal, rims, share, first_out, second_out):
    for q in range(QUADS):
        here = slice(LANES * q, LANES * (q + 1))
        mass = nodal[4:5, here]
        block = jnp.concatenate([spectral[q, 0], spectral[q, 1]], axis=1)
        for c in range(3):
            share[ROWS * c : ROWS * (c + 1), here] = mass * jnp.where(
                mass > 0.0, unpacked(block, c), 0.0
            )
    share[3 * ROWS : 3 * ROWS + 1, :] = nodal[4:5, :]
    share[3 * ROWS + 1 : 3 * ROWS + 2, :] = nodal[5:6, :]
    share[3 * ROWS + 2 :, :] = jnp.zeros((STACK - 3 * ROWS - 2, WIDE), f32)
    rim = times_incidence(share[...], rims[...])
    first_out[...] = rim[:, :LANES]
    second_out[...] = rim[:, LANES:]


def joined(parity, share, own, first_in, second_in, joins, single):
    lane = lax.broadcasted_iota(jnp.int32, (1, LANES), 1)
    near = jnp.where(lane < EDGE, first_in[...], own[...])
    other = jnp.where(parity[0] > 0, second_in[0], second_in[1])
    sums = jnp.concatenate([near, other], axis=1)
    return share[...] * single + times_incidence(sums, joins[...])


def star_kernel(
    mode, parity, share, own, first_in, second_in, joins, rims, field, nodal, derive,
    star, inverse, share_out, first_out, second_out,
):
    metric = nodal[...]
    total = joined(parity, share, own, first_in, second_in, joins, metric[6:7])
    inside = metric[5:6] > 0.0
    scale = TIME_STEP / jnp.where(inside, total[3 * ROWS : 3 * ROWS + 1], 1.0)
    inverse[...] = jnp.where(
        inside, 1.0 / jnp.where(inside, total[3 * ROWS + 1 : 3 * ROWS + 2], 1.0), 0.0
    )
    star[...] = field[...] + scale * total[: 3 * ROWS]
    table = derive[...]
    star_x = gradient(star[0:ROWS], metric, table)[0]
    star_y = gradient(star[ROWS : 2 * ROWS], metric, table)[1]
    divergence = star_x + star_y + along_z(star[2 * ROWS :], mode[0])
    result = (-1.0 / TIME_STEP) * (metric[4:5] * divergence)
    share_out[...] = result
    rim = times_incidence(result, rims[...])
    first_out[...] = rim[:, :LANES]
    second_out[...] = rim[:, LANES:]


def lane_sum(x):
    total = x[:, :LANES]
    for q in range(1, QUADS):
        total = total + x[:, LANES * q : LANES * (q + 1)]
    return jnp.sum(total, axis=1, keepdims=True)


def helmholtz_kernel(
    mode, parity, share, own, first_in, second_in, joins, rims, nodal, inverse, derive, derive_back,
    right, right_x, right_y, share_out, first_out, second_out, sums,
):
    metric = nodal[...]
    total = joined(parity, share, own, first_in, second_in, joins, metric[6:7])
    mass = metric[4:5]
    rate, even = rates(mode[0])
    shift = rate * rate + PENALTY
    grad_x, grad_y = gradient(total, metric, derive[...])
    right[...] = total
    right_x[...] = grad_x
    right_y[...] = grad_y
    flux_x = mass * grad_x
    flux_y = mass * grad_y
    weighted = shift * (mass * total)
    part_r = metric[0:1] * flux_x + metric[1:2] * flux_y
    part_s = metric[2:3] * flux_x + metric[3:4] * flux_y
    both = jnp.concatenate([stacked(part_r), stacked(part_s)], axis=1)
    result = unstacked(times_table(both, derive_back[...])) + weighted
    share_out[...] = result
    rim = times_incidence(result, rims[...])
    first_out[...] = rim[:, :LANES]
    second_out[...] = rim[:, LANES:]
    square = lane_sum(total * total * inverse[...])
    energy = lane_sum(flux_x * grad_x + flux_y * grad_y + weighted * total)
    column = lax.broadcasted_iota(jnp.int32, (ROWS, LANES), 1)
    sums[...] = jnp.where(column == 0, square, jnp.where(column == 1, energy, 0.0))


def image_kernel(
    mode, parity, share, own, first_in, second_in, joins, nodal, inverse, derive, sums,
    image, image_x, image_y, spread,
):
    metric = nodal[...]
    total = joined(parity, share, own, first_in, second_in, joins, metric[6:7])
    mass = metric[4:5]
    rate, even = rates(mode[0])
    shift = rate * rate + PENALTY
    grad_x, grad_y = gradient(total, metric, derive[...])
    image[...] = total
    image_x[...] = grad_x
    image_y[...] = grad_y
    square = lane_sum(total * total * inverse[...])
    energy = lane_sum(mass * (grad_x * grad_x + grad_y * grad_y + shift * (total * total)))
    column = lax.broadcasted_iota(jnp.int32, (ROWS, LANES), 1)
    table = jnp.where(column == 2, square, jnp.where(column == 3, energy, sums[...]))
    table = jnp.concatenate([table, jnp.zeros((LANES - ROWS, LANES), f32)], axis=0)
    turned = jnp.transpose(table)
    short = jnp.concatenate(
        [
            turned[0:1] + pltpu.roll(turned[1:2], ROWS, 1),
            turned[2:3] + pltpu.roll(turned[3:4], ROWS, 1),
        ],
        axis=1,
    )
    spread[...] = jnp.broadcast_to(short, spread.shape)


def finish_kernel(
    mode, gathered, star, right, right_x, right_y, image, image_x, image_y,
    velocity_out, pressure_out,
):
    sums = jnp.sum(gathered[...], axis=0, keepdims=True)
    first = sums[:, :LANES]
    second = sums[:, LANES:]
    g0 = first
    g1 = pltpu.roll(first, ROWS, 1)
    g2 = second
    g3 = pltpu.roll(second, ROWS, 1)
    step0 = g0 / g1
    new = step0 * step0 * g2 - g0
    ratio = new / g0
    curve = (1.0 + ratio) * ((1.0 + ratio) * g1 - 2.0 * step0 * g2) + step0 * step0 * g3
    step1 = new / curve
    by_right = step0 + step1 * (1.0 + ratio)
    by_image = -step1 * step0
    pair = jnp.concatenate([by_right, by_image, jnp.zeros((6, LANES), f32)], axis=0)
    turned = jnp.transpose(pair)
    by_right = turned[:ROWS, 0:1]
    by_image = turned[:ROWS, 1:2]
    pressure = by_right * right[...] + by_image * image[...]
    slopes = [
        by_right * right_x[...] + by_image * image_x[...],
        by_right * right_y[...] + by_image * image_y[...],
        along_z(pressure, mode[0]),
    ]
    outs = [star[ROWS * c : ROWS * (c + 1)] - TIME_STEP * slopes[c] for c in range(3)]
    for q in range(QUADS):
        here = slice(QUAD_NODES * q, QUAD_NODES * (q + 1))
        there = slice(LANES * q, LANES * q + QUAD_NODES)
        for c in range(3):
            velocity_out[c, :, here] = outs[c][:, there]
        pressure_out[:, here] = pressure[:, there]


VMEM = pl.BlockSpec(memory_space=pltpu.VMEM)
SMEM = pl.BlockSpec(memory_space=pltpu.SMEM)
ANY = pl.BlockSpec(memory_space=pl.ANY)


def call(kernel, ins, outs, scratch=(), flops=0, name=None, aliases={}):
    specs = [SMEM if a.dtype == jnp.int32 and a.shape == (1,) else VMEM for a in ins]
    specs = [ANY if i in aliases else spec for i, spec in enumerate(specs)]
    shapes = [jax.ShapeDtypeStruct(s, d) for s, d in outs]
    size = sum(math.prod(a.shape) * a.dtype.itemsize for a in list(ins) + shapes)
    return pl.pallas_call(
        kernel,
        in_specs=specs,
        out_specs=[ANY if i in aliases.values() else VMEM for i in range(len(shapes))],
        out_shape=shapes,
        scratch_shapes=list(scratch),
        input_output_aliases=aliases,
        name=name,
        cost_estimate=pl.CostEstimate(flops=flops, bytes_accessed=size, transcendentals=0),
        compiler_params=pltpu.CompilerParams(vmem_limit_bytes=40 * 1024 * 1024),
    )(*ins)


def on_device(velocity, metric, mass, local_ids, edge_ids):
    derive, derive_back = (jnp.asarray(t) for t in derivative_tables())
    fourier = jnp.asarray(fourier_tables())
    mode = lax.axis_index("mode").astype(jnp.int32).reshape(1)
    parity = (lax.axis_index("elem") % 2).astype(jnp.int32).reshape(1)
    count = lax.axis_size("elem")
    across = [(i, (i + 1) % count) for i in range(1, count, 2)]
    across = across + [(target, source) for source, target in across]
    beside = [[i, i + 1] for i in range(0, count, 2)]

    def swap(first, second):
        return (
            lax.ppermute(first, "elem", across),
            lax.all_gather(second, "elem", axis_index_groups=beside),
        )

    block = (QUADS, 2, ROWS, LANES)
    (packed,) = call(
        pack_kernel, [velocity], [(block, f32)],
        name="pack",
    )
    nodal = jnp.concatenate([metric, mass[None]], axis=0)
    tables = [fourier, derive]
    field, nodal, own_metric, joins, rims, fourier, derive = call(
        prepare_kernel,
        [mode, parity, velocity, nodal, local_ids[None], edge_ids[0]] + tables,
        [
            ((3 * ROWS, WIDE), f32),
            ((8, WIDE), f32),
            ((8, LANES), f32),
            ((2 * LANES, WIDE), bf16),
            ((WIDE, 2 * LANES), bf16),
        ]
        + [(t.shape, bf16) for t in tables],
        flops=1 << 24,
        name="prepare",
        aliases={6: 5, 7: 6},
    )
    arrived = lax.all_to_all(packed, "mode", 0, 0)
    (spectral,) = call(
        convect_kernel,
        [arrived, own_metric, fourier, derive],
        [(block, f32)],
        scratch=[pltpu.VMEM((HALF, 2 * PACK), f32)] * 2 + [pltpu.VMEM((HALF, PACK), f32)] * 2,
        flops=1 << 30,
        name="convect",
    )
    returned = lax.all_to_all(spectral, "mode", 0, 0)
    rim_out = [((STACK, LANES), f32)] * 2
    share, first_out, second_out = call(
        weigh_kernel, [returned, nodal, rims], [((STACK, WIDE), f32)] + rim_out,
        flops=1 << 28, name="weigh",
    )
    first_in, second_in = swap(first_out, second_out)
    one = ((ROWS, WIDE), f32)
    rim_out = [((ROWS, LANES), f32)] * 2
    star, inverse, share, first_out, second_out = call(
        star_kernel,
        [mode, parity, share, first_out, first_in, second_in, joins, rims, field, nodal, derive],
        [((3 * ROWS, WIDE), f32), ((1, WIDE), f32), one] + rim_out,
        flops=1 << 29, name="star",
    )
    first_in, second_in = swap(first_out, second_out)
    right, right_x, right_y, share, first_out, second_out, sums = call(
        helmholtz_kernel,
        [mode, parity, share, first_out, first_in, second_in, joins, rims, nodal, inverse, derive, derive_back],
        [one, one, one, one] + rim_out + [((ROWS, LANES), f32)],
        flops=1 << 29, name="helmholtz",
    )
    first_in, second_in = swap(first_out, second_out)
    image, image_x, image_y, spread = call(
        image_kernel,
        [mode, parity, share, first_out, first_in, second_in, joins, nodal, inverse, derive, sums],
        [one, one, one, ((count, 1, 2 * LANES), f32)],
        flops=1 << 29, name="image",
    )
    gathered = lax.all_to_all(spread, "elem", 0, 0)
    gathered = gathered.reshape(count, 2 * LANES)
    velocity_new, pressure = call(
        finish_kernel,
        [mode, gathered, star, right, right_x, right_y, image, image_x, image_y],
        [((3, ROWS, QUADS * QUAD_NODES), f32), ((ROWS, QUADS * QUAD_NODES), f32)],
        name="finish",
    )
    return velocity_new, pressure


def solution(mesh):
    in_specs = (
        P(None, "mode", "elem"),
        P(None, "elem"),
        P("elem"),
        P("elem"),
        P("elem", None, None),
    )
    out_specs = (P(None, "mode", "elem"), P("mode", "elem"))
    return jax.shard_map(
        on_device, mesh=mesh, in_specs=in_specs, out_specs=out_specs, check_vma=False
    )
```

```python
import functools
import math

import jax
import jax.numpy as jnp
import numpy as np
from jax import lax
from jax.experimental import pallas as pl
from jax.experimental.pallas import tpu as pltpu
from jax.sharding import PartitionSpec as P

SIDE = 9
QUAD_NODES = 81
PLANES = 512
QUADS = 8
EDGE = 65
LANES = 128
WIDE = QUADS * LANES
PACK = 256
ROWS = 64
KEPT = 192
STACK = 200
CHUNK = 64
HALF = 256

SCALE = 2.0**-12
PENALTY = 1.0
TIME_STEP = 0.01

f32 = jnp.float32
bf16 = jnp.bfloat16


def legendre_pair(points, degree):
    previous = points * 0.0 + 1.0
    current = points.copy()
    for order in range(2, degree + 1):
        following = ((2.0 * order - 1.0) * points * current - (order - 1.0) * previous) / order
        previous = current
        current = following
    return (previous, current)


def derivative_matrix():
    degree = SIDE - 1
    points = np.cos(math.pi * np.arange(degree + 1) / degree)
    for sweep in range(100):
        lower, upper = legendre_pair(points, degree)
        points = points - (points * upper - lower) / ((degree + 1.0) * upper)
    points = points[::-1].copy()
    values = legendre_pair(points, degree)[1]
    identity = np.eye(SIDE)
    differ = points[:, None] - points[None, :] + identity
    matrix = np.where(identity > 0.5, 0.0, values[:, None] / (values[None, :] * differ))
    matrix[0, 0] = -degree * (degree + 1) / 4.0
    matrix[degree, degree] = degree * (degree + 1) / 4.0
    return matrix


def halves(table):
    high = table.astype(np.float32).astype(jnp.bfloat16)
    low = (table - high.astype(np.float64)).astype(np.float32).astype(jnp.bfloat16)
    return high, low


def as_right(table):
    high, low = halves(table)
    return np.concatenate([high, high, low], axis=0)


def as_left(table):
    high, low = halves(table)
    return np.concatenate([high, high, low], axis=1)


def derivative_tables():
    matrix = derivative_matrix()
    table = np.zeros((LANES, 2 * LANES))
    table[:QUAD_NODES, :QUAD_NODES] = np.kron(matrix, np.eye(SIDE)).T
    table[:QUAD_NODES, LANES : LANES + QUAD_NODES] = np.kron(np.eye(SIDE), matrix).T
    table = table.astype(np.float32).astype(np.float64)
    return as_right(table), as_right(table.T.copy())


def fourier_tables():
    index = np.arange(HALF)
    angles = 2.0 * math.pi / PLANES * (index[:, None] * index[None, :] % PLANES)
    return np.stack([as_left(np.cos(angles)), as_left(np.sin(angles))])


def split2(x):
    high = x.astype(bf16)
    return high, (x - high.astype(f32)).astype(bf16)


def mm(a, b):
    return jnp.dot(a, b, preferred_element_type=f32)


def times_table(x, table):
    high, low = split2(x)
    return mm(jnp.concatenate([high, low, high], axis=1), table)


def table_times(table, x):
    high, low = split2(x)
    return mm(table, jnp.concatenate([high, low, high], axis=0))


def times_incidence(x, incidence):
    rows = x.shape[0]
    out = mm(jnp.concatenate(split2(x), axis=0), incidence)
    return out[:rows] + out[rows:]


def stacked(x):
    return jnp.concatenate([x[:, LANES * q : LANES * (q + 1)] for q in range(QUADS)], axis=0)


def unstacked(x):
    rows = x.shape[0] // QUADS
    return jnp.concatenate([x[rows * q : rows * (q + 1)] for q in range(QUADS)], axis=1)


def gradient(x, metric, table):
    derived = times_table(stacked(x), table)
    along_r = unstacked(derived[:, :LANES])
    along_s = unstacked(derived[:, LANES:])
    return (
        metric[0:1] * along_r + metric[2:3] * along_s,
        metric[1:2] * along_r + metric[3:4] * along_s,
    )


def rates(mode):
    row = lax.broadcasted_iota(jnp.int32, (ROWS, 1), 0)
    return (8.0 / PLANES) * ((mode * ROWS + row) // 2).astype(f32), row % 2 == 0


def along_z(x, mode):
    rate, even = rates(mode)
    return rate * jnp.where(even, pltpu.roll(x, ROWS - 1, 0), -pltpu.roll(x, 1, 0))


def lanes_at():
    return lax.broadcasted_iota(jnp.int32, (1, LANES), 1)


def unpacked(x, field):
    first, second = x[:, :LANES], x[:, LANES:]
    if field == 0:
        return first
    if field == 1:
        both = jnp.where(lanes_at() < QUAD_NODES, second, first)
        return pltpu.roll(both, LANES - QUAD_NODES, 1)
    return pltpu.roll(second, 2 * (LANES - QUAD_NODES), 1)


def repacked(fields):
    lane = lanes_at()
    second_at = 2 * QUAD_NODES - LANES
    middle = pltpu.roll(fields[1], QUAD_NODES, 1)
    last = jnp.where(lane < second_at + QUAD_NODES, pltpu.roll(fields[2], second_at, 1), 0.0)
    return jnp.concatenate(
        [jnp.where(lane < QUAD_NODES, fields[0], middle), jnp.where(lane < second_at, middle, last)],
        axis=1,
    )


def pack_kernel(velocity, packed):
    for q in range(QUADS):
        for c in range(3):
            start, stop = QUAD_NODES * c, QUAD_NODES * (c + 1)
            for tile in range(start // LANES, (stop - 1) // LANES + 1):
                low, high = max(start, LANES * tile), min(stop, LANES * (tile + 1))
                node = QUAD_NODES * q - start
                packed[q, tile, :, low - LANES * tile : high - LANES * tile] = velocity[
                    c, :, node + low : node + high
                ]
        packed[q, 1, :, 3 * QUAD_NODES - LANES :] = jnp.zeros((ROWS, PACK - 3 * QUAD_NODES), f32)


def matches(column, row):
    return jnp.where(column == row, 1.0, 0.0)


def prepare_kernel(
    mode, parity, velocity, nodal, ids, edges, fourier, derive,
    field, nodal_wide, own_metric, joins, rims, fourier_on, derive_on,
):
    lane = lax.broadcasted_iota(jnp.int32, (1, LANES), 1)
    inside = lane < QUAD_NODES
    field[...] = jnp.zeros_like(field)
    nodal_wide[...] = jnp.zeros_like(nodal_wide)
    for q in range(QUADS):
        here = slice(LANES * q, LANES * q + QUAD_NODES)
        there = slice(QUAD_NODES * q, QUAD_NODES * (q + 1))
        for c in range(3):
            field[ROWS * c : ROWS * (c + 1), here] = velocity[c, :, there]
        nodal_wide[0:5, here] = nodal[0:5, there]
        nodal_wide[5:6, here] = jnp.ones((1, QUAD_NODES), f32)
    own = jnp.zeros((8, LANES), f32)
    for q in range(QUADS):
        own = own + jnp.where(mode[0] == q, nodal_wide[:, LANES * q : LANES * (q + 1)], 0.0)
    own_metric[...] = own
    ids_row = [
        jnp.concatenate(
            [
                ids[:, QUAD_NODES * q : QUAD_NODES * (q + 1)],
                jnp.full((1, LANES - QUAD_NODES), -1, jnp.int32),
            ],
            axis=1,
        ).astype(f32)
        for q in range(QUADS)
    ]
    ids_wide = jnp.concatenate(ids_row, axis=1)
    odd = parity[0] > 0
    edge_row = [
        jnp.concatenate(
            [
                jnp.where(odd, edges[1 - s : 2 - s, :], edges[s : s + 1, :]),
                jnp.full((1, LANES - EDGE), -2, jnp.int32),
            ],
            axis=1,
        ).astype(f32)
        for s in range(2)
    ]
    columns = jnp.transpose(jnp.concatenate(ids_row, axis=0))
    column = [columns[:, q : q + 1] for q in range(QUADS)]
    row_at = lax.broadcasted_iota(jnp.int32, (LANES, LANES), 0)
    lane_at = lax.broadcasted_iota(jnp.int32, (LANES, LANES), 1)
    opens = []
    for q in range(QUADS):
        total = jnp.zeros((LANES, LANES), f32)
        before = jnp.zeros((LANES, LANES), f32)
        for p in range(QUADS):
            same = matches(column[p], ids_row[q])
            total = total + same
            if p < q:
                before = before + same
            if p == q:
                before = before + jnp.where(row_at < lane_at, same, 0.0)
        copies = jnp.sum(total, axis=0, keepdims=True)
        earlier = jnp.sum(before, axis=0, keepdims=True)
        shared = jnp.where(inside & (copies > 1.5), 1.0, 0.0)
        opens.append(jnp.where(earlier < 0.5, shared, 0.0))
        nodal_wide[6:7, LANES * q : LANES * (q + 1)] = jnp.where(inside, 1.0 - shared, 0.0)
    opens = jnp.concatenate(opens, axis=0)
    triangle = jnp.where(row_at < lane_at, 1.0, 0.0).astype(bf16)
    rank = mm(opens.astype(bf16), triangle)
    counts = jnp.sum(opens, axis=1, keepdims=True)
    offset = jnp.zeros((1, 1), f32)
    offsets = []
    for q in range(QUADS):
        offsets.append(offset)
        offset = offset + counts[q : q + 1]
    slot = jnp.where(opens > 0.5, rank + jnp.concatenate(offsets, axis=0) + float(EDGE), -1.0)
    slots = jnp.transpose(slot)
    lanes = lane.astype(f32)
    hits = jnp.zeros((LANES, LANES), f32)
    named = jnp.zeros((LANES, LANES), f32)
    for q in range(QUADS):
        hit = matches(slots[:, q : q + 1], lanes)
        hits = hits + hit
        named = named + hit * column[q]
    hits = jnp.sum(hits, axis=0, keepdims=True)
    named = jnp.sum(named, axis=0, keepdims=True)
    first = jnp.where(lane < EDGE, edge_row[0], jnp.where(hits > 0.5, named, -3.0))
    keys = [first, edge_row[1]]
    key_columns = jnp.transpose(jnp.concatenate(keys + [first] * 6, axis=0))
    for q in range(QUADS):
        for s in range(2):
            rims[LANES * q : LANES * (q + 1), LANES * s : LANES * (s + 1)] = matches(
                column[q], keys[s]
            ).astype(bf16)
    for s in range(2):
        joins[LANES * s : LANES * (s + 1), :] = matches(
            key_columns[:, s : s + 1], ids_wide
        ).astype(bf16)


def convect_kernel(packed, own_metric, fourier, derive, out, even, odd, sums, differences):
    metric = own_metric[...]
    table = derive[...]
    index = lax.broadcasted_iota(jnp.int32, (HALF, 1), 0)
    rate = (8.0 / PLANES) * index.astype(f32)
    sign = jnp.where(index % 2 == 0, 1.0, -1.0)
    cosines, sines = (
        jnp.concatenate(
            [
                jnp.concatenate(
                    [packed[m, tile, pl.ds(parity, ROWS // 2, stride=2), :] for tile in range(2)],
                    axis=1,
                )
                for m in range(QUADS)
            ],
            axis=0,
        )
        for parity in range(2)
    )
    highest = sines[0:1]
    to_even = jnp.concatenate([cosines, rate * sines], axis=1)
    to_odd = jnp.concatenate([sines, -rate * cosines], axis=1)
    even[...] = table_times(fourier[0], to_even)
    even[:, :PACK] = even[:, :PACK] + sign * highest
    middle = jnp.sum(sign * to_even, axis=0, keepdims=True)
    middle = middle + jnp.concatenate([highest, jnp.zeros_like(highest)], axis=1)
    odd[...] = table_times(fourier[1], to_odd)
    opening = lax.broadcasted_iota(jnp.int32, (CHUNK, 1), 0) == 0
    product_middle = None
    for i in range(HALF // CHUNK):
        rows = slice(CHUNK * i, CHUNK * (i + 1))
        part_even = even[rows]
        part_odd = odd[rows]
        ahead = part_even + part_odd
        if i == 0:
            part_even = jnp.where(opening, middle, part_even)
        wide = jnp.concatenate([ahead, part_even - part_odd], axis=0)
        value = wide[:, :PACK]
        slope = wide[:, PACK:]
        speed = [unpacked(value, c) for c in range(3)]
        derived = times_table(jnp.concatenate(speed, axis=0), table)
        weight_r = speed[0] * metric[0:1] + speed[1] * metric[1:2]
        weight_s = speed[0] * metric[2:3] + speed[1] * metric[3:4]
        terms = []
        for c in range(3):
            part = derived[2 * CHUNK * c : 2 * CHUNK * (c + 1)]
            terms.append(
                weight_r * part[:, :LANES]
                + weight_s * part[:, LANES:]
                + speed[2] * unpacked(slope, c)
            )
        total = repacked(terms)
        ahead = total[:CHUNK]
        mirror = total[CHUNK:]
        differences[rows, :] = ahead - mirror
        if i == 0:
            product_middle = mirror[0:1]
            mirror = jnp.where(opening, 0.0, mirror)
        sums[rows, :] = ahead + mirror
    index = index[:KEPT]
    weight = jnp.where(index <= PLANES // 3, -2.0 / PLANES, 0.0)
    result = table_times(fourier[0, :KEPT], sums[...]) + sign[:KEPT] * product_middle
    results = [jnp.where(index == 0, 0.5 * weight, weight) * result]
    result = table_times(fourier[1, :KEPT], differences[...])
    results.append(jnp.where(index == 0, 0.0, weight) * result)
    half = ROWS // 2
    for m in range(KEPT // half):
        for tile in range(2):
            for parity in range(2):
                out[m, tile, pl.ds(parity, half, stride=2), :] = results[parity][
                    half * m : half * (m + 1), LANES * tile : LANES * (tile + 1)
                ]
    out[KEPT // half :] = jnp.zeros((QUADS - KEPT // half, 2, ROWS, LANES), f32)


def weigh_kernel(spectral, nodal, rims, share, first_out, second_out):
    for q in range(QUADS):
        here = slice(LANES * q, LANES * (q + 1))
        mass = nodal[4:5, here]
        block = jnp.concatenate([spectral[q, 0], spectral[q, 1]], axis=1)
        for c in range(3):
            share[ROWS * c : ROWS * (c + 1), here] = mass * jnp.where(
                mass > 0.0, unpacked(block, c), 0.0
            )
    share[3 * ROWS : 3 * ROWS + 1, :] = nodal[4:5, :]
    share[3 * ROWS + 1 : 3 * ROWS + 2, :] = nodal[5:6, :]
    share[3 * ROWS + 2 :, :] = jnp.zeros((STACK - 3 * ROWS - 2, WIDE), f32)
    rim = times_incidence(share[...], rims[...])
    first_out[...] = rim[:, :LANES]
    second_out[...] = rim[:, LANES:]


def joined(parity, share, own, first_in, second_in, joins, single):
    lane = lax.broadcasted_iota(jnp.int32, (1, LANES), 1)
    near = jnp.where(lane < EDGE, first_in[...], own[...])
    other = jnp.where(parity[0] > 0, second_in[0], second_in[1])
    sums = jnp.concatenate([near, other], axis=1)
    return share[...] * single + times_incidence(sums, joins[...])


def star_kernel(
    mode, parity, share, own, first_in, second_in, joins, rims, field, nodal, derive,
    star, inverse, share_out, first_out, second_out,
):
    metric = nodal[...]
    total = joined(parity, share, own, first_in, second_in, joins, metric[6:7])
    inside = metric[5:6] > 0.0
    scale = TIME_STEP / jnp.where(inside, total[3 * ROWS : 3 * ROWS + 1], 1.0)
    inverse[...] = jnp.where(
        inside, 1.0 / jnp.where(inside, total[3 * ROWS + 1 : 3 * ROWS + 2], 1.0), 0.0
    )
    star[...] = field[...] + scale * total[: 3 * ROWS]
    table = derive[...]
    star_x = gradient(star[0:ROWS], metric, table)[0]
    star_y = gradient(star[ROWS : 2 * ROWS], metric, table)[1]
    divergence = star_x + star_y + along_z(star[2 * ROWS :], mode[0])
    result = (-1.0 / TIME_STEP) * (metric[4:5] * divergence)
    share_out[...] = result
    rim = times_incidence(result, rims[...])
    first_out[...] = rim[:, :LANES]
    second_out[...] = rim[:, LANES:]


def lane_sum(x):
    total = x[:, :LANES]
    for q in range(1, QUADS):
        total = total + x[:, LANES * q : LANES * (q + 1)]
    return jnp.sum(total, axis=1, keepdims=True)


def helmholtz_kernel(
    mode, parity, share, own, first_in, second_in, joins, rims, nodal, inverse, derive, derive_back,
    right, right_x, right_y, share_out, first_out, second_out, sums,
):
    metric = nodal[...]
    total = joined(parity, share, own, first_in, second_in, joins, metric[6:7])
    mass = metric[4:5]
    rate, even = rates(mode[0])
    shift = rate * rate + PENALTY
    grad_x, grad_y = gradient(total, metric, derive[...])
    right[...] = total
    right_x[...] = grad_x
    right_y[...] = grad_y
    flux_x = mass * grad_x
    flux_y = mass * grad_y
    weighted = shift * (mass * total)
    part_r = metric[0:1] * flux_x + metric[1:2] * flux_y
    part_s = metric[2:3] * flux_x + metric[3:4] * flux_y
    both = jnp.concatenate([stacked(part_r), stacked(part_s)], axis=1)
    result = unstacked(times_table(both, derive_back[...])) + weighted
    share_out[...] = result
    rim = times_incidence(result, rims[...])
    first_out[...] = rim[:, :LANES]
    second_out[...] = rim[:, LANES:]
    square = lane_sum(total * total * inverse[...])
    energy = SCALE * lane_sum(flux_x * grad_x + flux_y * grad_y + weighted * total)
    column = lax.broadcasted_iota(jnp.int32, (ROWS, LANES), 1)
    sums[...] = jnp.where(column == 0, square, jnp.where(column == 1, energy, 0.0))


def image_kernel(
    mode, parity, share, own, first_in, second_in, joins, nodal, inverse, derive, sums,
    image, image_x, image_y, spread,
):
    metric = nodal[...]
    total = joined(parity, share, own, first_in, second_in, joins, metric[6:7])
    mass = metric[4:5]
    rate, even = rates(mode[0])
    shift = rate * rate + PENALTY
    grad_x, grad_y = gradient(total, metric, derive[...])
    image[...] = total
    image_x[...] = grad_x
    image_y[...] = grad_y
    square = lane_sum(total * total * (SCALE**2 * inverse[...]))
    energy = grad_x * grad_x + grad_y * grad_y + shift * (total * total)
    energy = lane_sum((SCALE**3 * mass) * energy)
    column = lax.broadcasted_iota(jnp.int32, (ROWS, LANES), 1)
    table = jnp.where(column == 2, square, jnp.where(column == 3, energy, sums[...]))
    table = jnp.concatenate([table, jnp.zeros((LANES - ROWS, LANES), f32)], axis=0)
    turned = jnp.transpose(table)
    short = jnp.concatenate(
        [
            turned[0:1] + pltpu.roll(turned[1:2], ROWS, 1),
            turned[2:3] + pltpu.roll(turned[3:4], ROWS, 1),
        ],
        axis=1,
    )
    spread[...] = jnp.broadcast_to(short, spread.shape)


def finish_kernel(
    mode, gathered, star, right, right_x, right_y, image, image_x, image_y,
    velocity_out, pressure_out,
):
    sums = jnp.sum(gathered[...], axis=0, keepdims=True)
    first = sums[:, :LANES]
    second = sums[:, LANES:]
    g0 = first
    g1 = pltpu.roll(first, ROWS, 1)
    g2 = second
    g3 = pltpu.roll(second, ROWS, 1)
    step0 = g0 / g1
    new = step0 * step0 * g2 - g0
    ratio = new / g0
    curve = (1.0 + ratio) * ((1.0 + ratio) * g1 - 2.0 * step0 * g2) + step0 * step0 * g3
    step1 = new / curve
    by_right = SCALE * (step0 + step1 * (1.0 + ratio))
    by_image = -(SCALE * step1) * (SCALE * step0)
    pair = jnp.concatenate([by_right, by_image, jnp.zeros((6, LANES), f32)], axis=0)
    turned = jnp.transpose(pair)
    by_right = turned[:ROWS, 0:1]
    by_image = turned[:ROWS, 1:2]
    pressure = by_right * right[...] + by_image * image[...]
    slopes = [
        by_right * right_x[...] + by_image * image_x[...],
        by_right * right_y[...] + by_image * image_y[...],
        along_z(pressure, mode[0]),
    ]
    outs = [star[ROWS * c : ROWS * (c + 1)] - TIME_STEP * slopes[c] for c in range(3)]
    for q in range(QUADS):
        here = slice(QUAD_NODES * q, QUAD_NODES * (q + 1))
        there = slice(LANES * q, LANES * q + QUAD_NODES)
        for c in range(3):
            velocity_out[c, :, here] = outs[c][:, there]
        pressure_out[:, here] = pressure[:, there]


VMEM = pl.BlockSpec(memory_space=pltpu.VMEM)
SMEM = pl.BlockSpec(memory_space=pltpu.SMEM)
ANY = pl.BlockSpec(memory_space=pl.ANY)


def call(kernel, ins, outs, scratch=(), flops=0, name=None, aliases={}):
    specs = [SMEM if a.dtype == jnp.int32 and a.shape == (1,) else VMEM for a in ins]
    specs = [ANY if i in aliases else spec for i, spec in enumerate(specs)]
    shapes = [jax.ShapeDtypeStruct(s, d) for s, d in outs]
    size = sum(math.prod(a.shape) * a.dtype.itemsize for a in list(ins) + shapes)
    return pl.pallas_call(
        kernel,
        in_specs=specs,
        out_specs=[ANY if i in aliases.values() else VMEM for i in range(len(shapes))],
        out_shape=shapes,
        scratch_shapes=list(scratch),
        input_output_aliases=aliases,
        name=name,
        cost_estimate=pl.CostEstimate(flops=flops, bytes_accessed=size, transcendentals=0),
        compiler_params=pltpu.CompilerParams(vmem_limit_bytes=40 * 1024 * 1024),
    )(*ins)


def on_device(velocity, metric, mass, local_ids, edge_ids):
    derive, derive_back = (jnp.asarray(t) for t in derivative_tables())
    fourier = jnp.asarray(fourier_tables())
    mode = lax.axis_index("mode").astype(jnp.int32).reshape(1)
    parity = (lax.axis_index("elem") % 2).astype(jnp.int32).reshape(1)
    count = lax.axis_size("elem")
    across = [(i, (i + 1) % count) for i in range(1, count, 2)]
    across = across + [(target, source) for source, target in across]
    beside = [[i, i + 1] for i in range(0, count, 2)]

    def swap(first, second):
        return (
            lax.ppermute(first, "elem", across),
            lax.all_gather(second, "elem", axis_index_groups=beside),
        )

    block = (QUADS, 2, ROWS, LANES)
    (packed,) = call(
        pack_kernel, [velocity], [(block, f32)],
        name="pack",
    )
    nodal = jnp.concatenate([metric, mass[None]], axis=0)
    tables = [fourier, derive]
    field, nodal, own_metric, joins, rims, fourier, derive = call(
        prepare_kernel,
        [mode, parity, velocity, nodal, local_ids[None], edge_ids[0]] + tables,
        [
            ((3 * ROWS, WIDE), f32),
            ((8, WIDE), f32),
            ((8, LANES), f32),
            ((2 * LANES, WIDE), bf16),
            ((WIDE, 2 * LANES), bf16),
        ]
        + [(t.shape, bf16) for t in tables],
        flops=1 << 24,
        name="prepare",
        aliases={6: 5, 7: 6},
    )
    arrived = lax.all_to_all(packed, "mode", 0, 0)
    (spectral,) = call(
        convect_kernel,
        [arrived, own_metric, fourier, derive],
        [(block, f32)],
        scratch=[pltpu.VMEM((HALF, 2 * PACK), f32)] * 2 + [pltpu.VMEM((HALF, PACK), f32)] * 2,
        flops=1 << 30,
        name="convect",
    )
    returned = lax.all_to_all(spectral, "mode", 0, 0)
    rim_out = [((STACK, LANES), f32)] * 2
    share, first_out, second_out = call(
        weigh_kernel, [returned, nodal, rims], [((STACK, WIDE), f32)] + rim_out,
        flops=1 << 28, name="weigh",
    )
    first_in, second_in = swap(first_out, second_out)
    one = ((ROWS, WIDE), f32)
    rim_out = [((ROWS, LANES), f32)] * 2
    star, inverse, share, first_out, second_out = call(
        star_kernel,
        [mode, parity, share, first_out, first_in, second_in, joins, rims, field, nodal, derive],
        [((3 * ROWS, WIDE), f32), ((1, WIDE), f32), one] + rim_out,
        flops=1 << 29, name="star",
    )
    first_in, second_in = swap(first_out, second_out)
    right, right_x, right_y, share, first_out, second_out, sums = call(
        helmholtz_kernel,
        [mode, parity, share, first_out, first_in, second_in, joins, rims, nodal, inverse, derive, derive_back],
        [one, one, one, one] + rim_out + [((ROWS, LANES), f32)],
        flops=1 << 29, name="helmholtz",
    )
    first_in, second_in = swap(first_out, second_out)
    image, image_x, image_y, spread = call(
        image_kernel,
        [mode, parity, share, first_out, first_in, second_in, joins, nodal, inverse, derive, sums],
        [one, one, one, ((count, 1, 2 * LANES), f32)],
        flops=1 << 29, name="image",
    )
    gathered = lax.all_to_all(spread, "elem", 0, 0)
    gathered = gathered.reshape(count, 2 * LANES)
    velocity_new, pressure = call(
        finish_kernel,
        [mode, gathered, star, right, right_x, right_y, image, image_x, image_y],
        [((3, ROWS, QUADS * QUAD_NODES), f32), ((ROWS, QUADS * QUAD_NODES), f32)],
        name="finish",
    )
    return velocity_new, pressure


def solution(mesh):
    in_specs = (
        P(None, "mode", "elem"),
        P(None, "elem"),
        P("elem"),
        P("elem"),
        P("elem", None, None),
    )
    out_specs = (P(None, "mode", "elem"), P("mode", "elem"))
    return jax.shard_map(
        on_device, mesh=mesh, in_specs=in_specs, out_specs=out_specs, check_vma=False
    )
```

```python
import functools
import math

import jax
import jax.numpy as jnp
import numpy as np
from jax import lax
from jax.experimental import pallas as pl
from jax.experimental.pallas import tpu as pltpu
from jax.sharding import PartitionSpec as P

SIDE = 9
QUAD_NODES = 81
PLANES = 512
QUADS = 8
EDGE = 65
LANES = 128
WIDE = QUADS * LANES
PACK = 256
ROWS = 64
KEPT = 192
STACK = 200
CHUNK = 64
HALF = 256

SCALE = 2.0**-12
PENALTY = 1.0
TIME_STEP = 0.01

f32 = jnp.float32
bf16 = jnp.bfloat16


def legendre_pair(points, degree):
    previous = points * 0.0 + 1.0
    current = points.copy()
    for order in range(2, degree + 1):
        following = ((2.0 * order - 1.0) * points * current - (order - 1.0) * previous) / order
        previous = current
        current = following
    return (previous, current)


def derivative_matrix():
    degree = SIDE - 1
    points = np.cos(math.pi * np.arange(degree + 1) / degree)
    for sweep in range(100):
        lower, upper = legendre_pair(points, degree)
        points = points - (points * upper - lower) / ((degree + 1.0) * upper)
    points = points[::-1].copy()
    values = legendre_pair(points, degree)[1]
    identity = np.eye(SIDE)
    differ = points[:, None] - points[None, :] + identity
    matrix = np.where(identity > 0.5, 0.0, values[:, None] / (values[None, :] * differ))
    matrix[0, 0] = -degree * (degree + 1) / 4.0
    matrix[degree, degree] = degree * (degree + 1) / 4.0
    return matrix


def halves(table):
    high = table.astype(np.float32).astype(jnp.bfloat16)
    low = (table - high.astype(np.float64)).astype(np.float32).astype(jnp.bfloat16)
    return high, low


def as_right(table):
    high, middle = halves(table)
    rest = table - high.astype(np.float64) - middle.astype(np.float64)
    return np.concatenate([high, middle, rest.astype(np.float32).astype(jnp.bfloat16)], axis=0)


def as_left(table):
    return np.concatenate(halves(table), axis=1)


def derivative_tables():
    matrix = derivative_matrix()
    table = np.zeros((LANES, 2 * LANES))
    table[:QUAD_NODES, :QUAD_NODES] = np.kron(matrix, np.eye(SIDE)).T
    table[:QUAD_NODES, LANES : LANES + QUAD_NODES] = np.kron(np.eye(SIDE), matrix).T
    table = table.astype(np.float32).astype(np.float64)
    return as_right(table), as_right(table.T.copy())


def fourier_tables():
    index = np.arange(HALF)
    angles = 2.0 * math.pi / PLANES * (index[:, None] * index[None, :] % PLANES)
    return np.stack([as_left(np.cos(angles)), as_left(np.sin(angles))])


def split2(x):
    high = x.astype(bf16)
    return high, (x - high.astype(f32)).astype(bf16)


def mm(a, b):
    return jnp.dot(a, b, preferred_element_type=f32)


def split3(x):
    high = x.astype(bf16)
    rest = x - high.astype(f32)
    middle = rest.astype(bf16)
    return high, middle, (rest - middle.astype(f32)).astype(bf16)


def times_table(x, table):
    inner = x.shape[1]
    high, low = split2(x)
    table = jnp.concatenate([table[:inner], table[: 2 * inner]], axis=0)
    return mm(jnp.concatenate([low, high, high], axis=1), table)


def times_fine(x, table):
    inner = x.shape[1]
    high, middle, low = split3(x)
    table = jnp.concatenate([table[:inner], table[: 2 * inner], table], axis=0)
    return mm(jnp.concatenate([low, middle, middle, high, high, high], axis=1), table)


def table_times(table, x):
    inner = x.shape[0]
    high, low = split2(x)
    table = jnp.concatenate([table[:, :inner], table], axis=1)
    return mm(table, jnp.concatenate([low, high, high], axis=0))


def times_incidence(x, incidence):
    rows = x.shape[0]
    out = mm(jnp.concatenate(split2(x), axis=0), incidence)
    return out[:rows] + out[rows:]


def stacked(x):
    return jnp.concatenate([x[:, LANES * q : LANES * (q + 1)] for q in range(QUADS)], axis=0)


def unstacked(x):
    rows = x.shape[0] // QUADS
    return jnp.concatenate([x[rows * q : rows * (q + 1)] for q in range(QUADS)], axis=1)


def gradient(x, metric, table, times=times_table):
    derived = times(stacked(x), table)
    along_r = unstacked(derived[:, :LANES])
    along_s = unstacked(derived[:, LANES:])
    return (
        metric[0:1] * along_r + metric[2:3] * along_s,
        metric[1:2] * along_r + metric[3:4] * along_s,
    )


def rates(mode):
    row = lax.broadcasted_iota(jnp.int32, (ROWS, 1), 0)
    return (8.0 / PLANES) * ((mode * ROWS + row) // 2).astype(f32), row % 2 == 0


def along_z(x, mode):
    rate, even = rates(mode)
    return rate * jnp.where(even, pltpu.roll(x, ROWS - 1, 0), -pltpu.roll(x, 1, 0))


def lanes_at():
    return lax.broadcasted_iota(jnp.int32, (1, LANES), 1)


def unpacked(x, field):
    first, second = x[:, :LANES], x[:, LANES:]
    if field == 0:
        return first
    if field == 1:
        both = jnp.where(lanes_at() < QUAD_NODES, second, first)
        return pltpu.roll(both, LANES - QUAD_NODES, 1)
    return pltpu.roll(second, 2 * (LANES - QUAD_NODES), 1)


def repacked(fields):
    lane = lanes_at()
    second_at = 2 * QUAD_NODES - LANES
    middle = pltpu.roll(fields[1], QUAD_NODES, 1)
    last = jnp.where(lane < second_at + QUAD_NODES, pltpu.roll(fields[2], second_at, 1), 0.0)
    return jnp.concatenate(
        [jnp.where(lane < QUAD_NODES, fields[0], middle), jnp.where(lane < second_at, middle, last)],
        axis=1,
    )


def pack_kernel(velocity, packed):
    for q in range(QUADS):
        for c in range(3):
            start, stop = QUAD_NODES * c, QUAD_NODES * (c + 1)
            for tile in range(start // LANES, (stop - 1) // LANES + 1):
                low, high = max(start, LANES * tile), min(stop, LANES * (tile + 1))
                node = QUAD_NODES * q - start
                packed[q, tile, :, low - LANES * tile : high - LANES * tile] = velocity[
                    c, :, node + low : node + high
                ]
        packed[q, 1, :, 3 * QUAD_NODES - LANES :] = jnp.zeros((ROWS, PACK - 3 * QUAD_NODES), f32)


def matches(column, row):
    return jnp.where(column == row, 1.0, 0.0)


def prepare_kernel(
    mode, parity, velocity, nodal, ids, edges, fourier, derive,
    field, nodal_wide, own_metric, joins, rims, fourier_on, derive_on,
):
    lane = lax.broadcasted_iota(jnp.int32, (1, LANES), 1)
    inside = lane < QUAD_NODES
    field[...] = jnp.zeros_like(field)
    nodal_wide[...] = jnp.zeros_like(nodal_wide)
    for q in range(QUADS):
        here = slice(LANES * q, LANES * q + QUAD_NODES)
        there = slice(QUAD_NODES * q, QUAD_NODES * (q + 1))
        for c in range(3):
            field[ROWS * c : ROWS * (c + 1), here] = velocity[c, :, there]
        nodal_wide[0:5, here] = nodal[0:5, there]
        nodal_wide[5:6, here] = jnp.ones((1, QUAD_NODES), f32)
    own = jnp.zeros((8, LANES), f32)
    for q in range(QUADS):
        own = own + jnp.where(mode[0] == q, nodal_wide[:, LANES * q : LANES * (q + 1)], 0.0)
    own_metric[...] = own
    ids_row = [
        jnp.concatenate(
            [
                ids[:, QUAD_NODES * q : QUAD_NODES * (q + 1)],
                jnp.full((1, LANES - QUAD_NODES), -1, jnp.int32),
            ],
            axis=1,
        ).astype(f32)
        for q in range(QUADS)
    ]
    ids_wide = jnp.concatenate(ids_row, axis=1)
    odd = parity[0] > 0
    edge_row = [
        jnp.concatenate(
            [
                jnp.where(odd, edges[1 - s : 2 - s, :], edges[s : s + 1, :]),
                jnp.full((1, LANES - EDGE), -2, jnp.int32),
            ],
            axis=1,
        ).astype(f32)
        for s in range(2)
    ]
    columns = jnp.transpose(jnp.concatenate(ids_row, axis=0))
    column = [columns[:, q : q + 1] for q in range(QUADS)]
    row_at = lax.broadcasted_iota(jnp.int32, (LANES, LANES), 0)
    lane_at = lax.broadcasted_iota(jnp.int32, (LANES, LANES), 1)
    opens = []
    for q in range(QUADS):
        total = jnp.zeros((LANES, LANES), f32)
        before = jnp.zeros((LANES, LANES), f32)
        for p in range(QUADS):
            same = matches(column[p], ids_row[q])
            total = total + same
            if p < q:
                before = before + same
            if p == q:
                before = before + jnp.where(row_at < lane_at, same, 0.0)
        copies = jnp.sum(total, axis=0, keepdims=True)
        earlier = jnp.sum(before, axis=0, keepdims=True)
        shared = jnp.where(inside & (copies > 1.5), 1.0, 0.0)
        opens.append(jnp.where(earlier < 0.5, shared, 0.0))
        nodal_wide[6:7, LANES * q : LANES * (q + 1)] = jnp.where(inside, 1.0 - shared, 0.0)
    opens = jnp.concatenate(opens, axis=0)
    triangle = jnp.where(row_at < lane_at, 1.0, 0.0).astype(bf16)
    rank = mm(opens.astype(bf16), triangle)
    counts = jnp.sum(opens, axis=1, keepdims=True)
    offset = jnp.zeros((1, 1), f32)
    offsets = []
    for q in range(QUADS):
        offsets.append(offset)
        offset = offset + counts[q : q + 1]
    slot = jnp.where(opens > 0.5, rank + jnp.concatenate(offsets, axis=0) + float(EDGE), -1.0)
    slots = jnp.transpose(slot)
    lanes = lane.astype(f32)
    hits = jnp.zeros((LANES, LANES), f32)
    named = jnp.zeros((LANES, LANES), f32)
    for q in range(QUADS):
        hit = matches(slots[:, q : q + 1], lanes)
        hits = hits + hit
        named = named + hit * column[q]
    hits = jnp.sum(hits, axis=0, keepdims=True)
    named = jnp.sum(named, axis=0, keepdims=True)
    first = jnp.where(lane < EDGE, edge_row[0], jnp.where(hits > 0.5, named, -3.0))
    keys = [first, edge_row[1]]
    key_columns = jnp.transpose(jnp.concatenate(keys + [first] * 6, axis=0))
    for q in range(QUADS):
        for s in range(2):
            rims[LANES * q : LANES * (q + 1), LANES * s : LANES * (s + 1)] = matches(
                column[q], keys[s]
            ).astype(bf16)
    for s in range(2):
        joins[LANES * s : LANES * (s + 1), :] = matches(
            key_columns[:, s : s + 1], ids_wide
        ).astype(bf16)


def convect_kernel(packed, own_metric, fourier, derive, out, even, odd, sums, differences):
    metric = own_metric[...]
    table = derive[...]
    index = lax.broadcasted_iota(jnp.int32, (HALF, 1), 0)
    rate = (8.0 / PLANES) * index.astype(f32)
    sign = jnp.where(index % 2 == 0, 1.0, -1.0)
    cosines, sines = (
        jnp.concatenate(
            [
                jnp.concatenate(
                    [packed[m, tile, pl.ds(parity, ROWS // 2, stride=2), :] for tile in range(2)],
                    axis=1,
                )
                for m in range(QUADS)
            ],
            axis=0,
        )
        for parity in range(2)
    )
    highest = sines[0:1]
    to_even = jnp.concatenate([cosines, rate * sines], axis=1)
    to_odd = jnp.concatenate([sines, -rate * cosines], axis=1)
    even[...] = table_times(fourier[0], to_even)
    even[:, :PACK] = even[:, :PACK] + sign * highest
    middle = jnp.sum(sign * to_even, axis=0, keepdims=True)
    middle = middle + jnp.concatenate([highest, jnp.zeros_like(highest)], axis=1)
    odd[...] = table_times(fourier[1], to_odd)
    opening = lax.broadcasted_iota(jnp.int32, (CHUNK, 1), 0) == 0
    product_middle = None
    for i in range(HALF // CHUNK):
        rows = slice(CHUNK * i, CHUNK * (i + 1))
        part_even = even[rows]
        part_odd = odd[rows]
        ahead = part_even + part_odd
        if i == 0:
            part_even = jnp.where(opening, middle, part_even)
        wide = jnp.concatenate([ahead, part_even - part_odd], axis=0)
        value = wide[:, :PACK]
        slope = wide[:, PACK:]
        speed = [unpacked(value, c) for c in range(3)]
        derived = times_fine(jnp.concatenate(speed, axis=0), table)
        weight_r = speed[0] * metric[0:1] + speed[1] * metric[1:2]
        weight_s = speed[0] * metric[2:3] + speed[1] * metric[3:4]
        terms = []
        for c in range(3):
            part = derived[2 * CHUNK * c : 2 * CHUNK * (c + 1)]
            terms.append(
                weight_r * part[:, :LANES]
                + weight_s * part[:, LANES:]
                + speed[2] * unpacked(slope, c)
            )
        total = repacked(terms)
        ahead = total[:CHUNK]
        mirror = total[CHUNK:]
        differences[rows, :] = ahead - mirror
        if i == 0:
            product_middle = mirror[0:1]
            mirror = jnp.where(opening, 0.0, mirror)
        sums[rows, :] = ahead + mirror
    index = index[:KEPT]
    weight = jnp.where(index <= PLANES // 3, -2.0 / PLANES, 0.0)
    result = table_times(fourier[0, :KEPT], sums[...]) + sign[:KEPT] * product_middle
    results = [jnp.where(index == 0, 0.5 * weight, weight) * result]
    result = table_times(fourier[1, :KEPT], differences[...])
    results.append(jnp.where(index == 0, 0.0, weight) * result)
    half = ROWS // 2
    for m in range(KEPT // half):
        for tile in range(2):
            for parity in range(2):
                out[m, tile, pl.ds(parity, half, stride=2), :] = results[parity][
                    half * m : half * (m + 1), LANES * tile : LANES * (tile + 1)
                ]
    out[KEPT // half :] = jnp.zeros((QUADS - KEPT // half, 2, ROWS, LANES), f32)


def weigh_kernel(spectral, nodal, rims, share, first_out, second_out):
    for q in range(QUADS):
        here = slice(LANES * q, LANES * (q + 1))
        mass = nodal[4:5, here]
        block = jnp.concatenate([spectral[q, 0], spectral[q, 1]], axis=1)
        for c in range(3):
            share[ROWS * c : ROWS * (c + 1), here] = mass * jnp.where(
                mass > 0.0, unpacked(block, c), 0.0
            )
    share[3 * ROWS : 3 * ROWS + 1, :] = nodal[4:5, :]
    share[3 * ROWS + 1 : 3 * ROWS + 2, :] = nodal[5:6, :]
    share[3 * ROWS + 2 :, :] = jnp.zeros((STACK - 3 * ROWS - 2, WIDE), f32)
    rim = times_incidence(share[...], rims[...])
    first_out[...] = rim[:, :LANES]
    second_out[...] = rim[:, LANES:]


def joined(parity, share, own, first_in, second_in, joins, single):
    lane = lax.broadcasted_iota(jnp.int32, (1, LANES), 1)
    near = jnp.where(lane < EDGE, first_in[...], own[...])
    other = jnp.where(parity[0] > 0, second_in[0], second_in[1])
    sums = jnp.concatenate([near, other], axis=1)
    return share[...] * single + times_incidence(sums, joins[...])


def star_kernel(
    mode, parity, share, own, first_in, second_in, joins, rims, field, nodal, derive,
    star, inverse, share_out, first_out, second_out,
):
    metric = nodal[...]
    total = joined(parity, share, own, first_in, second_in, joins, metric[6:7])
    inside = metric[5:6] > 0.0
    scale = TIME_STEP / jnp.where(inside, total[3 * ROWS : 3 * ROWS + 1], 1.0)
    inverse[...] = jnp.where(
        inside, 1.0 / jnp.where(inside, total[3 * ROWS + 1 : 3 * ROWS + 2], 1.0), 0.0
    )
    star[...] = field[...] + scale * total[: 3 * ROWS]
    table = derive[...]
    star_x = gradient(star[0:ROWS], metric, table, times_fine)[0]
    star_y = gradient(star[ROWS : 2 * ROWS], metric, table, times_fine)[1]
    divergence = star_x + star_y + along_z(star[2 * ROWS :], mode[0])
    result = (-1.0 / TIME_STEP) * (metric[4:5] * divergence)
    share_out[...] = result
    rim = times_incidence(result, rims[...])
    first_out[...] = rim[:, :LANES]
    second_out[...] = rim[:, LANES:]


def lane_sum(x):
    total = x[:, :LANES]
    for q in range(1, QUADS):
        total = total + x[:, LANES * q : LANES * (q + 1)]
    return jnp.sum(total, axis=1, keepdims=True)


def helmholtz_kernel(
    mode, parity, share, own, first_in, second_in, joins, rims, nodal, inverse, derive, derive_back,
    right, right_x, right_y, share_out, first_out, second_out, sums,
):
    metric = nodal[...]
    total = joined(parity, share, own, first_in, second_in, joins, metric[6:7])
    mass = metric[4:5]
    rate, even = rates(mode[0])
    shift = rate * rate + PENALTY
    grad_x, grad_y = gradient(total, metric, derive[...])
    right[...] = total
    right_x[...] = grad_x
    right_y[...] = grad_y
    flux_x = mass * grad_x
    flux_y = mass * grad_y
    weighted = shift * (mass * total)
    part_r = metric[0:1] * flux_x + metric[1:2] * flux_y
    part_s = metric[2:3] * flux_x + metric[3:4] * flux_y
    both = jnp.concatenate([stacked(part_r), stacked(part_s)], axis=1)
    result = unstacked(times_table(both, derive_back[...])) + weighted
    share_out[...] = result
    rim = times_incidence(result, rims[...])
    first_out[...] = rim[:, :LANES]
    second_out[...] = rim[:, LANES:]
    square = lane_sum(total * total * inverse[...])
    energy = SCALE * lane_sum(flux_x * grad_x + flux_y * grad_y + weighted * total)
    column = lax.broadcasted_iota(jnp.int32, (ROWS, LANES), 1)
    sums[...] = jnp.where(column == 0, square, jnp.where(column == 1, energy, 0.0))


def image_kernel(
    mode, parity, share, own, first_in, second_in, joins, nodal, inverse, derive, sums,
    image, image_x, image_y, spread,
):
    metric = nodal[...]
    total = joined(parity, share, own, first_in, second_in, joins, metric[6:7])
    mass = metric[4:5]
    rate, even = rates(mode[0])
    shift = rate * rate + PENALTY
    grad_x, grad_y = gradient(total, metric, derive[...])
    image[...] = total
    image_x[...] = grad_x
    image_y[...] = grad_y
    square = lane_sum(total * total * (SCALE**2 * inverse[...]))
    energy = grad_x * grad_x + grad_y * grad_y + shift * (total * total)
    energy = lane_sum((SCALE**3 * mass) * energy)
    column = lax.broadcasted_iota(jnp.int32, (ROWS, LANES), 1)
    table = jnp.where(column == 2, square, jnp.where(column == 3, energy, sums[...]))
    table = jnp.concatenate([table, jnp.zeros((LANES - ROWS, LANES), f32)], axis=0)
    turned = jnp.transpose(table)
    short = jnp.concatenate(
        [
            turned[0:1] + pltpu.roll(turned[1:2], ROWS, 1),
            turned[2:3] + pltpu.roll(turned[3:4], ROWS, 1),
        ],
        axis=1,
    )
    spread[...] = jnp.broadcast_to(short, spread.shape)


def finish_kernel(
    mode, gathered, star, right, right_x, right_y, image, image_x, image_y,
    velocity_out, pressure_out,
):
    sums = jnp.sum(gathered[...], axis=0, keepdims=True)
    first = sums[:, :LANES]
    second = sums[:, LANES:]
    g0 = first
    g1 = pltpu.roll(first, ROWS, 1)
    g2 = second
    g3 = pltpu.roll(second, ROWS, 1)
    step0 = g0 / g1
    new = step0 * step0 * g2 - g0
    ratio = new / g0
    curve = (1.0 + ratio) * ((1.0 + ratio) * g1 - 2.0 * step0 * g2) + step0 * step0 * g3
    step1 = new / curve
    by_right = SCALE * (step0 + step1 * (1.0 + ratio))
    by_image = -(SCALE * step1) * (SCALE * step0)
    pair = jnp.concatenate([by_right, by_image, jnp.zeros((6, LANES), f32)], axis=0)
    turned = jnp.transpose(pair)
    by_right = turned[:ROWS, 0:1]
    by_image = turned[:ROWS, 1:2]
    pressure = by_right * right[...] + by_image * image[...]
    slopes = [
        by_right * right_x[...] + by_image * image_x[...],
        by_right * right_y[...] + by_image * image_y[...],
        along_z(pressure, mode[0]),
    ]
    outs = [star[ROWS * c : ROWS * (c + 1)] - TIME_STEP * slopes[c] for c in range(3)]
    for q in range(QUADS):
        here = slice(QUAD_NODES * q, QUAD_NODES * (q + 1))
        there = slice(LANES * q, LANES * q + QUAD_NODES)
        for c in range(3):
            velocity_out[c, :, here] = outs[c][:, there]
        pressure_out[:, here] = pressure[:, there]


VMEM = pl.BlockSpec(memory_space=pltpu.VMEM)
SMEM = pl.BlockSpec(memory_space=pltpu.SMEM)
ANY = pl.BlockSpec(memory_space=pl.ANY)


def call(kernel, ins, outs, scratch=(), flops=0, name=None, aliases={}):
    specs = [SMEM if a.dtype == jnp.int32 and a.shape == (1,) else VMEM for a in ins]
    specs = [ANY if i in aliases else spec for i, spec in enumerate(specs)]
    shapes = [jax.ShapeDtypeStruct(s, d) for s, d in outs]
    size = sum(math.prod(a.shape) * a.dtype.itemsize for a in list(ins) + shapes)
    return pl.pallas_call(
        kernel,
        in_specs=specs,
        out_specs=[ANY if i in aliases.values() else VMEM for i in range(len(shapes))],
        out_shape=shapes,
        scratch_shapes=list(scratch),
        input_output_aliases=aliases,
        name=name,
        cost_estimate=pl.CostEstimate(flops=flops, bytes_accessed=size, transcendentals=0),
        compiler_params=pltpu.CompilerParams(vmem_limit_bytes=40 * 1024 * 1024),
    )(*ins)


def on_device(velocity, metric, mass, local_ids, edge_ids):
    derive, derive_back = (jnp.asarray(t) for t in derivative_tables())
    fourier = jnp.asarray(fourier_tables())
    mode = lax.axis_index("mode").astype(jnp.int32).reshape(1)
    parity = (lax.axis_index("elem") % 2).astype(jnp.int32).reshape(1)
    count = lax.axis_size("elem")
    across = [(i, (i + 1) % count) for i in range(1, count, 2)]
    across = across + [(target, source) for source, target in across]
    beside = [[i, i + 1] for i in range(0, count, 2)]

    def swap(first, second):
        return (
            lax.ppermute(first, "elem", across),
            lax.all_gather(second, "elem", axis_index_groups=beside),
        )

    block = (QUADS, 2, ROWS, LANES)
    (packed,) = call(
        pack_kernel, [velocity], [(block, f32)],
        name="pack",
    )
    nodal = jnp.concatenate([metric, mass[None]], axis=0)
    tables = [fourier, derive]
    field, nodal, own_metric, joins, rims, fourier, derive = call(
        prepare_kernel,
        [mode, parity, velocity, nodal, local_ids[None], edge_ids[0]] + tables,
        [
            ((3 * ROWS, WIDE), f32),
            ((8, WIDE), f32),
            ((8, LANES), f32),
            ((2 * LANES, WIDE), bf16),
            ((WIDE, 2 * LANES), bf16),
        ]
        + [(t.shape, bf16) for t in tables],
        flops=1 << 24,
        name="prepare",
        aliases={6: 5, 7: 6},
    )
    arrived = lax.all_to_all(packed, "mode", 0, 0)
    (spectral,) = call(
        convect_kernel,
        [arrived, own_metric, fourier, derive],
        [(block, f32)],
        scratch=[pltpu.VMEM((HALF, 2 * PACK), f32)] * 2 + [pltpu.VMEM((HALF, PACK), f32)] * 2,
        flops=1 << 30,
        name="convect",
    )
    returned = lax.all_to_all(spectral, "mode", 0, 0)
    rim_out = [((STACK, LANES), f32)] * 2
    share, first_out, second_out = call(
        weigh_kernel, [returned, nodal, rims], [((STACK, WIDE), f32)] + rim_out,
        flops=1 << 28, name="weigh",
    )
    first_in, second_in = swap(first_out, second_out)
    one = ((ROWS, WIDE), f32)
    rim_out = [((ROWS, LANES), f32)] * 2
    star, inverse, share, first_out, second_out = call(
        star_kernel,
        [mode, parity, share, first_out, first_in, second_in, joins, rims, field, nodal, derive],
        [((3 * ROWS, WIDE), f32), ((1, WIDE), f32), one] + rim_out,
        flops=1 << 29, name="star",
    )
    first_in, second_in = swap(first_out, second_out)
    right, right_x, right_y, share, first_out, second_out, sums = call(
        helmholtz_kernel,
        [mode, parity, share, first_out, first_in, second_in, joins, rims, nodal, inverse, derive, derive_back],
        [one, one, one, one] + rim_out + [((ROWS, LANES), f32)],
        flops=1 << 29, name="helmholtz",
    )
    first_in, second_in = swap(first_out, second_out)
    image, image_x, image_y, spread = call(
        image_kernel,
        [mode, parity, share, first_out, first_in, second_in, joins, nodal, inverse, derive, sums],
        [one, one, one, ((count, 1, 2 * LANES), f32)],
        flops=1 << 29, name="image",
    )
    gathered = lax.all_to_all(spread, "elem", 0, 0)
    gathered = gathered.reshape(count, 2 * LANES)
    velocity_new, pressure = call(
        finish_kernel,
        [mode, gathered, star, right, right_x, right_y, image, image_x, image_y],
        [((3, ROWS, QUADS * QUAD_NODES), f32), ((ROWS, QUADS * QUAD_NODES), f32)],
        name="finish",
    )
    return velocity_new, pressure


def solution(mesh):
    in_specs = (
        P(None, "mode", "elem"),
        P(None, "elem"),
        P("elem"),
        P("elem"),
        P("elem", None, None),
    )
    out_specs = (P(None, "mode", "elem"), P("mode", "elem"))
    return jax.shard_map(
        on_device, mesh=mesh, in_specs=in_specs, out_specs=out_specs, check_vma=False
    )
```

```python
import functools
import math

import jax
import jax.numpy as jnp
import numpy as np
from jax import lax
from jax.experimental import pallas as pl
from jax.experimental.pallas import tpu as pltpu
from jax.sharding import PartitionSpec as P

SIDE = 9
QUAD_NODES = 81
PLANES = 512
QUADS = 8
EDGE = 65
LANES = 128
WIDE = QUADS * LANES
PACK = 256
ROWS = 64
KEPT = 192
STACK = 200
CHUNK = 64
HALF = 256

SCALE = 2.0**-12
PENALTY = 1.0
TIME_STEP = 0.01

f32 = jnp.float32
bf16 = jnp.bfloat16


def legendre_pair(points, degree):
    previous = points * 0.0 + 1.0
    current = points.copy()
    for order in range(2, degree + 1):
        following = ((2.0 * order - 1.0) * points * current - (order - 1.0) * previous) / order
        previous = current
        current = following
    return (previous, current)


def derivative_matrix():
    degree = SIDE - 1
    points = np.cos(math.pi * np.arange(degree + 1) / degree)
    for sweep in range(100):
        lower, upper = legendre_pair(points, degree)
        points = points - (points * upper - lower) / ((degree + 1.0) * upper)
    points = points[::-1].copy()
    values = legendre_pair(points, degree)[1]
    identity = np.eye(SIDE)
    differ = points[:, None] - points[None, :] + identity
    matrix = np.where(identity > 0.5, 0.0, values[:, None] / (values[None, :] * differ))
    matrix[0, 0] = -degree * (degree + 1) / 4.0
    matrix[degree, degree] = degree * (degree + 1) / 4.0
    return matrix


def halves(table):
    high = table.astype(np.float32).astype(jnp.bfloat16)
    low = (table - high.astype(np.float64)).astype(np.float32).astype(jnp.bfloat16)
    return high, low


def as_right(table):
    high, middle = halves(table)
    rest = table - high.astype(np.float64) - middle.astype(np.float64)
    return np.concatenate([high, middle, rest.astype(np.float32).astype(jnp.bfloat16)], axis=0)


def as_left(table):
    return np.concatenate(halves(table), axis=1)


def derivative_tables():
    matrix = derivative_matrix()
    table = np.zeros((LANES, 2 * LANES))
    table[:QUAD_NODES, :QUAD_NODES] = np.kron(matrix, np.eye(SIDE)).T
    table[:QUAD_NODES, LANES : LANES + QUAD_NODES] = np.kron(np.eye(SIDE), matrix).T
    table = table.astype(np.float32).astype(np.float64)
    return as_right(table), as_right(table.T.copy())


def fourier_tables():
    index = np.arange(HALF)
    angles = 2.0 * math.pi / PLANES * (index[:, None] * index[None, :] % PLANES)
    return np.stack([as_left(np.cos(angles)), as_left(np.sin(angles))])


def split2(x):
    high = x.astype(bf16)
    return high, (x - high.astype(f32)).astype(bf16)


def mm(a, b):
    return jnp.dot(a, b, preferred_element_type=f32)


def split3(x):
    high = x.astype(bf16)
    rest = x - high.astype(f32)
    middle = rest.astype(bf16)
    return high, middle, (rest - middle.astype(f32)).astype(bf16)


def times_table(x, table):
    inner = x.shape[1]
    high, low = split2(x)
    table = jnp.concatenate([table[:inner], table[: 2 * inner]], axis=0)
    return mm(jnp.concatenate([low, high, high], axis=1), table)


def times_fine(x, table):
    inner = x.shape[1]
    high, middle, low = split3(x)
    table = jnp.concatenate([table[:inner], table[: 2 * inner], table], axis=0)
    return mm(jnp.concatenate([low, middle, middle, high, high, high], axis=1), table)


def table_times(table, x):
    inner = x.shape[0]
    high, low = split2(x)
    table = jnp.concatenate([table[:, :inner], table], axis=1)
    return mm(table, jnp.concatenate([low, high, high], axis=0))


def times_incidence(x, incidence):
    rows = x.shape[0]
    out = mm(jnp.concatenate(split2(x), axis=0), incidence)
    return out[:rows] + out[rows:]


def stacked(x):
    return jnp.concatenate([x[:, LANES * q : LANES * (q + 1)] for q in range(QUADS)], axis=0)


def unstacked(x):
    rows = x.shape[0] // QUADS
    return jnp.concatenate([x[rows * q : rows * (q + 1)] for q in range(QUADS)], axis=1)


def gradient(x, metric, table, times=times_table):
    derived = times(stacked(x), table)
    along_r = unstacked(derived[:, :LANES])
    along_s = unstacked(derived[:, LANES:])
    return (
        metric[0:1] * along_r + metric[2:3] * along_s,
        metric[1:2] * along_r + metric[3:4] * along_s,
    )


def rates(mode):
    row = lax.broadcasted_iota(jnp.int32, (ROWS, 1), 0)
    return (8.0 / PLANES) * ((mode * ROWS + row) // 2).astype(f32), row % 2 == 0


def along_z(x, mode):
    rate, even = rates(mode)
    return rate * jnp.where(even, pltpu.roll(x, ROWS - 1, 0), -pltpu.roll(x, 1, 0))


def lanes_at():
    return lax.broadcasted_iota(jnp.int32, (1, LANES), 1)


def unpacked(x, field):
    first, second = x[:, :LANES], x[:, LANES:]
    if field == 0:
        return first
    if field == 1:
        both = jnp.where(lanes_at() < QUAD_NODES, second, first)
        return pltpu.roll(both, LANES - QUAD_NODES, 1)
    return pltpu.roll(second, 2 * (LANES - QUAD_NODES), 1)


def repacked(fields):
    lane = lanes_at()
    second_at = 2 * QUAD_NODES - LANES
    middle = pltpu.roll(fields[1], QUAD_NODES, 1)
    last = jnp.where(lane < second_at + QUAD_NODES, pltpu.roll(fields[2], second_at, 1), 0.0)
    return jnp.concatenate(
        [jnp.where(lane < QUAD_NODES, fields[0], middle), jnp.where(lane < second_at, middle, last)],
        axis=1,
    )


def pack_kernel(velocity, packed_far, packed, left):
    half = QUADS // 2
    copies = [
        pltpu.make_async_copy(
            packed.at[pl.ds(half * i, half)], packed_far.at[pl.ds(half * i, half)], left.at[i]
        )
        for i in range(2)
    ]
    for q in range(QUADS):
        for c in range(3):
            start, stop = QUAD_NODES * c, QUAD_NODES * (c + 1)
            for tile in range(start // LANES, (stop - 1) // LANES + 1):
                low, high = max(start, LANES * tile), min(stop, LANES * (tile + 1))
                node = QUAD_NODES * q - start
                packed[q, tile, :, low - LANES * tile : high - LANES * tile] = velocity[
                    c, :, node + low : node + high
                ]
        packed[q, 1, :, 3 * QUAD_NODES - LANES :] = jnp.zeros((ROWS, PACK - 3 * QUAD_NODES), f32)
        if q % half == half - 1:
            copies[q // half].start()
    for copy in copies:
        copy.wait()


def matches(column, row):
    return jnp.where(column == row, 1.0, 0.0)


def prepare_kernel(
    mode, parity, velocity, nodal, ids, edges, fourier, derive,
    field, nodal_wide, own_metric, joins, rims, fourier_on, derive_on,
):
    lane = lax.broadcasted_iota(jnp.int32, (1, LANES), 1)
    inside = lane < QUAD_NODES
    field[...] = jnp.zeros_like(field)
    nodal_wide[...] = jnp.zeros_like(nodal_wide)
    for q in range(QUADS):
        here = slice(LANES * q, LANES * q + QUAD_NODES)
        there = slice(QUAD_NODES * q, QUAD_NODES * (q + 1))
        for c in range(3):
            field[ROWS * c : ROWS * (c + 1), here] = velocity[c, :, there]
        nodal_wide[0:5, here] = nodal[0:5, there]
        nodal_wide[5:6, here] = jnp.ones((1, QUAD_NODES), f32)
    own = jnp.zeros((8, LANES), f32)
    for q in range(QUADS):
        own = own + jnp.where(mode[0] == q, nodal_wide[:, LANES * q : LANES * (q + 1)], 0.0)
    own_metric[...] = own
    ids_row = [
        jnp.concatenate(
            [
                ids[:, QUAD_NODES * q : QUAD_NODES * (q + 1)],
                jnp.full((1, LANES - QUAD_NODES), -1, jnp.int32),
            ],
            axis=1,
        ).astype(f32)
        for q in range(QUADS)
    ]
    ids_wide = jnp.concatenate(ids_row, axis=1)
    odd = parity[0] > 0
    edge_row = [
        jnp.concatenate(
            [
                jnp.where(odd, edges[1 - s : 2 - s, :], edges[s : s + 1, :]),
                jnp.full((1, LANES - EDGE), -2, jnp.int32),
            ],
            axis=1,
        ).astype(f32)
        for s in range(2)
    ]
    columns = jnp.transpose(jnp.concatenate(ids_row, axis=0))
    column = [columns[:, q : q + 1] for q in range(QUADS)]
    row_at = lax.broadcasted_iota(jnp.int32, (LANES, LANES), 0)
    lane_at = lax.broadcasted_iota(jnp.int32, (LANES, LANES), 1)
    opens = []
    for q in range(QUADS):
        total = jnp.zeros((LANES, LANES), f32)
        before = jnp.zeros((LANES, LANES), f32)
        for p in range(QUADS):
            same = matches(column[p], ids_row[q])
            total = total + same
            if p < q:
                before = before + same
            if p == q:
                before = before + jnp.where(row_at < lane_at, same, 0.0)
        copies = jnp.sum(total, axis=0, keepdims=True)
        earlier = jnp.sum(before, axis=0, keepdims=True)
        shared = jnp.where(inside & (copies > 1.5), 1.0, 0.0)
        opens.append(jnp.where(earlier < 0.5, shared, 0.0))
        nodal_wide[6:7, LANES * q : LANES * (q + 1)] = jnp.where(inside, 1.0 - shared, 0.0)
    opens = jnp.concatenate(opens, axis=0)
    triangle = jnp.where(row_at < lane_at, 1.0, 0.0).astype(bf16)
    rank = mm(opens.astype(bf16), triangle)
    counts = jnp.sum(opens, axis=1, keepdims=True)
    offset = jnp.zeros((1, 1), f32)
    offsets = []
    for q in range(QUADS):
        offsets.append(offset)
        offset = offset + counts[q : q + 1]
    slot = jnp.where(opens > 0.5, rank + jnp.concatenate(offsets, axis=0) + float(EDGE), -1.0)
    slots = jnp.transpose(slot)
    lanes = lane.astype(f32)
    hits = jnp.zeros((LANES, LANES), f32)
    named = jnp.zeros((LANES, LANES), f32)
    for q in range(QUADS):
        hit = matches(slots[:, q : q + 1], lanes)
        hits = hits + hit
        named = named + hit * column[q]
    hits = jnp.sum(hits, axis=0, keepdims=True)
    named = jnp.sum(named, axis=0, keepdims=True)
    first = jnp.where(lane < EDGE, edge_row[0], jnp.where(hits > 0.5, named, -3.0))
    keys = [first, edge_row[1]]
    key_columns = jnp.transpose(jnp.concatenate(keys + [first] * 6, axis=0))
    for q in range(QUADS):
        for s in range(2):
            rims[LANES * q : LANES * (q + 1), LANES * s : LANES * (s + 1)] = matches(
                column[q], keys[s]
            ).astype(bf16)
    for s in range(2):
        joins[LANES * s : LANES * (s + 1), :] = matches(
            key_columns[:, s : s + 1], ids_wide
        ).astype(bf16)


def convect_kernel(packed, own_metric, fourier, derive, out, even, odd, sums, differences):
    metric = own_metric[...]
    table = derive[...]
    index = lax.broadcasted_iota(jnp.int32, (HALF, 1), 0)
    rate = (8.0 / PLANES) * index.astype(f32)
    sign = jnp.where(index % 2 == 0, 1.0, -1.0)
    cosines, sines = (
        jnp.concatenate(
            [
                jnp.concatenate(
                    [packed[m, tile, pl.ds(parity, ROWS // 2, stride=2), :] for tile in range(2)],
                    axis=1,
                )
                for m in range(QUADS)
            ],
            axis=0,
        )
        for parity in range(2)
    )
    highest = sines[0:1]
    to_even = jnp.concatenate([cosines, rate * sines], axis=1)
    to_odd = jnp.concatenate([sines, -rate * cosines], axis=1)
    even[...] = table_times(fourier[0], to_even)
    even[:, :PACK] = even[:, :PACK] + sign * highest
    middle = jnp.sum(sign * to_even, axis=0, keepdims=True)
    middle = middle + jnp.concatenate([highest, jnp.zeros_like(highest)], axis=1)
    odd[...] = table_times(fourier[1], to_odd)
    opening = lax.broadcasted_iota(jnp.int32, (CHUNK, 1), 0) == 0
    product_middle = None
    for i in range(HALF // CHUNK):
        rows = slice(CHUNK * i, CHUNK * (i + 1))
        part_even = even[rows]
        part_odd = odd[rows]
        ahead = part_even + part_odd
        if i == 0:
            part_even = jnp.where(opening, middle, part_even)
        wide = jnp.concatenate([ahead, part_even - part_odd], axis=0)
        value = wide[:, :PACK]
        slope = wide[:, PACK:]
        speed = [unpacked(value, c) for c in range(3)]
        derived = times_fine(jnp.concatenate(speed, axis=0), table)
        weight_r = speed[0] * metric[0:1] + speed[1] * metric[1:2]
        weight_s = speed[0] * metric[2:3] + speed[1] * metric[3:4]
        terms = []
        for c in range(3):
            part = derived[2 * CHUNK * c : 2 * CHUNK * (c + 1)]
            terms.append(
                weight_r * part[:, :LANES]
                + weight_s * part[:, LANES:]
                + speed[2] * unpacked(slope, c)
            )
        total = repacked(terms)
        ahead = total[:CHUNK]
        mirror = total[CHUNK:]
        differences[rows, :] = ahead - mirror
        if i == 0:
            product_middle = mirror[0:1]
            mirror = jnp.where(opening, 0.0, mirror)
        sums[rows, :] = ahead + mirror
    index = index[:KEPT]
    weight = jnp.where(index <= PLANES // 3, -2.0 / PLANES, 0.0)
    result = table_times(fourier[0, :KEPT], sums[...]) + sign[:KEPT] * product_middle
    results = [jnp.where(index == 0, 0.5 * weight, weight) * result]
    result = table_times(fourier[1, :KEPT], differences[...])
    results.append(jnp.where(index == 0, 0.0, weight) * result)
    half = ROWS // 2
    for m in range(KEPT // half):
        for tile in range(2):
            for parity in range(2):
                out[m, tile, pl.ds(parity, half, stride=2), :] = results[parity][
                    half * m : half * (m + 1), LANES * tile : LANES * (tile + 1)
                ]
    out[KEPT // half :] = jnp.zeros((QUADS - KEPT // half, 2, ROWS, LANES), f32)


def weigh_kernel(spectral, nodal, rims, share, first_out, second_out):
    for q in range(QUADS):
        here = slice(LANES * q, LANES * (q + 1))
        mass = nodal[4:5, here]
        block = jnp.concatenate([spectral[q, 0], spectral[q, 1]], axis=1)
        for c in range(3):
            share[ROWS * c : ROWS * (c + 1), here] = mass * jnp.where(
                mass > 0.0, unpacked(block, c), 0.0
            )
    share[3 * ROWS : 3 * ROWS + 1, :] = nodal[4:5, :]
    share[3 * ROWS + 1 : 3 * ROWS + 2, :] = nodal[5:6, :]
    share[3 * ROWS + 2 :, :] = jnp.zeros((STACK - 3 * ROWS - 2, WIDE), f32)
    rim = times_incidence(share[...], rims[...])
    first_out[...] = rim[:, :LANES]
    second_out[...] = rim[:, LANES:]


def joined(parity, share, own, first_in, second_in, joins, single):
    lane = lax.broadcasted_iota(jnp.int32, (1, LANES), 1)
    near = jnp.where(lane < EDGE, first_in[...], own[...])
    other = jnp.where(parity[0] > 0, second_in[0], second_in[1])
    sums = jnp.concatenate([near, other], axis=1)
    return share[...] * single + times_incidence(sums, joins[...])


def star_kernel(
    mode, parity, share, own, first_in, second_in, joins, rims, field, nodal, derive,
    star, inverse, share_out, first_out, second_out,
):
    metric = nodal[...]
    total = joined(parity, share, own, first_in, second_in, joins, metric[6:7])
    inside = metric[5:6] > 0.0
    scale = TIME_STEP / jnp.where(inside, total[3 * ROWS : 3 * ROWS + 1], 1.0)
    inverse[...] = jnp.where(
        inside, 1.0 / jnp.where(inside, total[3 * ROWS + 1 : 3 * ROWS + 2], 1.0), 0.0
    )
    star[...] = field[...] + scale * total[: 3 * ROWS]
    table = derive[...]
    star_x = gradient(star[0:ROWS], metric, table, times_fine)[0]
    star_y = gradient(star[ROWS : 2 * ROWS], metric, table, times_fine)[1]
    divergence = star_x + star_y + along_z(star[2 * ROWS :], mode[0])
    result = (-1.0 / TIME_STEP) * (metric[4:5] * divergence)
    share_out[...] = result
    rim = times_incidence(result, rims[...])
    first_out[...] = rim[:, :LANES]
    second_out[...] = rim[:, LANES:]


def lane_sum(x):
    total = x[:, :LANES]
    for q in range(1, QUADS):
        total = total + x[:, LANES * q : LANES * (q + 1)]
    return jnp.sum(total, axis=1, keepdims=True)


def helmholtz_kernel(
    mode, parity, share, own, first_in, second_in, joins, rims, nodal, inverse, derive, derive_back,
    right, right_x, right_y, share_out, first_out, second_out, sums,
):
    metric = nodal[...]
    total = joined(parity, share, own, first_in, second_in, joins, metric[6:7])
    mass = metric[4:5]
    rate, even = rates(mode[0])
    shift = rate * rate + PENALTY
    grad_x, grad_y = gradient(total, metric, derive[...])
    right[...] = total
    right_x[...] = grad_x
    right_y[...] = grad_y
    flux_x = mass * grad_x
    flux_y = mass * grad_y
    weighted = shift * (mass * total)
    part_r = metric[0:1] * flux_x + metric[1:2] * flux_y
    part_s = metric[2:3] * flux_x + metric[3:4] * flux_y
    both = jnp.concatenate([stacked(part_r), stacked(part_s)], axis=1)
    result = unstacked(times_table(both, derive_back[...])) + weighted
    share_out[...] = result
    rim = times_incidence(result, rims[...])
    first_out[...] = rim[:, :LANES]
    second_out[...] = rim[:, LANES:]
    square = lane_sum(total * total * inverse[...])
    energy = SCALE * lane_sum(flux_x * grad_x + flux_y * grad_y + weighted * total)
    column = lax.broadcasted_iota(jnp.int32, (ROWS, LANES), 1)
    sums[...] = jnp.where(column == 0, square, jnp.where(column == 1, energy, 0.0))


def image_kernel(
    mode, parity, share, own, first_in, second_in, joins, nodal, inverse, derive, sums,
    image, image_x, image_y, spread,
):
    metric = nodal[...]
    total = joined(parity, share, own, first_in, second_in, joins, metric[6:7])
    mass = metric[4:5]
    rate, even = rates(mode[0])
    shift = rate * rate + PENALTY
    grad_x, grad_y = gradient(total, metric, derive[...])
    image[...] = total
    image_x[...] = grad_x
    image_y[...] = grad_y
    square = lane_sum(total * total * (SCALE**2 * inverse[...]))
    energy = grad_x * grad_x + grad_y * grad_y + shift * (total * total)
    energy = lane_sum((SCALE**3 * mass) * energy)
    column = lax.broadcasted_iota(jnp.int32, (ROWS, LANES), 1)
    table = jnp.where(column == 2, square, jnp.where(column == 3, energy, sums[...]))
    table = jnp.concatenate([table, jnp.zeros((LANES - ROWS, LANES), f32)], axis=0)
    turned = jnp.transpose(table)
    short = jnp.concatenate(
        [
            turned[0:1] + pltpu.roll(turned[1:2], ROWS, 1),
            turned[2:3] + pltpu.roll(turned[3:4], ROWS, 1),
        ],
        axis=1,
    )
    spread[...] = jnp.broadcast_to(short, spread.shape)


def finish_kernel(
    mode, gathered, star, right, right_x, right_y, image, image_x, image_y,
    velocity_out, pressure_out,
):
    sums = jnp.sum(gathered[...], axis=0, keepdims=True)
    first = sums[:, :LANES]
    second = sums[:, LANES:]
    g0 = first
    g1 = pltpu.roll(first, ROWS, 1)
    g2 = second
    g3 = pltpu.roll(second, ROWS, 1)
    step0 = g0 / g1
    new = step0 * step0 * g2 - g0
    ratio = new / g0
    curve = (1.0 + ratio) * ((1.0 + ratio) * g1 - 2.0 * step0 * g2) + step0 * step0 * g3
    step1 = new / curve
    by_right = SCALE * (step0 + step1 * (1.0 + ratio))
    by_image = -(SCALE * step1) * (SCALE * step0)
    pair = jnp.concatenate([by_right, by_image, jnp.zeros((6, LANES), f32)], axis=0)
    turned = jnp.transpose(pair)
    by_right = turned[:ROWS, 0:1]
    by_image = turned[:ROWS, 1:2]
    pressure = by_right * right[...] + by_image * image[...]
    slopes = [
        by_right * right_x[...] + by_image * image_x[...],
        by_right * right_y[...] + by_image * image_y[...],
        along_z(pressure, mode[0]),
    ]
    outs = [star[ROWS * c : ROWS * (c + 1)] - TIME_STEP * slopes[c] for c in range(3)]
    for q in range(QUADS):
        here = slice(QUAD_NODES * q, QUAD_NODES * (q + 1))
        there = slice(LANES * q, LANES * q + QUAD_NODES)
        for c in range(3):
            velocity_out[c, :, here] = outs[c][:, there]
        pressure_out[:, here] = pressure[:, there]


VMEM = pl.BlockSpec(memory_space=pltpu.VMEM)
SMEM = pl.BlockSpec(memory_space=pltpu.SMEM)
ANY = pl.BlockSpec(memory_space=pl.ANY)


def call(kernel, ins, outs, scratch=(), flops=0, name=None, aliases={}, far_outs=()):
    specs = [SMEM if a.dtype == jnp.int32 and a.shape == (1,) else VMEM for a in ins]
    specs = [ANY if i in aliases else spec for i, spec in enumerate(specs)]
    shapes = [jax.ShapeDtypeStruct(s, d) for s, d in outs]
    size = sum(math.prod(a.shape) * a.dtype.itemsize for a in list(ins) + shapes)
    return pl.pallas_call(
        kernel,
        in_specs=specs,
        out_specs=[ANY if i in aliases.values() or i in far_outs else VMEM for i in range(len(shapes))],
        out_shape=shapes,
        scratch_shapes=list(scratch),
        input_output_aliases=aliases,
        name=name,
        cost_estimate=pl.CostEstimate(flops=flops, bytes_accessed=size, transcendentals=0),
        compiler_params=pltpu.CompilerParams(vmem_limit_bytes=40 * 1024 * 1024),
    )(*ins)


def on_device(velocity, metric, mass, local_ids, edge_ids):
    derive, derive_back = (jnp.asarray(t) for t in derivative_tables())
    fourier = jnp.asarray(fourier_tables())
    mode = lax.axis_index("mode").astype(jnp.int32).reshape(1)
    parity = (lax.axis_index("elem") % 2).astype(jnp.int32).reshape(1)
    count = lax.axis_size("elem")
    across = [(i, (i + 1) % count) for i in range(1, count, 2)]
    across = across + [(target, source) for source, target in across]
    beside = [[i, i + 1] for i in range(0, count, 2)]

    def swap(first, second):
        return (
            lax.ppermute(first, "elem", across),
            lax.all_gather(second, "elem", axis_index_groups=beside),
        )

    block = (QUADS, 2, ROWS, LANES)
    (packed,) = call(
        pack_kernel, [velocity], [(block, f32)],
        scratch=[pltpu.VMEM(block, f32), pltpu.SemaphoreType.DMA((2,))],
        name="pack", far_outs=(0,),
    )
    nodal = jnp.concatenate([metric, mass[None]], axis=0)
    tables = [fourier, derive]
    field, nodal, own_metric, joins, rims, fourier, derive = call(
        prepare_kernel,
        [mode, parity, velocity, nodal, local_ids[None], edge_ids[0]] + tables,
        [
            ((3 * ROWS, WIDE), f32),
            ((8, WIDE), f32),
            ((8, LANES), f32),
            ((2 * LANES, WIDE), bf16),
            ((WIDE, 2 * LANES), bf16),
        ]
        + [(t.shape, bf16) for t in tables],
        flops=1 << 24,
        name="prepare",
        aliases={6: 5, 7: 6},
    )
    arrived = lax.all_to_all(packed, "mode", 0, 0)
    (spectral,) = call(
        convect_kernel,
        [arrived, own_metric, fourier, derive],
        [(block, f32)],
        scratch=[pltpu.VMEM((HALF, 2 * PACK), f32)] * 2 + [pltpu.VMEM((HALF, PACK), f32)] * 2,
        flops=1 << 30,
        name="convect",
    )
    returned = lax.all_to_all(spectral, "mode", 0, 0)
    rim_out = [((STACK, LANES), f32)] * 2
    share, first_out, second_out = call(
        weigh_kernel, [returned, nodal, rims], [((STACK, WIDE), f32)] + rim_out,
        flops=1 << 28, name="weigh",
    )
    first_in, second_in = swap(first_out, second_out)
    one = ((ROWS, WIDE), f32)
    rim_out = [((ROWS, LANES), f32)] * 2
    star, inverse, share, first_out, second_out = call(
        star_kernel,
        [mode, parity, share, first_out, first_in, second_in, joins, rims, field, nodal, derive],
        [((3 * ROWS, WIDE), f32), ((1, WIDE), f32), one] + rim_out,
        flops=1 << 29, name="star",
    )
    first_in, second_in = swap(first_out, second_out)
    right, right_x, right_y, share, first_out, second_out, sums = call(
        helmholtz_kernel,
        [mode, parity, share, first_out, first_in, second_in, joins, rims, nodal, inverse, derive, derive_back],
        [one, one, one, one] + rim_out + [((ROWS, LANES), f32)],
        flops=1 << 29, name="helmholtz",
    )
    first_in, second_in = swap(first_out, second_out)
    image, image_x, image_y, spread = call(
        image_kernel,
        [mode, parity, share, first_out, first_in, second_in, joins, nodal, inverse, derive, sums],
        [one, one, one, ((count, 1, 2 * LANES), f32)],
        flops=1 << 29, name="image",
    )
    gathered = lax.all_to_all(spread, "elem", 0, 0)
    gathered = gathered.reshape(count, 2 * LANES)
    velocity_new, pressure = call(
        finish_kernel,
        [mode, gathered, star, right, right_x, right_y, image, image_x, image_y],
        [((3, ROWS, QUADS * QUAD_NODES), f32), ((ROWS, QUADS * QUAD_NODES), f32)],
        name="finish",
    )
    return velocity_new, pressure


def solution(mesh):
    in_specs = (
        P(None, "mode", "elem"),
        P(None, "elem"),
        P("elem"),
        P("elem"),
        P("elem", None, None),
    )
    out_specs = (P(None, "mode", "elem"), P("mode", "elem"))
    return jax.shard_map(
        on_device, mesh=mesh, in_specs=in_specs, out_specs=out_specs, check_vma=False
    )
```
